32 devices in a mesh: hop: 2 (over x), batch: 16 (over z, y, core).
Axes of the slice: x: 2, y: 2, z: 4, core: 2. Of those that a mesh axis runs over, the one named last changes fastest.
Arguments:
- section_rows: bfloat16 [2, 2048, 2048], P('hop', 'batch'), may hold values from -6 to 6
- weights: bfloat16 [2, 2048, 2048], P('hop'), may hold values from -0.125 to 0.125
- relation_table: bfloat16 [256, 2048], replicated, may hold values from -4 to 4
- relation_ids: int32 [2048], P('batch'), may hold values from 0 to 255
Outputs:
- weight_grad: float32 [2, 2048, 2048], P('hop', 'batch')
- relation_grad: float32 [256, 2048], P(('hop', 'batch'))
- query_grad: bfloat16 [2048, 2048], P('batch')
The draws below stay inside these ranges and needn't reach their ends.
Inputs may be any that keep to these rules, and one draw needn't show every extreme that they name: `relation_ids`: relation index of each query.
All inputs are finite; a program needn't handle non-finite values.
Results may differ from the reference program's by a relative error of at most 0.0064.
Values may be sent and summed in bfloat16 or wider, within the bound.
No kernel may reach another device: no remote copies, remote signals or barrier semaphores. Data moves between devices by JAX's collectives and lax.ppermute only.
A program may use at most 128 MiB of HBM per device.

```python
import jax
import jax.numpy as jnp
from jax import lax

D = 2048
HID = 2048
NREL = 256
TOKENS = 2048


def touch_ends(drawn, stream_key, low, high):
    place = [jax.random.randint(jax.random.fold_in(stream_key, axis), (), 0, length) for axis, length in enumerate(drawn.shape)]
    longest = drawn.shape.index(max(drawn.shape))
    next_to = place[:longest] + [(place[longest] + 1) % drawn.shape[longest]] + place[longest + 1:]
    return drawn.at[tuple(place)].set(low).at[tuple(next_to)].set(high)


def block_scale(stream_key, extent, split, smallest, largest):
    level = 1.0
    for dim, shards_of in split:
        steps = jax.random.uniform(jax.random.fold_in(jax.random.fold_in(stream_key, 6), dim), (shards_of,), jnp.float32, smallest / len(split), largest / len(split))
        level = level * jnp.repeat(jnp.exp(steps), extent[dim] // shards_of).reshape((-1,) + (1,) * (len(extent) - 1 - dim))
    return level


def gaussian(key, extent, spread, reach, shards=(), kind=jnp.bfloat16):
    array = spread * jax.random.normal(key, extent, jnp.float32)
    if shards:
        array = array * block_scale(key, extent, shards, -0.22, 0.18)
    return jnp.clip(array, -reach, reach).astype(kind)


def setup_inputs(seed: int = 0) -> dict:
    key_list = jax.random.split(jax.random.key(seed), 5)
    return {
        "section_rows": gaussian(key_list[0], (2, TOKENS, HID), 1.0, 6.0, ((0, 2), (1, 16))),
        "weights": gaussian(key_list[1], (2, D, HID), D ** -0.5, 0.125, ((0, 2),)),
        "relation_table": gaussian(key_list[2], (NREL, D), 0.7, 4.0),
        "relation_ids": touch_ends(jax.random.randint(key_list[3], (TOKENS,), 0, NREL), jax.random.fold_in(key_list[3], 1), 0, NREL - 1).astype(jnp.int32),
    }


def reference(section_rows, weights, relation_table, relation_ids):
    half = D // 2
    hidden_one = section_rows[0]
    cotangent = section_rows[1]
    query = lax.dot_general(hidden_one, weights[0], (((1,), (1,)), ((), ())), preferred_element_type=jnp.float32).astype(jnp.bfloat16)
    rel = relation_table[relation_ids].astype(jnp.float32)
    r_re = rel[:, :half]
    r_im = rel[:, half:]
    qf = query.astype(jnp.float32)
    q_re = qf[:, :half]
    q_im = qf[:, half:]
    mixed = jnp.concatenate([q_re * r_re - q_im * r_im, q_re * r_im + q_im * r_re], axis=1).astype(jnp.bfloat16)
    pre = jnp.dot(mixed, weights[1], preferred_element_type=jnp.float32)
    sig = jax.nn.sigmoid(pre)
    grad_pre = (cotangent.astype(jnp.float32) * (sig * (1.0 + pre * (1.0 - sig)))).astype(jnp.bfloat16)
    grad_mixed = lax.dot_general(grad_pre, weights[1], (((1,), (1,)), ((), ())), preferred_element_type=jnp.float32)
    gz_re = grad_mixed[:, :half]
    gz_im = grad_mixed[:, half:]
    query_grad = jnp.concatenate([gz_re * r_re + gz_im * r_im, gz_im * r_re - gz_re * r_im], axis=1).astype(jnp.bfloat16)
    grad_rel = jnp.concatenate([gz_re * q_re + gz_im * q_im, gz_im * q_re - gz_re * q_im], axis=1)
    relation_grad = jax.ops.segment_sum(grad_rel, relation_ids, num_segments=NREL) * jnp.sqrt(jnp.float32(NREL) / jnp.float32(TOKENS))
    scale = 1.0 / jnp.sqrt(jnp.float32(TOKENS))
    grad_zero = jnp.dot(query_grad.T, hidden_one, preferred_element_type=jnp.float32) * scale
    grad_one = jnp.dot(mixed.T, grad_pre, preferred_element_type=jnp.float32) * scale
    weight_grad = jnp.stack([grad_zero, grad_one], axis=0)
    return (weight_grad, relation_grad, query_grad)
```

```python
import jax
import jax.numpy as jnp
from jax import lax
from jax.sharding import PartitionSpec as P

F32 = jnp.float32
BF16 = jnp.bfloat16


def dot(a, b, ca, cb):
    return lax.dot_general(a, b, (((ca,), (cb,)), ((), ())), preferred_element_type=F32)


def split_sum(onehot, values):
    head = values.astype(BF16)
    rest = (values - head.astype(F32)).astype(BF16)
    return dot(onehot, head, 0, 0) + dot(onehot, rest, 0, 0)


def trail(query, cotangent, weight, table, ids):
    count_rel, width = table.shape
    half = width // 2
    onehot = (ids[:, None] == lax.iota(jnp.int32, count_rel)[None, :]).astype(BF16)
    rel = dot(onehot, table, 1, 0)
    r_re, r_im = rel[:, :half], rel[:, half:]
    qf = query.astype(F32)
    q_re, q_im = qf[:, :half], qf[:, half:]
    mixed = jnp.concatenate(
        [q_re * r_re - q_im * r_im, q_re * r_im + q_im * r_re], axis=1
    ).astype(BF16)
    pre = dot(mixed, weight, 1, 0)
    sig = jax.nn.sigmoid(pre)
    grad_pre = (cotangent.astype(F32) * (sig * (1.0 + pre * (1.0 - sig)))).astype(BF16)
    gz = dot(grad_pre, weight, 1, 1)
    gz_re, gz_im = gz[:, :half], gz[:, half:]
    grad_query = jnp.concatenate(
        [gz_re * r_re + gz_im * r_im, gz_im * r_re - gz_re * r_im], axis=1
    ).astype(BF16)
    grad_rel = jnp.concatenate([gz_re * q_re + gz_im * q_im, gz_im * q_re - gz_re * q_im], axis=1)
    return mixed, grad_pre, grad_query, split_sum(onehot, grad_rel).astype(BF16)


def local(section_rows, weights, relation_table, relation_ids):
    rows = section_rows[0]
    weight = weights[0]
    rows_dev, width = rows.shape
    count_rel = relation_table.shape[0]
    batch = lax.axis_size("batch")
    first = lax.axis_index("hop") == 0
    total_rows = rows_dev * batch
    zeros = jnp.zeros((rows_dev, width), BF16)

    query = lax.cond(first, lambda: dot(rows, weight, 1, 1).astype(BF16), lambda: zeros)
    received = lax.ppermute(query, "hop", [(0, 1)])
    mixed, grad_pre, grad_query, rel_part = lax.cond(
        first,
        lambda: (zeros, zeros, zeros, jnp.zeros((count_rel, width), BF16)),
        lambda: trail(received, rows, weight, relation_table, relation_ids),
    )
    right = jnp.where(first, rows, grad_pre)
    right_all = lax.all_gather(right, "batch", axis=0, tiled=True)

    half_rel = count_rel // 2
    query_back = lax.ppermute(grad_query, "hop", [(1, 0)])
    rel_back = lax.ppermute(rel_part[:half_rel], "hop", [(1, 0)])
    query_grad = jnp.where(first, query_back, grad_query)
    left = jnp.where(first, query_back, mixed)
    rel_own = jnp.where(first, rel_back, rel_part[half_rel:])

    cols = width // batch
    left_sent = left.reshape(rows_dev, batch, cols).transpose(1, 0, 2)
    left_cols = lax.all_to_all(left_sent, "batch", 0, 0, tiled=True).reshape(total_rows, cols)
    rel_rows = lax.all_to_all(
        rel_own.reshape(batch, half_rel // batch, width), "batch", 0, 0, tiled=True
    )
    relation_grad = jnp.sum(rel_rows.astype(F32), axis=0) * jnp.sqrt(F32(count_rel) / F32(total_rows))
    weight_grad = dot(left_cols, right_all, 0, 0) * (1.0 / jnp.sqrt(F32(total_rows)))
    return weight_grad[None], relation_grad, query_grad


def solution(mesh):
    return jax.shard_map(
        local,
        mesh=mesh,
        in_specs=(P("hop", "batch", None), P("hop", None, None), P(), P("batch")),
        out_specs=(P("hop", "batch", None), P(("hop", "batch"), None), P("batch", None)),
        check_vma=False,
    )
```

```python
import jax
import jax.numpy as jnp
from jax import lax
from jax.sharding import Mesh
from jax.sharding import PartitionSpec as P

F32 = jnp.float32
BF16 = jnp.bfloat16


def dot(a, b, ca, cb):
    return lax.dot_general(a, b, (((ca,), (cb,)), ((), ())), preferred_element_type=F32)


def split_sum(onehot, values):
    head = values.astype(BF16)
    rest = (values - head.astype(F32)).astype(BF16)
    return dot(onehot, head, 0, 0) + dot(onehot, rest, 0, 0)


def swap_core(block):
    return lax.ppermute(block, "core", [(0, 1), (1, 0)])


def local(section_rows, weights, relation_table, relation_ids):
    rows = section_rows[0]
    weight = weights[0]
    rows_dev, width = rows.shape
    half = width // 2
    count_rel = relation_table.shape[0]
    chips = lax.axis_size("chip")
    first = lax.axis_index("hop") == 0
    core = lax.axis_index("core")
    total_rows = rows_dev * chips * 2

    query = dot(rows, weight, 1, 1).astype(BF16)
    query = lax.ppermute(query, "hop", [(0, 1), (1, 0)])

    onehot = (relation_ids[:, None] == lax.iota(jnp.int32, count_rel)[None, :]).astype(BF16)
    rel = dot(onehot, relation_table, 1, 0)
    r_re, r_im = rel[:, :half], rel[:, half:]
    qf = query.astype(F32)
    q_re, q_im = qf[:, :half], qf[:, half:]
    mixed = jnp.concatenate(
        [q_re * r_re - q_im * r_im, q_re * r_im + q_im * r_re], axis=1
    ).astype(BF16)
    pre = dot(mixed, weight, 1, 0)
    sig = jax.nn.sigmoid(pre)
    grad_pre = (rows.astype(F32) * (sig * (1.0 + pre * (1.0 - sig)))).astype(BF16)

    right = jnp.where(first, rows, grad_pre)
    right_all = lax.all_gather(right, "chip", axis=0, tiled=True)

    gz = dot(grad_pre, weight, 1, 1)
    gz_re, gz_im = gz[:, :half], gz[:, half:]
    grad_query = jnp.concatenate(
        [gz_re * r_re + gz_im * r_im, gz_im * r_re - gz_re * r_im], axis=1
    ).astype(BF16)
    query_back = lax.ppermute(grad_query, "hop", [(1, 0)])
    query_grad = jnp.where(first, query_back, grad_query)
    left = jnp.where(first, query_back, mixed)
    cols = width // chips
    left_sent = left.reshape(rows_dev, chips, cols).transpose(1, 0, 2)
    left_cols = lax.all_to_all(left_sent, "chip", 0, 0, tiled=True).reshape(rows_dev * chips, cols)

    grad_rel = jnp.concatenate([gz_re * q_re + gz_im * q_im, gz_im * q_re - gz_re * q_im], axis=1)
    owned = count_rel // (4 * chips)
    rel_part = split_sum(onehot, grad_rel).reshape(2, chips, 2, owned, width)
    rel_keep = lax.dynamic_index_in_dim(rel_part, core, 2, keepdims=False)
    rel_give = lax.dynamic_index_in_dim(rel_part, 1 - core, 2, keepdims=False)
    rel_chip = (rel_keep + swap_core(rel_give)).astype(BF16)
    rel_back = lax.ppermute(rel_chip[0], "hop", [(1, 0)])
    rel_sent = jnp.where(first, rel_back, rel_chip[1])
    rel_rows = lax.all_to_all(rel_sent, "chip", 0, 0, tiled=True)
    relation_grad = jnp.sum(rel_rows.astype(F32), axis=0) * jnp.sqrt(F32(count_rel) / F32(total_rows))

    partial = dot(left_cols, right_all, 0, 0).reshape(2, cols // 2, width)
    keep = lax.dynamic_index_in_dim(partial, core, 0, keepdims=False)
    give = lax.dynamic_index_in_dim(partial, 1 - core, 0, keepdims=False)
    weight_grad = (keep + swap_core(give)) * (1.0 / jnp.sqrt(F32(total_rows)))
    return weight_grad[None], relation_grad, query_grad


def solution(mesh):
    hops, batch = mesh.devices.shape
    fine = Mesh(mesh.devices.reshape(hops, batch // 2, 2), ("hop", "chip", "core"))
    rows = ("chip", "core")
    return jax.shard_map(
        local,
        mesh=fine,
        in_specs=(P("hop", rows, None), P("hop", None, None), P(), P(rows)),
        out_specs=(P("hop", rows, None), P(("hop", "chip", "core"), None), P(rows, None)),
        check_vma=False,
    )
```

```python
import jax
import jax.numpy as jnp
from jax import lax
from jax.sharding import Mesh
from jax.sharding import PartitionSpec as P

F32 = jnp.float32
BF16 = jnp.bfloat16
CHUNKS = 2


def dot(a, b, ca, cb):
    return lax.dot_general(a, b, (((ca,), (cb,)), ((), ())), preferred_element_type=F32)


def split_sum(onehot, values):
    head = values.astype(BF16)
    rest = (values - head.astype(F32)).astype(BF16)
    return dot(onehot, head, 0, 0) + dot(onehot, rest, 0, 0)


def swap_core(block):
    return lax.ppermute(block, "core", [(0, 1), (1, 0)])


def ring_order(chips):
    return list(range(0, chips, 2)) + list(range(1, chips, 2))[::-1]


def local(section_rows, weights, relation_table, relation_ids):
    rows = section_rows[0]
    weight = weights[0]
    rows_dev, width = rows.shape
    half = width // 2
    count_rel = relation_table.shape[0]
    chips = lax.axis_size("chip")
    first = lax.axis_index("hop") == 0
    core = lax.axis_index("core")
    total_rows = rows_dev * chips * 2
    cols = width // chips
    piece = half // CHUNKS
    exchange = [(0, 1), (1, 0)]

    onehot = (relation_ids[:, None] == lax.iota(jnp.int32, count_rel)[None, :]).astype(BF16)
    rel = dot(onehot, relation_table, 1, 0)
    r_re, r_im = rel[:, :half], rel[:, half:]

    sent = []
    for c in range(CHUNKS):
        re = dot(rows, weight[c * piece:(c + 1) * piece], 1, 1)
        im = dot(rows, weight[half + c * piece:half + (c + 1) * piece], 1, 1)
        sent.append(lax.ppermute(jnp.concatenate([re, im], axis=1).astype(BF16), "hop", exchange))

    pre = jnp.zeros((rows_dev, weight.shape[1]), F32)
    q_res, q_ims, z_res, z_ims = [], [], [], []
    for c in range(CHUNKS):
        qf = sent[c].astype(F32)
        q_re, q_im = qf[:, :piece], qf[:, piece:]
        a, b = r_re[:, c * piece:(c + 1) * piece], r_im[:, c * piece:(c + 1) * piece]
        z_re = (q_re * a - q_im * b).astype(BF16)
        z_im = (q_re * b + q_im * a).astype(BF16)
        pre = pre + dot(z_re, weight[c * piece:(c + 1) * piece], 1, 0)
        pre = pre + dot(z_im, weight[half + c * piece:half + (c + 1) * piece], 1, 0)
        q_res.append(q_re)
        q_ims.append(q_im)
        z_res.append(z_re)
        z_ims.append(z_im)
    mixed = jnp.concatenate(z_res + z_ims, axis=1)
    q_re, q_im = jnp.concatenate(q_res, axis=1), jnp.concatenate(q_ims, axis=1)
    sig = jax.nn.sigmoid(pre)
    grad_pre = (rows.astype(F32) * (sig * (1.0 + pre * (1.0 - sig)))).astype(BF16)

    ring = ring_order(chips)
    up = [(ring[i], ring[(i + 1) % chips]) for i in range(chips)]
    down = [(b, a) for a, b in up]
    place = jnp.array([ring.index(i) for i in range(chips)], jnp.int32)[lax.axis_index("chip")]
    chip_at = jnp.array(ring, jnp.int32)
    right = jnp.where(first, rows, grad_pre)
    blocks = [(right, 0)]
    fwd = bwd = right
    for s in range(1, chips // 2 + 1):
        fwd = lax.ppermute(fwd, "chip", up)
        blocks.append((fwd, -s))
        if s < chips - s:
            bwd = lax.ppermute(bwd, "chip", down)
            blocks.append((bwd, s))

    def columns(left):
        return left.reshape(rows_dev, chips, cols).transpose(1, 0, 2)

    mixed_cols = lax.all_to_all(columns(mixed), "chip", 0, 0, tiled=True)

    gz = dot(grad_pre, weight, 1, 1)
    gz_re, gz_im = gz[:, :half], gz[:, half:]
    grad_query = jnp.concatenate(
        [gz_re * r_re + gz_im * r_im, gz_im * r_re - gz_re * r_im], axis=1
    ).astype(BF16)
    query_back = lax.ppermute(grad_query, "hop", [(1, 0)])
    query_grad = jnp.where(first, query_back, grad_query)

    grad_rel = jnp.concatenate([gz_re * q_re + gz_im * q_im, gz_im * q_re - gz_re * q_im], axis=1)
    owned = count_rel // (4 * chips)
    rel_part = split_sum(onehot, grad_rel).reshape(2, chips, 2, owned, width)
    rel_keep = lax.dynamic_index_in_dim(rel_part, core, 2, keepdims=False)
    rel_give = lax.dynamic_index_in_dim(rel_part, 1 - core, 2, keepdims=False)
    rel_chip = (rel_keep + swap_core(rel_give)).astype(BF16)
    rel_sent = rel_chip.transpose(1, 0, 2, 3)

    if rows_dev * cols == 2 * owned * width:
        shared = jnp.where(first, columns(query_back).reshape(chips, 2 * owned, width), rel_sent.reshape(chips, 2 * owned, width))
        shared = lax.all_to_all(shared, "chip", 0, 0, tiled=True)
        query_cols = shared.reshape(chips, rows_dev, cols)
        rel_rows = shared.reshape(chips, 2, owned, width)
    else:
        query_cols = lax.all_to_all(columns(query_back), "chip", 0, 0, tiled=True)
        rel_rows = lax.all_to_all(rel_sent, "chip", 0, 0, tiled=True)
    rel_sum = jnp.sum(rel_rows.astype(F32), axis=0) * jnp.sqrt(F32(count_rel) / F32(total_rows))
    relation_grad = jnp.where(first, lax.ppermute(rel_sum[0], "hop", [(1, 0)]), rel_sum[1])

    left_cols = jnp.where(first, query_cols, mixed_cols)
    partial = jnp.zeros((cols, width), F32)
    for block, step in blocks:
        source = chip_at[(place + step) % chips]
        partial = partial + dot(lax.dynamic_index_in_dim(left_cols, source, 0, keepdims=False), block, 0, 0)
    partial = partial.reshape(2, cols // 2, width)
    keep = lax.dynamic_index_in_dim(partial, core, 0, keepdims=False)
    give = lax.dynamic_index_in_dim(partial, 1 - core, 0, keepdims=False)
    weight_grad = (keep + swap_core(give)) * (1.0 / jnp.sqrt(F32(total_rows)))
    return weight_grad[None], relation_grad, query_grad


def solution(mesh):
    hops, batch = mesh.devices.shape
    fine = Mesh(mesh.devices.reshape(hops, batch // 2, 2), ("hop", "chip", "core"))
    rows = ("chip", "core")
    return jax.shard_map(
        local,
        mesh=fine,
        in_specs=(P("hop", rows, None), P("hop", None, None), P(), P(rows)),
        out_specs=(P("hop", rows, None), P(("hop", "chip", "core"), None), P(rows, None)),
        check_vma=False,
    )
```

```python
import jax
import jax.numpy as jnp
from jax import lax
from jax.experimental import pallas as pl
from jax.experimental.pallas import tpu as pltpu
from jax.sharding import Mesh
from jax.sharding import PartitionSpec as P

F32 = jnp.float32
BF16 = jnp.bfloat16
TILE = 256


def dot(a, b, ca, cb):
    return lax.dot_general(a, b, (((ca,), (cb,)), ((), ())), preferred_element_type=F32)


def swap_core(block):
    return lax.ppermute(block, "core", [(0, 1), (1, 0)])


def mix(q_re, q_im, r_re, r_im):
    return (q_re * r_re - q_im * r_im).astype(BF16), (q_re * r_im + q_im * r_re).astype(BF16)


def trail_body(first, q_re, q_im, rows, weight, rel, onehot, right, query_grad, give, keep, mixed, hidden):
    width = weight.shape[0]
    half = width // 2
    is_first = first[0] == 1
    owned = give.shape[0]

    def at(step, base=0):
        return pl.ds(pl.multiple_of(base + step * TILE, TILE), TILE)

    def make_mixed(step, carry):
        z_re, z_im = mix(
            q_re[:, at(step)].astype(F32), q_im[:, at(step)].astype(F32),
            rel[:, at(step)].astype(F32), rel[:, at(step, half)].astype(F32),
        )
        mixed[:, at(step)] = z_re
        mixed[:, at(step, half)] = z_im
        return carry

    lax.fori_loop(0, half // TILE, make_mixed, 0)

    def make_hidden(step, carry):
        pre = dot(mixed[...], weight[:, at(step)], 1, 0)
        sig = jax.nn.sigmoid(pre)
        cot = rows[:, at(step)]
        grad = (cot.astype(F32) * (sig * (1.0 + pre * (1.0 - sig)))).astype(BF16)
        hidden[:, at(step)] = grad
        right[:, at(step)] = jnp.where(is_first, cot, grad)
        return carry

    lax.fori_loop(0, weight.shape[1] // TILE, make_hidden, 0)

    def make_query(step, carry):
        gz_re = dot(hidden[...], weight[at(step), :], 1, 1)
        gz_im = dot(hidden[...], weight[at(step, half), :], 1, 1)
        r_re, r_im = rel[:, at(step)].astype(F32), rel[:, at(step, half)].astype(F32)
        query_grad[:, at(step)] = (gz_re * r_re + gz_im * r_im).astype(BF16)
        query_grad[:, at(step, half)] = (gz_im * r_re - gz_re * r_im).astype(BF16)
        a, b = q_re[:, at(step)].astype(F32), q_im[:, at(step)].astype(F32)
        for base, grad in ((0, gz_re * a + gz_im * b), (half, gz_im * a - gz_re * b)):
            head = grad.astype(BF16)
            rest = (grad - head.astype(F32)).astype(BF16)
            total = dot(onehot[...], head, 1, 0) + dot(onehot[...], rest, 1, 0)
            give[:, at(step, base)] = total[:owned]
            keep[:, at(step, base)] = total[owned:]
        return carry

    lax.fori_loop(0, half // TILE, make_query, 0)


def trail(first, q_re, q_im, rows, weight, rel, onehot):
    rows_dev, hidden = rows.shape
    width = weight.shape[0]
    count_rel = onehot.shape[0]
    vmem = pl.BlockSpec(memory_space=pltpu.VMEM)
    flops = 4 * rows_dev * width * hidden + 4 * rows_dev * count_rel * width
    return pl.pallas_call(
        trail_body,
        out_shape=(
            jax.ShapeDtypeStruct((rows_dev, hidden), BF16),
            jax.ShapeDtypeStruct((rows_dev, width), BF16),
            jax.ShapeDtypeStruct((count_rel // 2, width), F32),
            jax.ShapeDtypeStruct((count_rel // 2, width), F32),
        ),
        in_specs=[pl.BlockSpec(memory_space=pltpu.SMEM)] + [vmem] * 6,
        out_specs=(vmem,) * 4,
        scratch_shapes=[pltpu.VMEM((rows_dev, width), BF16), pltpu.VMEM((rows_dev, hidden), BF16)],
        compiler_params=pltpu.CompilerParams(vmem_limit_bytes=40 * 1024 * 1024),
        cost_estimate=pl.CostEstimate(
            flops=flops, bytes_accessed=2 * width * hidden, transcendentals=rows_dev * hidden
        ),
    )(first, q_re, q_im, rows, weight, rel, onehot)


def local(section_rows, weights, relation_table, relation_ids):
    rows = section_rows[0]
    weight = weights[0]
    rows_dev, width = rows.shape
    half = width // 2
    count_rel = relation_table.shape[0]
    chips = lax.axis_size("chip")
    first = lax.axis_index("hop") == 0
    core = lax.axis_index("core")
    chip = lax.axis_index("chip")
    total_rows = rows_dev * chips * 2
    cols = width // chips
    owned = count_rel // (4 * chips)

    def columns(left):
        return left.reshape(left.shape[0], chips, cols).transpose(1, 0, 2)

    own_re = dot(rows, weight[:half], 1, 1).astype(BF16)
    q_re = lax.ppermute(own_re, "hop", [(0, 1)])
    own_im = dot(rows, weight[half:], 1, 1).astype(BF16)
    q_im = lax.ppermute(own_im, "hop", [(0, 1)])

    onehot = (relation_ids[:, None] == lax.iota(jnp.int32, count_rel)[None, :]).astype(BF16)
    rel = dot(onehot, relation_table, 1, 0).astype(BF16)
    number = lax.iota(jnp.int32, count_rel)
    side = number // (count_rel // 2)
    dest = number % (count_rel // 2) // (2 * owned)
    hop = number % (2 * owned) // owned
    which_core = jnp.where(side == 1, core, 1 - core)
    relation = ((hop * chips + dest) * 2 + which_core) * owned + number % owned
    onehot_t = (relation[:, None] == relation_ids[None, :]).astype(BF16)

    relf = rel.astype(F32)
    own_z = jnp.concatenate(
        mix(own_re.astype(F32), own_im.astype(F32), relf[:, :half], relf[:, half:]), axis=1
    )
    z_cols = lax.all_to_all(columns(own_z), "chip", 0, 0, tiled=True)

    right, grad_query, rel_give, rel_keep = trail(
        first.astype(jnp.int32).reshape(1), q_re, q_im, rows, weight, rel, onehot_t
    )
    query_back = lax.ppermute(grad_query, "hop", [(1, 0)])
    query_grad = jnp.where(first, query_back, grad_query)
    z_cols, _ = lax.optimization_barrier((z_cols, grad_query))
    z_cols = lax.ppermute(z_cols, "hop", [(0, 1)])
    rel_got = swap_core(rel_give)

    def chip_at(place):
        place = lax.rem(place, chips)
        return jnp.where(place < (chips + 1) // 2, 2 * place, 2 * (chips - place) - 1)

    ring = list(range(0, chips, 2)) + list(range(1, chips, 2))[::-1]
    place = jnp.where(lax.rem(chip, 2) == 0, chip // 2, chips - 1 - chip // 2)
    up = [(ring[i], ring[(i + 1) % chips]) for i in range(chips)]
    down = [(b, a) for a, b in up]
    blocks = [(right, 0)]
    fwd = bwd = right
    for s in range(1, chips // 2 + 1):
        fwd = lax.ppermute(fwd, "chip", up)
        blocks.append((fwd, chips - s))
        if s < chips - s:
            bwd = lax.ppermute(bwd, "chip", down)
            blocks.append((bwd, s))

    rel_sent = (rel_keep + rel_got).astype(BF16).reshape(chips, 2 * owned, chips, cols)
    rel_sent = rel_sent.transpose(0, 2, 1, 3).reshape(chips, 2 * owned * chips, cols)
    if rel_sent.shape[1] == rows_dev:
        shared = jnp.where(first, columns(query_back), rel_sent)
        shared, _ = lax.optimization_barrier((shared, (blocks[1][0], blocks[2][0])))
        query_cols = rel_rows = lax.all_to_all(shared, "chip", 0, 0, tiled=True)
    else:
        query_cols = lax.all_to_all(columns(query_back), "chip", 0, 0, tiled=True)
        rel_rows = lax.all_to_all(rel_sent, "chip", 0, 0, tiled=True)
    rel_sum = jnp.sum(rel_rows.astype(F32), axis=0) * jnp.sqrt(F32(count_rel) / F32(total_rows))
    rel_sum = rel_sum.reshape(chips, 2 * owned, cols).transpose(1, 0, 2).reshape(2, owned, width)
    relation_grad = jnp.where(first, lax.ppermute(rel_sum[0], "hop", [(1, 0)]), rel_sum[1])

    left_cols = jnp.where(first, query_cols, z_cols)
    partial = jnp.zeros((cols, width), F32)
    for block, step in blocks:
        left = lax.dynamic_index_in_dim(left_cols, chip_at(place + step), 0, keepdims=False)
        partial = partial + dot(left, block, 0, 0)
    partial = partial.reshape(2, cols // 2, width)
    keep = lax.dynamic_index_in_dim(partial, core, 0, keepdims=False)
    give = lax.dynamic_index_in_dim(partial, 1 - core, 0, keepdims=False)
    weight_grad = (keep + swap_core(give)) * (1.0 / jnp.sqrt(F32(total_rows)))
    return weight_grad[None], relation_grad, query_grad


def solution(mesh):
    hops, batch = mesh.devices.shape
    fine = Mesh(mesh.devices.reshape(hops, batch // 2, 2), ("hop", "chip", "core"))
    rows = ("chip", "core")
    return jax.shard_map(
        local,
        mesh=fine,
        in_specs=(P("hop", rows, None), P("hop", None, None), P(), P(rows)),
        out_specs=(P("hop", rows, None), P(("hop", "chip", "core"), None), P(rows, None)),
        check_vma=False,
    )
```

```python
import jax
import jax.numpy as jnp
from jax import lax
from jax.experimental import pallas as pl
from jax.experimental.pallas import tpu as pltpu
from jax.sharding import Mesh
from jax.sharding import PartitionSpec as P

F32 = jnp.float32
BF16 = jnp.bfloat16
TILE = 256


def dot(a, b, ca, cb):
    return lax.dot_general(a, b, (((ca,), (cb,)), ((), ())), preferred_element_type=F32)


def swap_core(block):
    return lax.ppermute(block, "core", [(0, 1), (1, 0)])


def mix(q_re, q_im, r_re, r_im):
    return (q_re * r_re - q_im * r_im).astype(BF16), (q_re * r_im + q_im * r_re).astype(BF16)


def at(step, base=0):
    return pl.ds(pl.multiple_of(base + step * TILE, TILE), TILE)


def lead_body(rows, weight, onehot, table, query, mixed, rel, held, sems):
    half = weight.shape[0] // 2
    steps = half // TILE

    def load(step, side):
        piece = at(step, side * half)
        return pltpu.make_async_copy(weight.at[piece], held.at[piece], sems.at[2 * step + side])

    for step in range(steps):
        for side in range(2):
            load(step, side).start()
    for step in range(steps):
        span = pl.ds(step * TILE, TILE)
        r_re = dot(onehot[...], table[:, at(step)], 1, 0)
        r_im = dot(onehot[...], table[:, at(step, half)], 1, 0)
        load(step, 0).wait()
        q_re = dot(rows[...], held[at(step)], 1, 1).astype(BF16)
        load(step, 1).wait()
        q_im = dot(rows[...], held[at(step, half)], 1, 1).astype(BF16)
        query[0, :, span], query[1, :, span] = q_re, q_im
        rel[0, :, span], rel[1, :, span] = r_re.astype(BF16), r_im.astype(BF16)
        z_re, z_im = mix(q_re.astype(F32), q_im.astype(F32), r_re, r_im)
        if mixed.shape[2] == TILE:
            mixed[step], mixed[steps + step] = z_re, z_im
        else:
            mixed[0, :, span], mixed[1, :, span] = z_re, z_im


def lead(rows, weight, onehot, table, chips):
    rows_dev, hidden = rows.shape
    width = weight.shape[0]
    half = width // 2
    cols = width // chips
    count_rel = table.shape[0]
    vmem = pl.BlockSpec(memory_space=pltpu.VMEM)
    pair = jax.ShapeDtypeStruct((2, rows_dev, half), BF16)
    apart = jax.ShapeDtypeStruct((chips, rows_dev, cols), BF16) if cols == TILE else pair
    query, mixed, rel = pl.pallas_call(
        lead_body,
        out_shape=(pair, apart, pair),
        in_specs=[vmem, pl.BlockSpec(memory_space=pltpu.HBM), vmem, vmem],
        out_specs=(vmem,) * 3,
        scratch_shapes=[
            pltpu.VMEM((width, hidden), BF16),
            pltpu.SemaphoreType.DMA((width // TILE,)),
        ],
        compiler_params=pltpu.CompilerParams(vmem_limit_bytes=56 * 1024 * 1024),
        cost_estimate=pl.CostEstimate(
            flops=2 * rows_dev * width * (hidden + count_rel), bytes_accessed=2 * width * hidden, transcendentals=0
        ),
    )(rows, weight, onehot, table)
    if cols != TILE:
        mixed = mixed.reshape(2, rows_dev, chips // 2, cols).transpose(0, 2, 1, 3).reshape(chips, rows_dev, cols)
    return query, mixed, rel


def trail_body(first, query, rows, weight, rel, onehot, right, query_grad, give, keep, mixed, hidden, held, sems):
    width = weight.shape[0]
    half = width // 2
    is_first = first[0] == 1
    owned = give.shape[0]
    tiles = weight.shape[1] // TILE

    def load(step):
        return pltpu.make_async_copy(weight.at[:, at(step)], held.at[:, at(step)], sems.at[step])

    for step in range(tiles):
        load(step).start()

    def make_mixed(step, carry):
        mixed[:, at(step)], mixed[:, at(step, half)] = mix(
            query[0, :, at(step)].astype(F32), query[1, :, at(step)].astype(F32),
            rel[0, :, at(step)].astype(F32), rel[1, :, at(step)].astype(F32),
        )
        return carry

    lax.fori_loop(0, half // TILE, make_mixed, 0)

    def make_hidden(step, carry):
        load(step).wait()
        pre = dot(mixed[...], held[:, at(step)], 1, 0)
        sig = jax.nn.sigmoid(pre)
        cot = rows[:, at(step)]
        grad = (cot.astype(F32) * (sig * (1.0 + pre * (1.0 - sig)))).astype(BF16)
        hidden[:, at(step)] = grad
        right[:, at(step)] = jnp.where(is_first, cot, grad)
        return carry

    lax.fori_loop(0, tiles, make_hidden, 0)

    def make_query(step, carry):
        gz_re = dot(hidden[...], held[at(step), :], 1, 1)
        gz_im = dot(hidden[...], held[at(step, half), :], 1, 1)
        r_re, r_im = rel[0, :, at(step)].astype(F32), rel[1, :, at(step)].astype(F32)
        query_grad[:, at(step)] = (gz_re * r_re + gz_im * r_im).astype(BF16)
        query_grad[:, at(step, half)] = (gz_im * r_re - gz_re * r_im).astype(BF16)
        a, b = query[0, :, at(step)].astype(F32), query[1, :, at(step)].astype(F32)
        for base, grad in ((0, gz_re * a + gz_im * b), (half, gz_im * a - gz_re * b)):
            head = grad.astype(BF16)
            rest = (grad - head.astype(F32)).astype(BF16)
            total = dot(onehot[...], head, 1, 0) + dot(onehot[...], rest, 1, 0)
            give[:, at(step, base)] = total[:owned]
            keep[:, at(step, base)] = total[owned:]
        return carry

    lax.fori_loop(0, half // TILE, make_query, 0)


def trail(first, query, rows, weight, rel, onehot):
    rows_dev, hidden = rows.shape
    width = weight.shape[0]
    count_rel = onehot.shape[0]
    vmem = pl.BlockSpec(memory_space=pltpu.VMEM)
    flops = 4 * rows_dev * width * hidden + 4 * rows_dev * count_rel * width
    return pl.pallas_call(
        trail_body,
        out_shape=(
            jax.ShapeDtypeStruct((rows_dev, hidden), BF16),
            jax.ShapeDtypeStruct((rows_dev, width), BF16),
            jax.ShapeDtypeStruct((count_rel // 2, width), F32),
            jax.ShapeDtypeStruct((count_rel // 2, width), F32),
        ),
        in_specs=[pl.BlockSpec(memory_space=pltpu.SMEM), vmem, vmem, pl.BlockSpec(memory_space=pltpu.HBM), vmem, vmem],
        out_specs=(vmem,) * 4,
        scratch_shapes=[
            pltpu.VMEM((rows_dev, width), BF16),
            pltpu.VMEM((rows_dev, hidden), BF16),
            pltpu.VMEM((width, hidden), BF16),
            pltpu.SemaphoreType.DMA((hidden // TILE,)),
        ],
        compiler_params=pltpu.CompilerParams(vmem_limit_bytes=56 * 1024 * 1024),
        cost_estimate=pl.CostEstimate(
            flops=flops, bytes_accessed=2 * width * hidden, transcendentals=rows_dev * hidden
        ),
    )(first, query, rows, weight, rel, onehot)


def local(section_rows, weights, relation_table, relation_ids):
    rows = section_rows[0]
    weight = weights[0]
    rows_dev, width = rows.shape
    half = width // 2
    count_rel = relation_table.shape[0]
    chips = lax.axis_size("chip")
    first = lax.axis_index("hop") == 0
    core = lax.axis_index("core")
    chip = lax.axis_index("chip")
    total_rows = rows_dev * chips * 2
    cols = width // chips
    owned = count_rel // (4 * chips)

    def columns(left):
        return left.reshape(left.shape[0], chips, cols).transpose(1, 0, 2)

    onehot = (relation_ids[:, None] == lax.iota(jnp.int32, count_rel)[None, :]).astype(BF16)
    number = lax.iota(jnp.int32, count_rel)
    side = number // (count_rel // 2)
    dest = number % (count_rel // 2) // (2 * owned)
    hop = number % (2 * owned) // owned
    which_core = jnp.where(side == 1, core, 1 - core)
    relation = ((hop * chips + dest) * 2 + which_core) * owned + number % owned
    onehot_t = (relation[:, None] == relation_ids[None, :]).astype(BF16)

    own_query, own_mixed, rel = lead(rows, weight, onehot, relation_table, chips)
    query = lax.ppermute(own_query, "hop", [(0, 1)])
    z_cols = lax.all_to_all(own_mixed, "chip", 0, 0, tiled=True)
    query, z_cols = lax.optimization_barrier((query, z_cols))

    right, grad_query, rel_give, rel_keep = trail(
        first.astype(jnp.int32).reshape(1), query, rows, weight, rel, onehot_t
    )
    query_back = lax.ppermute(grad_query, "hop", [(1, 0)])
    query_grad = jnp.where(first, query_back, grad_query)
    z_cols, _ = lax.optimization_barrier((z_cols, grad_query))
    z_cols = lax.ppermute(z_cols, "hop", [(0, 1)])
    rel_got = swap_core(rel_give)

    def chip_at(place):
        place = lax.rem(place, chips)
        return jnp.where(place < (chips + 1) // 2, 2 * place, 2 * (chips - place) - 1)

    ring = list(range(0, chips, 2)) + list(range(1, chips, 2))[::-1]
    place = jnp.where(lax.rem(chip, 2) == 0, chip // 2, chips - 1 - chip // 2)
    up = [(ring[i], ring[(i + 1) % chips]) for i in range(chips)]
    down = [(b, a) for a, b in up]
    blocks = [(right, 0, 0)]
    fwd = bwd = right
    for s in range(1, (chips + 1) // 2):
        fwd = lax.ppermute(fwd, "chip", up)
        bwd = lax.ppermute(bwd, "chip", down)
        blocks += [(fwd, chips - s, 0), (bwd, s, 0)]
    if chips % 2 == 0:
        mid = rows_dev // 2
        blocks.append((lax.ppermute(fwd[:mid], "chip", up), chips // 2, 0))
        blocks.append((lax.ppermute(bwd[mid:], "chip", down), chips // 2, mid))

    rel_sent = (rel_keep + rel_got).astype(BF16).reshape(chips, 2 * owned, chips, cols)
    rel_sent = rel_sent.transpose(0, 2, 1, 3).reshape(chips, 2 * owned * chips, cols)
    if rel_sent.shape[1] == rows_dev:
        shared = jnp.where(first, columns(query_back), rel_sent)
        shared, _ = lax.optimization_barrier((shared, (blocks[1][0], blocks[2][0])))
        query_cols = rel_rows = lax.all_to_all(shared, "chip", 0, 0, tiled=True)
    else:
        query_cols = lax.all_to_all(columns(query_back), "chip", 0, 0, tiled=True)
        rel_rows = lax.all_to_all(rel_sent, "chip", 0, 0, tiled=True)
    rel_sum = jnp.sum(rel_rows.astype(F32), axis=0) * jnp.sqrt(F32(count_rel) / F32(total_rows))
    rel_sum = rel_sum.reshape(chips, 2 * owned, cols).transpose(1, 0, 2).reshape(2, owned, width)
    relation_grad = jnp.where(first, lax.ppermute(rel_sum[0], "hop", [(1, 0)]), rel_sum[1])

    left_cols = jnp.where(first, query_cols, z_cols)
    partial = jnp.zeros((cols, width), F32)
    for block, step, base in blocks:
        left = lax.dynamic_index_in_dim(left_cols, chip_at(place + step), 0, keepdims=False)
        if step == chips // 2:
            left, relation_grad = lax.optimization_barrier((left, relation_grad))
        partial = partial + dot(left[base:base + block.shape[0]], block, 0, 0)
    partial = partial.reshape(2, cols // 2, width)
    keep = lax.dynamic_index_in_dim(partial, core, 0, keepdims=False)
    give = lax.dynamic_index_in_dim(partial, 1 - core, 0, keepdims=False)
    weight_grad = (keep + swap_core(give)) * (1.0 / jnp.sqrt(F32(total_rows)))
    return weight_grad[None], relation_grad, query_grad


def solution(mesh):
    hops, batch = mesh.devices.shape
    fine = Mesh(mesh.devices.reshape(hops, batch // 2, 2), ("hop", "chip", "core"))
    rows = ("chip", "core")
    return jax.shard_map(
        local,
        mesh=fine,
        in_specs=(P("hop", rows, None), P("hop", None, None), P(), P(rows)),
        out_specs=(P("hop", rows, None), P(("hop", "chip", "core"), None), P(rows, None)),
        check_vma=False,
    )
```

```python
import jax
import jax.numpy as jnp
from jax import lax
from jax.experimental import pallas as pl
from jax.experimental.pallas import tpu as pltpu
from jax.sharding import Mesh
from jax.sharding import PartitionSpec as P

F32 = jnp.float32
BF16 = jnp.bfloat16
TILE = 256
GRANT = 16 * 1024 * 1024


def dot(a, b, ca, cb):
    return lax.dot_general(a, b, (((ca,), (cb,)), ((), ())), preferred_element_type=F32)


def swap_core(block):
    return lax.ppermute(block, "core", [(0, 1), (1, 0)])


def mix(q_re, q_im, r_re, r_im):
    return (q_re * r_re - q_im * r_im).astype(BF16), (q_re * r_im + q_im * r_re).astype(BF16)


def at(step, base=0):
    return pl.ds(pl.multiple_of(base + step * TILE, TILE), TILE)


def lead_body(rows, weight, onehot, table, query, mixed, rel):
    half = weight.shape[0] // 2
    steps = half // TILE
    for step in range(steps):
        span = pl.ds(step * TILE, TILE)
        r_re = dot(onehot[...], table[:, at(step)], 1, 0)
        r_im = dot(onehot[...], table[:, at(step, half)], 1, 0)
        q_re = dot(rows[...], weight[at(step)], 1, 1).astype(BF16)
        q_im = dot(rows[...], weight[at(step, half)], 1, 1).astype(BF16)
        query[0, :, span], query[1, :, span] = q_re, q_im
        rel[0, :, span], rel[1, :, span] = r_re.astype(BF16), r_im.astype(BF16)
        z_re, z_im = mix(q_re.astype(F32), q_im.astype(F32), r_re, r_im)
        if mixed.shape[2] == TILE:
            mixed[step], mixed[steps + step] = z_re, z_im
        else:
            mixed[0, :, span], mixed[1, :, span] = z_re, z_im


def lead(rows, weight, onehot, table, chips):
    rows_dev, hidden = rows.shape
    width = weight.shape[0]
    half = width // 2
    cols = width // chips
    count_rel = table.shape[0]
    vmem = pl.BlockSpec(memory_space=pltpu.VMEM)
    pair = jax.ShapeDtypeStruct((2, rows_dev, half), BF16)
    apart = jax.ShapeDtypeStruct((chips, rows_dev, cols), BF16) if cols == TILE else pair
    query, mixed, rel = pl.pallas_call(
        lead_body,
        out_shape=(pair, apart, pair),
        in_specs=[vmem] * 4,
        out_specs=(vmem,) * 3,
        compiler_params=pltpu.CompilerParams(vmem_limit_bytes=GRANT),
        cost_estimate=pl.CostEstimate(
            flops=2 * rows_dev * width * (hidden + count_rel), bytes_accessed=2 * width * hidden, transcendentals=0
        ),
    )(rows, weight, onehot, table)
    if cols != TILE:
        mixed = mixed.reshape(2, rows_dev, chips // 2, cols).transpose(0, 2, 1, 3).reshape(chips, rows_dev, cols)
    return query, mixed, rel


def trail_body(first, query, rows, weight, rel, onehot, right, query_grad, give, keep, mixed, hidden):
    width = weight.shape[0]
    half = width // 2
    is_first = first[0] == 1
    owned = give.shape[0]

    def make_mixed(step, carry):
        mixed[:, at(step)], mixed[:, at(step, half)] = mix(
            query[0, :, at(step)].astype(F32), query[1, :, at(step)].astype(F32),
            rel[0, :, at(step)].astype(F32), rel[1, :, at(step)].astype(F32),
        )
        return carry

    lax.fori_loop(0, half // TILE, make_mixed, 0)

    def make_hidden(step, carry):
        pre = dot(mixed[...], weight[:, at(step)], 1, 0)
        sig = jax.nn.sigmoid(pre)
        cot = rows[:, at(step)]
        grad = (cot.astype(F32) * (sig * (1.0 + pre * (1.0 - sig)))).astype(BF16)
        hidden[:, at(step)] = grad
        right[:, at(step)] = jnp.where(is_first, cot, grad)
        return carry

    lax.fori_loop(0, weight.shape[1] // TILE, make_hidden, 0)

    def make_query(step, carry):
        gz_re = dot(hidden[...], weight[at(step), :], 1, 1)
        gz_im = dot(hidden[...], weight[at(step, half), :], 1, 1)
        r_re, r_im = rel[0, :, at(step)].astype(F32), rel[1, :, at(step)].astype(F32)
        query_grad[:, at(step)] = (gz_re * r_re + gz_im * r_im).astype(BF16)
        query_grad[:, at(step, half)] = (gz_im * r_re - gz_re * r_im).astype(BF16)
        a, b = query[0, :, at(step)].astype(F32), query[1, :, at(step)].astype(F32)
        for base, grad in ((0, gz_re * a + gz_im * b), (half, gz_im * a - gz_re * b)):
            head = grad.astype(BF16)
            rest = (grad - head.astype(F32)).astype(BF16)
            total = dot(onehot[...], head, 1, 0) + dot(onehot[...], rest, 1, 0)
            give[:, at(step, base)] = total[:owned]
            keep[:, at(step, base)] = total[owned:]
        return carry

    lax.fori_loop(0, half // TILE, make_query, 0)


def trail(first, query, rows, weight, rel, onehot):
    rows_dev, hidden = rows.shape
    width = weight.shape[0]
    count_rel = onehot.shape[0]
    vmem = pl.BlockSpec(memory_space=pltpu.VMEM)
    flops = 4 * rows_dev * width * hidden + 4 * rows_dev * count_rel * width
    return pl.pallas_call(
        trail_body,
        out_shape=(
            jax.ShapeDtypeStruct((rows_dev, hidden), BF16),
            jax.ShapeDtypeStruct((rows_dev, width), BF16),
            jax.ShapeDtypeStruct((count_rel // 2, width), F32),
            jax.ShapeDtypeStruct((count_rel // 2, width), F32),
        ),
        in_specs=[pl.BlockSpec(memory_space=pltpu.SMEM)] + [vmem] * 5,
        out_specs=(vmem,) * 4,
        scratch_shapes=[pltpu.VMEM((rows_dev, width), BF16), pltpu.VMEM((rows_dev, hidden), BF16)],
        compiler_params=pltpu.CompilerParams(vmem_limit_bytes=GRANT),
        cost_estimate=pl.CostEstimate(
            flops=flops, bytes_accessed=4 * width * hidden, transcendentals=rows_dev * hidden
        ),
    )(first, query, rows, weight, rel, onehot)


def local(section_rows, weights, relation_table, relation_ids):
    rows = section_rows[0]
    weight = weights[0]
    rows_dev, width = rows.shape
    half = width // 2
    count_rel = relation_table.shape[0]
    chips = lax.axis_size("chip")
    first = lax.axis_index("hop") == 0
    core = lax.axis_index("core")
    chip = lax.axis_index("chip")
    total_rows = rows_dev * chips * 2
    cols = width // chips
    owned = count_rel // (4 * chips)

    def columns(left):
        return left.reshape(left.shape[0], chips, cols).transpose(1, 0, 2)

    onehot = (relation_ids[:, None] == lax.iota(jnp.int32, count_rel)[None, :]).astype(BF16)
    number = lax.iota(jnp.int32, count_rel)
    side = number // (count_rel // 2)
    dest = number % (count_rel // 2) // (2 * owned)
    hop = number % (2 * owned) // owned
    which_core = jnp.where(side == 1, core, 1 - core)
    relation = ((hop * chips + dest) * 2 + which_core) * owned + number % owned
    onehot_t = (relation[:, None] == relation_ids[None, :]).astype(BF16)

    own_query, own_mixed, rel = lead(rows, weight, onehot, relation_table, chips)
    query = lax.ppermute(own_query, "hop", [(0, 1)])
    z_cols = lax.all_to_all(own_mixed, "chip", 0, 0, tiled=True)

    right, grad_query, rel_give, rel_keep = trail(
        first.astype(jnp.int32).reshape(1), query, rows, weight, rel, onehot_t
    )
    query_back = lax.ppermute(grad_query, "hop", [(1, 0)])
    query_grad = jnp.where(first, query_back, grad_query)
    z_cols, right = lax.optimization_barrier((z_cols, right))
    z_cols = lax.ppermute(z_cols, "hop", [(0, 1)])
    rel_got = swap_core(rel_give)

    def chip_at(place):
        place = lax.rem(place, chips)
        return jnp.where(place < (chips + 1) // 2, 2 * place, 2 * (chips - place) - 1)

    ring = list(range(0, chips, 2)) + list(range(1, chips, 2))[::-1]
    place = jnp.where(lax.rem(chip, 2) == 0, chip // 2, chips - 1 - chip // 2)
    up = [(ring[i], ring[(i + 1) % chips]) for i in range(chips)]
    down = [(b, a) for a, b in up]
    blocks = [(right, 0, 0)]
    mid = rows_dev // 2
    fwd = bwd = [right[:mid], right[mid:]]
    for s in range(1, (chips + 1) // 2):
        fwd = [lax.ppermute(part, "chip", up) for part in fwd]
        bwd = [lax.ppermute(part, "chip", down) for part in bwd]
        for base, ahead, behind in zip((0, mid), fwd, bwd):
            blocks += [(ahead, chips - s, base), (behind, s, base)]
    if chips % 2 == 0:
        blocks.append((lax.ppermute(fwd[0], "chip", up), chips // 2, 0))
        blocks.append((lax.ppermute(bwd[1], "chip", down), chips // 2, mid))

    rel_sent = (rel_keep + rel_got).astype(BF16).reshape(chips, 2 * owned, chips, cols)
    rel_sent = rel_sent.transpose(0, 2, 1, 3).reshape(chips, 2 * owned * chips, cols)
    if rel_sent.shape[1] == rows_dev:
        shared = jnp.where(first, columns(query_back), rel_sent)
        shared, _ = lax.optimization_barrier((shared, tuple(block for block, _, _ in blocks[1:5])))
        query_cols = rel_rows = lax.all_to_all(shared, "chip", 0, 0, tiled=True)
    else:
        query_cols = lax.all_to_all(columns(query_back), "chip", 0, 0, tiled=True)
        rel_rows = lax.all_to_all(rel_sent, "chip", 0, 0, tiled=True)
    rel_sum = jnp.sum(rel_rows.astype(F32), axis=0) * jnp.sqrt(F32(count_rel) / F32(total_rows))
    rel_sum = rel_sum.reshape(chips, 2 * owned, cols).transpose(1, 0, 2).reshape(2, owned, width)
    relation_grad = jnp.where(first, lax.ppermute(rel_sum[0], "hop", [(1, 0)]), rel_sum[1])

    left_cols = jnp.where(first, query_cols, z_cols)
    partial = jnp.zeros((cols, width), F32)
    for block, step, base in blocks:
        left = lax.dynamic_index_in_dim(left_cols, chip_at(place + step), 0, keepdims=False)
        if step == chips // 2:
            left, relation_grad = lax.optimization_barrier((left, relation_grad))
        partial = partial + dot(left[base:base + block.shape[0]], block, 0, 0)
    partial = partial.reshape(2, cols // 2, width)
    keep = lax.dynamic_index_in_dim(partial, core, 0, keepdims=False)
    give = lax.dynamic_index_in_dim(partial, 1 - core, 0, keepdims=False)
    weight_grad = (keep + swap_core(give)) * (1.0 / jnp.sqrt(F32(total_rows)))
    return weight_grad[None], relation_grad, query_grad


def solution(mesh):
    hops, batch = mesh.devices.shape
    fine = Mesh(mesh.devices.reshape(hops, batch // 2, 2), ("hop", "chip", "core"))
    rows = ("chip", "core")
    return jax.shard_map(
        local,
        mesh=fine,
        in_specs=(P("hop", rows, None), P("hop", None, None), P(), P(rows)),
        out_specs=(P("hop", rows, None), P(("hop", "chip", "core"), None), P(rows, None)),
        check_vma=False,
    )
```

```python
import jax
import jax.numpy as jnp
from jax import lax
from jax.experimental import pallas as pl
from jax.experimental.pallas import tpu as pltpu
from jax.sharding import Mesh
from jax.sharding import PartitionSpec as P

F32 = jnp.float32
BF16 = jnp.bfloat16
TILE = 256


def dot(a, b, ca, cb):
    return lax.dot_general(a, b, (((ca,), (cb,)), ((), ())), preferred_element_type=F32)


def swap_core(block):
    return lax.ppermute(block, "core", [(0, 1), (1, 0)])


def mix(q_re, q_im, r_re, r_im):
    return (q_re * r_re - q_im * r_im).astype(BF16), (q_re * r_im + q_im * r_re).astype(BF16)


def at(step, base=0):
    return pl.ds(pl.multiple_of(base + step * TILE, TILE), TILE)


def fetch(pairs, sems):
    copies = [pltpu.make_async_copy(source, target, sems.at[i]) for i, (source, target) in enumerate(pairs)]
    for copy in copies:
        copy.start()
    return copies


def wait(copies):
    for copy in copies:
        copy.wait()


def call(body, outs, args, scratch, grant, flops, moved):
    return pl.pallas_call(
        body,
        out_shape=outs,
        in_specs=[
            pl.BlockSpec(memory_space=pltpu.SMEM if arg.ndim == 1 else pl.ANY) for arg in args
        ],
        out_specs=(pl.BlockSpec(memory_space=pl.ANY),) * len(outs),
        scratch_shapes=scratch,
        compiler_params=pltpu.CompilerParams(vmem_limit_bytes=grant * 1024 * 1024),
        cost_estimate=pl.CostEstimate(flops=flops, bytes_accessed=moved, transcendentals=0),
    )(*args)


def room(*arrays):
    return [pltpu.VMEM(array.shape, array.dtype) for array in arrays]


def lead_body(
    rows_at, weight_at, onehot_at, table_at, query_at, mixed_at, rel_at,
    rows, weight, onehot, table, query, mixed, rel, small, large, stored,
):
    half = weight.shape[0] // 2
    steps = half // TILE
    early = fetch([(onehot_at, onehot), (rows_at, rows), (table_at, table)], small)
    pieces = [at(step, base) for step in range(steps) for base in (0, half)]
    loads = fetch([(weight_at.at[piece], weight.at[piece]) for piece in pieces], large)
    wait(early)
    for step in range(steps):
        span = pl.ds(step * TILE, TILE)
        r_re = dot(onehot[...], table[:, at(step)], 1, 0)
        r_im = dot(onehot[...], table[:, at(step, half)], 1, 0)
        rel[0, :, span], rel[1, :, span] = r_re.astype(BF16), r_im.astype(BF16)
        wait(loads[2 * step:2 * step + 2])
        q_re = dot(rows[...], weight[at(step)], 1, 1).astype(BF16)
        q_im = dot(rows[...], weight[at(step, half)], 1, 1).astype(BF16)
        query[0, :, span], query[1, :, span] = q_re, q_im
        z_re, z_im = mix(q_re.astype(F32), q_im.astype(F32), r_re, r_im)
        if mixed.shape[2] == TILE:
            mixed[step], mixed[steps + step] = z_re, z_im
        else:
            mixed[0, :, span], mixed[1, :, span] = z_re, z_im
    wait(fetch([(query, query_at), (mixed, mixed_at), (rel, rel_at)], stored))


def lead(rows, weight, onehot, table, chips):
    rows_dev, hidden = rows.shape
    width = weight.shape[0]
    half = width // 2
    cols = width // chips
    count_rel = table.shape[0]
    pair = jax.ShapeDtypeStruct((2, rows_dev, half), BF16)
    apart = jax.ShapeDtypeStruct((chips, rows_dev, cols), BF16) if cols == TILE else pair
    outs = (pair, apart, pair)
    args = (rows, weight, onehot, table)
    dma = pltpu.SemaphoreType.DMA
    query, mixed, rel = call(
        lead_body, outs, args,
        room(*args, *outs) + [dma((3,)), dma((width // TILE,)), dma((3,))],
        56, 2 * rows_dev * width * (hidden + count_rel), 2 * width * hidden,
    )
    if cols != TILE:
        mixed = mixed.reshape(2, rows_dev, chips // 2, cols).transpose(0, 2, 1, 3).reshape(chips, rows_dev, cols)
    return query, mixed, rel


def trail_body(
    first, query_at, rows_at, weight_at, rel_at, onehot_at, right_at, grad_at, give_at, keep_at,
    query, rows, weight, rel, onehot, right, query_grad, give, keep, mixed, hidden, small, large, stored, last,
):
    width = weight.shape[0]
    half = width // 2
    is_first = first[0] == 1
    owned = give.shape[0]
    early = fetch([(query_at, query), (rel_at, rel), (rows_at, rows), (onehot_at, onehot)], small)
    pieces = [at(step) for step in range(weight.shape[1] // TILE)]
    loads = fetch([(weight_at.at[:, piece], weight.at[:, piece]) for piece in pieces], large)
    wait(early)

    def make_mixed(step, carry):
        mixed[:, at(step)], mixed[:, at(step, half)] = mix(
            query[0, :, at(step)].astype(F32), query[1, :, at(step)].astype(F32),
            rel[0, :, at(step)].astype(F32), rel[1, :, at(step)].astype(F32),
        )
        return carry

    lax.fori_loop(0, half // TILE, make_mixed, 0)

    for step, load in enumerate(loads):
        load.wait()
        pre = dot(mixed[...], weight[:, at(step)], 1, 0)
        sig = jax.nn.sigmoid(pre)
        cot = rows[:, at(step)]
        grad = (cot.astype(F32) * (sig * (1.0 + pre * (1.0 - sig)))).astype(BF16)
        hidden[:, at(step)] = grad
        right[:, at(step)] = jnp.where(is_first, cot, grad)
    send = fetch([(right, right_at)], stored)

    def make_query(step, carry):
        gz_re = dot(hidden[...], weight[at(step), :], 1, 1)
        gz_im = dot(hidden[...], weight[at(step, half), :], 1, 1)
        r_re, r_im = rel[0, :, at(step)].astype(F32), rel[1, :, at(step)].astype(F32)
        query_grad[:, at(step)] = (gz_re * r_re + gz_im * r_im).astype(BF16)
        query_grad[:, at(step, half)] = (gz_im * r_re - gz_re * r_im).astype(BF16)
        a, b = query[0, :, at(step)].astype(F32), query[1, :, at(step)].astype(F32)
        for base, grad in ((0, gz_re * a + gz_im * b), (half, gz_im * a - gz_re * b)):
            head = grad.astype(BF16)
            rest = (grad - head.astype(F32)).astype(BF16)
            total = dot(onehot[...], head, 1, 0) + dot(onehot[...], rest, 1, 0)
            give[:, at(step, base)] = total[:owned]
            keep[:, at(step, base)] = total[owned:]
        return carry

    lax.fori_loop(0, half // TILE, make_query, 0)
    wait(fetch([(query_grad, grad_at), (give, give_at), (keep, keep_at)], last) + send)


def trail(first, query, rows, weight, rel, onehot):
    rows_dev, hidden = rows.shape
    width = weight.shape[0]
    count_rel = onehot.shape[0]
    partial = jax.ShapeDtypeStruct((count_rel // 2, width), F32)
    outs = (
        jax.ShapeDtypeStruct((rows_dev, hidden), BF16), jax.ShapeDtypeStruct((rows_dev, width), BF16),
        partial, partial,
    )
    args = (query, rows, weight, rel, onehot)
    dma = pltpu.SemaphoreType.DMA
    scratch = room(*args, *outs) + [pltpu.VMEM((rows_dev, width), BF16), pltpu.VMEM((rows_dev, hidden), BF16)]
    return call(
        trail_body, outs, (first,) + args,
        scratch + [dma((4,)), dma((hidden // TILE,)), dma((1,)), dma((3,))],
        56, 4 * rows_dev * width * (hidden + count_rel), 4 * width * hidden,
    )


def product_body(parts, before, order, left_at, *refs):
    count = sum(len(part) for part in parts)
    inputs = refs[:count + before]
    outs = refs[count + before:count + before + 2]
    left, blocks = refs[count + before + 2], refs[count + before + 3:-4]
    sums = refs[-4:-2]
    sems, stored = refs[-2:]
    pairs = [(left_at, left)] + list(zip(inputs[:count], blocks))
    pairs += list(zip(inputs[count:], sums)) if before else []
    wait(fetch(pairs, sems))
    owned = sums[0].shape[0]

    def column(step, carry):
        acc = jnp.zeros((left.shape[2], TILE), F32)
        taken = 0
        for number, part in enumerate(parts):
            block = jnp.concatenate([blocks[taken + i][:, at(step)] for i in range(len(part))], axis=0)
            taken += len(part)
            acc = acc + dot(left[order[number]], block, 0, 0)
        for i in range(2):
            half = acc[i * owned:(i + 1) * owned]
            sums[i][:, at(step)] = sums[i][:, at(step)] + half if before else half
        return carry

    lax.fori_loop(0, sums[0].shape[1] // TILE, column, 0)
    wait(fetch(list(zip(sums, outs)), stored))


def product(order, left, parts, before):
    chips, rows_dev, cols = left.shape
    width = parts[0][0].shape[1]
    blocks = [block for part in parts for block in part]
    partial = jax.ShapeDtypeStruct((cols // 2, width), F32)
    dma = pltpu.SemaphoreType.DMA

    def body(*refs):
        product_body(parts, len(before), *refs)

    return call(
        body, (partial, partial), (order, left, *blocks, *before),
        room(left, *blocks, partial, partial)
        + [dma((1 + len(blocks) + len(before),)), dma((2,))],
        48, 2 * cols * width * rows_dev * len(parts), 2 * width * rows_dev * len(parts),
    )


def local(section_rows, weights, relation_table, relation_ids):
    rows = section_rows[0]
    weight = weights[0]
    rows_dev, width = rows.shape
    half = width // 2
    count_rel = relation_table.shape[0]
    chips = lax.axis_size("chip")
    first = lax.axis_index("hop") == 0
    core = lax.axis_index("core")
    chip = lax.axis_index("chip")
    total_rows = rows_dev * chips * 2
    cols = width // chips
    owned = count_rel // (4 * chips)

    def columns(left):
        return left.reshape(left.shape[0], chips, cols).transpose(1, 0, 2)

    onehot = (relation_ids[:, None] == lax.iota(jnp.int32, count_rel)[None, :]).astype(BF16)
    number = lax.iota(jnp.int32, count_rel)
    side = number // (count_rel // 2)
    dest = number % (count_rel // 2) // (2 * owned)
    hop = number % (2 * owned) // owned
    which_core = jnp.where(side == 1, core, 1 - core)
    relation = ((hop * chips + dest) * 2 + which_core) * owned + number % owned
    onehot_t = (relation[:, None] == relation_ids[None, :]).astype(BF16)

    own_query, own_mixed, rel = lead(rows, weight, onehot, relation_table, chips)
    query = lax.ppermute(own_query, "hop", [(0, 1)])
    z_cols = lax.all_to_all(own_mixed, "chip", 0, 0, tiled=True)

    right, grad_query, rel_give, rel_keep = trail(
        first.astype(jnp.int32).reshape(1), query, rows, weight, rel, onehot_t
    )
    query_back = lax.ppermute(grad_query, "hop", [(1, 0)])
    query_grad = jnp.where(first, query_back, grad_query)
    z_cols, right = lax.optimization_barrier((z_cols, right))
    z_cols = lax.ppermute(z_cols, "hop", [(0, 1)])
    rel_got = swap_core(rel_give)

    def chip_at(place):
        place = lax.rem(place, chips)
        return jnp.where(place < (chips + 1) // 2, 2 * place, 2 * (chips - place) - 1)

    ring = list(range(0, chips, 2)) + list(range(1, chips, 2))[::-1]
    place = jnp.where(lax.rem(chip, 2) == 0, chip // 2, chips - 1 - chip // 2)
    up = [(ring[i], ring[(i + 1) % chips]) for i in range(chips)]
    down = [(b, a) for a, b in up]
    mid = rows_dev // 2
    fwd = bwd = (right[:mid], right[mid:])
    parts = [((right,), 0)]
    for s in range(1, (chips + 1) // 2):
        fwd = tuple(lax.ppermute(part, "chip", up) for part in fwd)
        bwd = tuple(lax.ppermute(part, "chip", down) for part in bwd)
        parts += [(fwd, chips - s), (bwd, s)]
    if chips % 2 == 0:
        far = (lax.ppermute(fwd[0], "chip", up), lax.ppermute(bwd[1], "chip", down))
        parts.append((far, chips // 2))

    rel_sent = (rel_keep + rel_got).astype(BF16).reshape(chips, 2 * owned, chips, cols)
    rel_sent = rel_sent.transpose(0, 2, 1, 3).reshape(chips, 2 * owned * chips, cols)
    if rel_sent.shape[1] == rows_dev:
        shared = jnp.where(first, columns(query_back), rel_sent)
        shared, _ = lax.optimization_barrier((shared, (parts[3][0][0], parts[4][0][0], z_cols)))
        query_cols = rel_rows = lax.all_to_all(shared, "chip", 0, 0, tiled=True)
    else:
        query_cols = lax.all_to_all(columns(query_back), "chip", 0, 0, tiled=True)
        rel_rows = lax.all_to_all(rel_sent, "chip", 0, 0, tiled=True)
    rel_sum = jnp.sum(rel_rows.astype(F32), axis=0) * jnp.sqrt(F32(count_rel) / F32(total_rows))
    rel_sum = rel_sum.reshape(chips, 2 * owned, cols).transpose(1, 0, 2).reshape(2, owned, width)
    relation_grad = jnp.where(first, lax.ppermute(rel_sum[0], "hop", [(1, 0)]), rel_sum[1])

    left_cols = jnp.where(first, query_cols, z_cols)
    lower, upper = left_cols[..., :cols // 2], left_cols[..., cols // 2:]
    left_cols = jnp.concatenate(
        [jnp.where(core == 0, upper, lower), jnp.where(core == 0, lower, upper)], axis=2
    )
    sums = ()
    split = len(parts) - 3
    for group in (parts[:split], parts[split:]):
        order = jnp.stack([chip_at(place + step) for _, step in group])
        sums = product(order, left_cols, [part for part, _ in group], sums)
        left_cols, relation_grad = lax.optimization_barrier((left_cols, relation_grad))
    give, keep = sums
    weight_grad = (keep + swap_core(give)) * (1.0 / jnp.sqrt(F32(total_rows)))
    return weight_grad[None], relation_grad, query_grad


def solution(mesh):
    hops, batch = mesh.devices.shape
    fine = Mesh(mesh.devices.reshape(hops, batch // 2, 2), ("hop", "chip", "core"))
    rows = ("chip", "core")
    return jax.shard_map(
        local,
        mesh=fine,
        in_specs=(P("hop", rows, None), P("hop", None, None), P(), P(rows)),
        out_specs=(P("hop", rows, None), P(("hop", "chip", "core"), None), P(rows, None)),
        check_vma=False,
    )
```

```python
import jax
import jax.numpy as jnp
from jax import lax
from jax.experimental import pallas as pl
from jax.experimental.pallas import tpu as pltpu
from jax.sharding import Mesh
from jax.sharding import PartitionSpec as P

F32 = jnp.float32
BF16 = jnp.bfloat16
TILE = 256
GRANT = 16 * 1024 * 1024
LEAD_GRANT = 40 * 1024 * 1024


def dot(a, b, ca, cb):
    return lax.dot_general(a, b, (((ca,), (cb,)), ((), ())), preferred_element_type=F32)


def swap_core(block):
    return lax.ppermute(block, "core", [(0, 1), (1, 0)])


def mix(q_re, q_im, r_re, r_im):
    return (q_re * r_re - q_im * r_im).astype(BF16), (q_re * r_im + q_im * r_re).astype(BF16)


def at(step, base=0):
    return pl.ds(pl.multiple_of(base + step * TILE, TILE), TILE)


def lead_body(
    rows_at, weight_at, onehot_at, table_at, query, mixed, rel, rows, weight, onehot, table, small, large
):
    half = weight.shape[0] // 2
    steps = half // TILE
    early = [
        pltpu.make_async_copy(source, target, small.at[i])
        for i, (source, target) in enumerate([(onehot_at, onehot), (rows_at, rows), (table_at, table)])
    ]
    pieces = [at(step, base) for step in range(steps) for base in (0, half)]
    loads = [
        pltpu.make_async_copy(weight_at.at[piece], weight.at[piece], large.at[i])
        for i, piece in enumerate(pieces)
    ]
    for copy in early + loads:
        copy.start()
    for copy in early:
        copy.wait()
    for step in range(steps):
        span = pl.ds(step * TILE, TILE)
        r_re = dot(onehot[...], table[:, at(step)], 1, 0)
        r_im = dot(onehot[...], table[:, at(step, half)], 1, 0)
        rel[0, :, span], rel[1, :, span] = r_re.astype(BF16), r_im.astype(BF16)
        loads[2 * step].wait()
        q_re = dot(rows[...], weight[at(step)], 1, 1).astype(BF16)
        loads[2 * step + 1].wait()
        q_im = dot(rows[...], weight[at(step, half)], 1, 1).astype(BF16)
        query[0, :, span], query[1, :, span] = q_re, q_im
        z_re, z_im = mix(q_re.astype(F32), q_im.astype(F32), r_re, r_im)
        if mixed.shape[2] == TILE:
            mixed[step], mixed[steps + step] = z_re, z_im
        else:
            mixed[0, :, span], mixed[1, :, span] = z_re, z_im


def lead(rows, weight, onehot, table, chips):
    rows_dev, hidden = rows.shape
    width = weight.shape[0]
    half = width // 2
    cols = width // chips
    count_rel = table.shape[0]
    vmem = pl.BlockSpec(memory_space=pltpu.VMEM)
    pair = jax.ShapeDtypeStruct((2, rows_dev, half), BF16)
    apart = jax.ShapeDtypeStruct((chips, rows_dev, cols), BF16) if cols == TILE else pair
    held = [jax.ShapeDtypeStruct(array.shape, BF16) for array in (rows, weight)]
    query, mixed, rel, rows, weight = pl.pallas_call(
        lead_body,
        out_shape=(pair, apart, pair, *held),
        in_specs=[pl.BlockSpec(memory_space=pl.ANY)] * 4,
        out_specs=(vmem,) * 5,
        scratch_shapes=[
            pltpu.VMEM(onehot.shape, BF16), pltpu.VMEM(table.shape, BF16),
            pltpu.SemaphoreType.DMA((3,)), pltpu.SemaphoreType.DMA((width // TILE,)),
        ],
        compiler_params=pltpu.CompilerParams(vmem_limit_bytes=LEAD_GRANT),
        cost_estimate=pl.CostEstimate(
            flops=2 * rows_dev * width * (hidden + count_rel), bytes_accessed=2 * width * hidden, transcendentals=0
        ),
    )(rows, weight, onehot, table)
    if cols != TILE:
        mixed = mixed.reshape(2, rows_dev, chips // 2, cols).transpose(0, 2, 1, 3).reshape(chips, rows_dev, cols)
    return query, mixed, rel, rows, weight


def trail_body(first, query, rows, weight, rel, onehot, right, query_grad, give, keep, mixed, hidden):
    width = weight.shape[0]
    half = width // 2
    is_first = first[0] == 1
    owned = give.shape[0]

    def make_mixed(step, carry):
        mixed[:, at(step)], mixed[:, at(step, half)] = mix(
            query[0, :, at(step)].astype(F32), query[1, :, at(step)].astype(F32),
            rel[0, :, at(step)].astype(F32), rel[1, :, at(step)].astype(F32),
        )
        return carry

    lax.fori_loop(0, half // TILE, make_mixed, 0)

    def make_hidden(step, carry):
        pre = dot(mixed[...], weight[:, at(step)], 1, 0)
        sig = jax.nn.sigmoid(pre)
        cot = rows[:, at(step)]
        grad = (cot.astype(F32) * (sig * (1.0 + pre * (1.0 - sig)))).astype(BF16)
        hidden[:, at(step)] = grad
        right[:, at(step)] = jnp.where(is_first, cot, grad)
        return carry

    lax.fori_loop(0, weight.shape[1] // TILE, make_hidden, 0)

    def make_query(step, carry):
        gz_re = dot(hidden[...], weight[at(step), :], 1, 1)
        gz_im = dot(hidden[...], weight[at(step, half), :], 1, 1)
        r_re, r_im = rel[0, :, at(step)].astype(F32), rel[1, :, at(step)].astype(F32)
        query_grad[:, at(step)] = (gz_re * r_re + gz_im * r_im).astype(BF16)
        query_grad[:, at(step, half)] = (gz_im * r_re - gz_re * r_im).astype(BF16)
        a, b = query[0, :, at(step)].astype(F32), query[1, :, at(step)].astype(F32)
        for base, grad in ((0, gz_re * a + gz_im * b), (half, gz_im * a - gz_re * b)):
            head = grad.astype(BF16)
            rest = (grad - head.astype(F32)).astype(BF16)
            total = dot(onehot[...], head, 1, 0) + dot(onehot[...], rest, 1, 0)
            give[:, at(step, base)] = total[:owned]
            keep[:, at(step, base)] = total[owned:]
        return carry

    lax.fori_loop(0, half // TILE, make_query, 0)


def trail(first, query, rows, weight, rel, onehot):
    rows_dev, hidden = rows.shape
    width = weight.shape[0]
    count_rel = onehot.shape[0]
    vmem = pl.BlockSpec(memory_space=pltpu.VMEM)
    flops = 4 * rows_dev * width * hidden + 4 * rows_dev * count_rel * width
    return pl.pallas_call(
        trail_body,
        out_shape=(
            jax.ShapeDtypeStruct((rows_dev, hidden), BF16),
            jax.ShapeDtypeStruct((rows_dev, width), BF16),
            jax.ShapeDtypeStruct((count_rel // 2, width), F32),
            jax.ShapeDtypeStruct((count_rel // 2, width), F32),
        ),
        in_specs=[pl.BlockSpec(memory_space=pltpu.SMEM)] + [vmem] * 5,
        out_specs=(vmem,) * 4,
        scratch_shapes=[pltpu.VMEM((rows_dev, width), BF16), pltpu.VMEM((rows_dev, hidden), BF16)],
        compiler_params=pltpu.CompilerParams(vmem_limit_bytes=GRANT),
        cost_estimate=pl.CostEstimate(
            flops=flops, bytes_accessed=4 * width * hidden, transcendentals=rows_dev * hidden
        ),
    )(first, query, rows, weight, rel, onehot)


def local(section_rows, weights, relation_table, relation_ids):
    rows = section_rows[0]
    weight = weights[0]
    rows_dev, width = rows.shape
    half = width // 2
    count_rel = relation_table.shape[0]
    chips = lax.axis_size("chip")
    first = lax.axis_index("hop") == 0
    core = lax.axis_index("core")
    chip = lax.axis_index("chip")
    total_rows = rows_dev * chips * 2
    cols = width // chips
    owned = count_rel // (4 * chips)

    def columns(left):
        return left.reshape(left.shape[0], chips, cols).transpose(1, 0, 2)

    onehot = (relation_ids[:, None] == lax.iota(jnp.int32, count_rel)[None, :]).astype(BF16)
    number = lax.iota(jnp.int32, count_rel)
    side = number // (count_rel // 2)
    dest = number % (count_rel // 2) // (2 * owned)
    hop = number % (2 * owned) // owned
    which_core = jnp.where(side == 1, core, 1 - core)
    relation = ((hop * chips + dest) * 2 + which_core) * owned + number % owned
    onehot_t = (relation[:, None] == relation_ids[None, :]).astype(BF16)

    own_query, own_mixed, rel, rows, weight = lead(rows, weight, onehot, relation_table, chips)
    query = lax.ppermute(own_query, "hop", [(0, 1)])
    z_cols = lax.all_to_all(own_mixed, "chip", 0, 0, tiled=True)

    right, grad_query, rel_give, rel_keep = trail(
        first.astype(jnp.int32).reshape(1), query, rows, weight, rel, onehot_t
    )
    query_back = lax.ppermute(grad_query, "hop", [(1, 0)])
    query_grad = jnp.where(first, query_back, grad_query)
    z_cols, right = lax.optimization_barrier((z_cols, right))
    z_cols = lax.ppermute(z_cols, "hop", [(0, 1)])
    rel_got = swap_core(rel_give)

    def chip_at(place):
        place = lax.rem(place, chips)
        return jnp.where(place < (chips + 1) // 2, 2 * place, 2 * (chips - place) - 1)

    ring = list(range(0, chips, 2)) + list(range(1, chips, 2))[::-1]
    place = jnp.where(lax.rem(chip, 2) == 0, chip // 2, chips - 1 - chip // 2)
    up = [(ring[i], ring[(i + 1) % chips]) for i in range(chips)]
    down = [(b, a) for a, b in up]
    blocks = [(right, 0, 0)]
    fwd = bwd = right
    for s in range(1, (chips + 1) // 2):
        fwd = lax.ppermute(fwd, "chip", up)
        bwd = lax.ppermute(bwd, "chip", down)
        blocks += [(fwd, chips - s, 0), (bwd, s, 0)]
    if chips % 2 == 0:
        mid = rows_dev // 2
        blocks.append((lax.ppermute(fwd[:mid], "chip", up), chips // 2, 0))
        blocks.append((lax.ppermute(bwd[mid:], "chip", down), chips // 2, mid))

    rel_sent = (rel_keep + rel_got).astype(BF16).reshape(chips, 2 * owned, chips, cols)
    rel_sent = rel_sent.transpose(0, 2, 1, 3).reshape(chips, 2 * owned * chips, cols)
    if rel_sent.shape[1] == rows_dev:
        shared = jnp.where(first, columns(query_back), rel_sent)
        shared, _ = lax.optimization_barrier((shared, (blocks[1][0], blocks[2][0])))
        query_cols = rel_rows = lax.all_to_all(shared, "chip", 0, 0, tiled=True)
    else:
        query_cols = lax.all_to_all(columns(query_back), "chip", 0, 0, tiled=True)
        rel_rows = lax.all_to_all(rel_sent, "chip", 0, 0, tiled=True)
    rel_sum = jnp.sum(rel_rows.astype(F32), axis=0) * jnp.sqrt(F32(count_rel) / F32(total_rows))
    rel_sum = rel_sum.reshape(chips, 2 * owned, cols).transpose(1, 0, 2).reshape(2, owned, width)
    relation_grad = jnp.where(first, lax.ppermute(rel_sum[0], "hop", [(1, 0)]), rel_sum[1])

    left_cols = jnp.where(first, query_cols, z_cols)
    partial = jnp.zeros((cols, width), F32)
    for block, step, base in blocks:
        left = lax.dynamic_index_in_dim(left_cols, chip_at(place + step), 0, keepdims=False)
        if step == chips // 2:
            left, relation_grad = lax.optimization_barrier((left, relation_grad))
        partial = partial + dot(left[base:base + block.shape[0]], block, 0, 0)
    partial = partial.reshape(2, cols // 2, width)
    keep = lax.dynamic_index_in_dim(partial, core, 0, keepdims=False)
    give = lax.dynamic_index_in_dim(partial, 1 - core, 0, keepdims=False)
    weight_grad = (keep + swap_core(give)) * (1.0 / jnp.sqrt(F32(total_rows)))
    return weight_grad[None], relation_grad, query_grad


def solution(mesh):
    hops, batch = mesh.devices.shape
    fine = Mesh(mesh.devices.reshape(hops, batch // 2, 2), ("hop", "chip", "core"))
    rows = ("chip", "core")
    return jax.shard_map(
        local,
        mesh=fine,
        in_specs=(P("hop", rows, None), P("hop", None, None), P(), P(rows)),
        out_specs=(P("hop", rows, None), P(("hop", "chip", "core"), None), P(rows, None)),
        check_vma=False,
    )
```

```python
import jax
import jax.numpy as jnp
from jax import lax
from jax.experimental import pallas as pl
from jax.experimental.pallas import tpu as pltpu
from jax.sharding import Mesh
from jax.sharding import PartitionSpec as P

F32 = jnp.float32
BF16 = jnp.bfloat16
TILE = 256


def dot(a, b, ca, cb):
    return lax.dot_general(a, b, (((ca,), (cb,)), ((), ())), preferred_element_type=F32)


def swap_core(block):
    return lax.ppermute(block, "core", [(0, 1), (1, 0)])


def mix(q_re, q_im, r_re, r_im):
    return (q_re * r_re - q_im * r_im).astype(BF16), (q_re * r_im + q_im * r_re).astype(BF16)


def at(step, base=0):
    return pl.ds(pl.multiple_of(base + step * TILE, TILE), TILE)


def lead_body(rows, weight, onehot, table, query, mixed, rel, held, sems):
    half = weight.shape[0] // 2
    steps = half // TILE

    def load(step, side):
        piece = at(step, side * half)
        return pltpu.make_async_copy(weight.at[piece], held.at[piece], sems.at[2 * step + side])

    for step in range(steps):
        for side in range(2):
            load(step, side).start()
    for step in range(steps):
        span = pl.ds(step * TILE, TILE)
        r_re = dot(onehot[...], table[:, at(step)], 1, 0)
        r_im = dot(onehot[...], table[:, at(step, half)], 1, 0)
        load(step, 0).wait()
        q_re = dot(rows[...], held[at(step)], 1, 1).astype(BF16)
        load(step, 1).wait()
        q_im = dot(rows[...], held[at(step, half)], 1, 1).astype(BF16)
        query[0, :, span], query[1, :, span] = q_re, q_im
        rel[0, :, span], rel[1, :, span] = r_re.astype(BF16), r_im.astype(BF16)
        z_re, z_im = mix(q_re.astype(F32), q_im.astype(F32), r_re, r_im)
        if mixed.shape[2] == TILE:
            mixed[step], mixed[steps + step] = z_re, z_im
        else:
            mixed[0, :, span], mixed[1, :, span] = z_re, z_im


def lead(rows, weight, onehot, table, chips):
    rows_dev, hidden = rows.shape
    width = weight.shape[0]
    half = width // 2
    cols = width // chips
    count_rel = table.shape[0]
    vmem = pl.BlockSpec(memory_space=pltpu.VMEM)
    pair = jax.ShapeDtypeStruct((2, rows_dev, half), BF16)
    apart = jax.ShapeDtypeStruct((chips, rows_dev, cols), BF16) if cols == TILE else pair
    query, mixed, rel = pl.pallas_call(
        lead_body,
        out_shape=(pair, apart, pair),
        in_specs=[vmem, pl.BlockSpec(memory_space=pltpu.HBM), vmem, vmem],
        out_specs=(vmem,) * 3,
        scratch_shapes=[
            pltpu.VMEM((width, hidden), BF16),
            pltpu.SemaphoreType.DMA((width // TILE,)),
        ],
        compiler_params=pltpu.CompilerParams(vmem_limit_bytes=56 * 1024 * 1024),
        cost_estimate=pl.CostEstimate(
            flops=2 * rows_dev * width * (hidden + count_rel), bytes_accessed=2 * width * hidden, transcendentals=0
        ),
    )(rows, weight, onehot, table)
    if cols != TILE:
        mixed = mixed.reshape(2, rows_dev, chips // 2, cols).transpose(0, 2, 1, 3).reshape(chips, rows_dev, cols)
    return query, mixed, rel


def hidden_body(first, query, rows, weight_at, rel, right, mixed, weight, sems):
    width, hidden = weight.shape
    half = width // 2
    is_first = first[0] == 1

    def load(step):
        return pltpu.make_async_copy(weight_at.at[:, at(step)], weight.at[:, at(step)], sems.at[step])

    for step in range(hidden // TILE):
        load(step).start()

    def make_mixed(step, carry):
        mixed[:, at(step)], mixed[:, at(step, half)] = mix(
            query[0, :, at(step)].astype(F32), query[1, :, at(step)].astype(F32),
            rel[0, :, at(step)].astype(F32), rel[1, :, at(step)].astype(F32),
        )
        return carry

    lax.fori_loop(0, half // TILE, make_mixed, 0)

    def make_hidden(step, carry):
        load(step).wait()
        pre = dot(mixed[...], weight[:, at(step)], 1, 0)
        sig = jax.nn.sigmoid(pre)
        cot = rows[:, at(step)]
        grad = (cot.astype(F32) * (sig * (1.0 + pre * (1.0 - sig)))).astype(BF16)
        right[:, at(step)] = jnp.where(is_first, cot, grad)
        return carry

    lax.fori_loop(0, hidden // TILE, make_hidden, 0)


def query_body(hidden, query, weight_at, rel, onehot, query_grad, give, keep, weight, sems):
    half = weight.shape[0] // 2
    owned = give.shape[0]

    def load(step, side):
        piece = at(step, side * half)
        return pltpu.make_async_copy(weight_at.at[piece], weight.at[piece], sems.at[2 * step + side])

    for step in range(half // TILE):
        for side in range(2):
            load(step, side).start()

    def make_query(step, carry):
        load(step, 0).wait()
        gz_re = dot(hidden[...], weight[at(step), :], 1, 1)
        load(step, 1).wait()
        gz_im = dot(hidden[...], weight[at(step, half), :], 1, 1)
        r_re, r_im = rel[0, :, at(step)].astype(F32), rel[1, :, at(step)].astype(F32)
        query_grad[:, at(step)] = (gz_re * r_re + gz_im * r_im).astype(BF16)
        query_grad[:, at(step, half)] = (gz_im * r_re - gz_re * r_im).astype(BF16)
        a, b = query[0, :, at(step)].astype(F32), query[1, :, at(step)].astype(F32)
        for base, grad in ((0, gz_re * a + gz_im * b), (half, gz_im * a - gz_re * b)):
            head = grad.astype(BF16)
            rest = (grad - head.astype(F32)).astype(BF16)
            total = dot(onehot[...], head, 1, 0) + dot(onehot[...], rest, 1, 0)
            give[:, at(step, base)] = total[:owned]
            keep[:, at(step, base)] = total[owned:]
        return carry

    lax.fori_loop(0, half // TILE, make_query, 0)


VMEM = pl.BlockSpec(memory_space=pltpu.VMEM)
LARGE = pl.BlockSpec(memory_space=pltpu.HBM)


def hidden_grad(first, query, rows, weight, rel):
    rows_dev, hidden = rows.shape
    width = weight.shape[0]
    return pl.pallas_call(
        hidden_body,
        out_shape=jax.ShapeDtypeStruct((rows_dev, hidden), BF16),
        in_specs=[pl.BlockSpec(memory_space=pltpu.SMEM), VMEM, VMEM, LARGE, VMEM],
        out_specs=VMEM,
        scratch_shapes=[
            pltpu.VMEM((rows_dev, width), BF16),
            pltpu.VMEM((width, hidden), BF16),
            pltpu.SemaphoreType.DMA((hidden // TILE,)),
        ],
        compiler_params=pltpu.CompilerParams(vmem_limit_bytes=56 * 1024 * 1024),
        cost_estimate=pl.CostEstimate(
            flops=2 * rows_dev * width * hidden, bytes_accessed=2 * width * hidden, transcendentals=rows_dev * hidden
        ),
    )(first, query, rows, weight, rel)


def query_and_relation_grad(hidden, query, weight, rel, onehot):
    rows_dev = hidden.shape[0]
    width = weight.shape[0]
    count_rel = onehot.shape[0]
    partial = jax.ShapeDtypeStruct((count_rel // 2, width), F32)
    return pl.pallas_call(
        query_body,
        out_shape=(jax.ShapeDtypeStruct((rows_dev, width), BF16), partial, partial),
        in_specs=[VMEM, VMEM, LARGE, VMEM, VMEM],
        out_specs=(VMEM,) * 3,
        scratch_shapes=[pltpu.VMEM(weight.shape, BF16), pltpu.SemaphoreType.DMA((width // TILE,))],
        compiler_params=pltpu.CompilerParams(vmem_limit_bytes=56 * 1024 * 1024),
        cost_estimate=pl.CostEstimate(
            flops=2 * rows_dev * width * (weight.shape[1] + 2 * count_rel),
            bytes_accessed=2 * width * weight.shape[1], transcendentals=0,
        ),
    )(hidden, query, weight, rel, onehot)


def local(section_rows, weights, relation_table, relation_ids):
    rows = section_rows[0]
    weight = weights[0]
    rows_dev, width = rows.shape
    half = width // 2
    count_rel = relation_table.shape[0]
    chips = lax.axis_size("chip")
    first = lax.axis_index("hop") == 0
    core = lax.axis_index("core")
    chip = lax.axis_index("chip")
    total_rows = rows_dev * chips * 2
    cols = width // chips
    owned = count_rel // (4 * chips)

    def columns(left):
        return left.reshape(left.shape[0], chips, cols).transpose(1, 0, 2)

    onehot = (relation_ids[:, None] == lax.iota(jnp.int32, count_rel)[None, :]).astype(BF16)
    number = lax.iota(jnp.int32, count_rel)
    side = number // (count_rel // 2)
    dest = number % (count_rel // 2) // (2 * owned)
    hop = number % (2 * owned) // owned
    which_core = jnp.where(side == 1, core, 1 - core)
    relation = ((hop * chips + dest) * 2 + which_core) * owned + number % owned
    onehot_t = (relation[:, None] == relation_ids[None, :]).astype(BF16)

    own_query, own_mixed, rel = lead(rows, weight, onehot, relation_table, chips)
    query = lax.ppermute(own_query, "hop", [(0, 1)])
    z_cols = lax.all_to_all(own_mixed, "chip", 0, 0, tiled=True)

    right = hidden_grad(first.astype(jnp.int32).reshape(1), query, rows, weight, rel)
    hidden, z_cols = lax.optimization_barrier((right, z_cols))
    grad_query, rel_give, rel_keep = query_and_relation_grad(hidden, query, weight, rel, onehot_t)
    query_back = lax.ppermute(grad_query, "hop", [(1, 0)])
    query_grad = jnp.where(first, query_back, grad_query)
    z_cols, _ = lax.optimization_barrier((z_cols, grad_query))
    z_cols = lax.ppermute(z_cols, "hop", [(0, 1)])
    rel_got = swap_core(rel_give)

    def chip_at(place):
        place = lax.rem(place, chips)
        return jnp.where(place < (chips + 1) // 2, 2 * place, 2 * (chips - place) - 1)

    ring = list(range(0, chips, 2)) + list(range(1, chips, 2))[::-1]
    place = jnp.where(lax.rem(chip, 2) == 0, chip // 2, chips - 1 - chip // 2)
    up = [(ring[i], ring[(i + 1) % chips]) for i in range(chips)]
    down = [(b, a) for a, b in up]
    blocks = [(right, 0, 0)]
    fwd = bwd = right
    for s in range(1, (chips + 1) // 2):
        fwd = lax.ppermute(fwd, "chip", up)
        bwd = lax.ppermute(bwd, "chip", down)
        blocks += [(fwd, chips - s, 0), (bwd, s, 0)]
    if chips % 2 == 0:
        mid = rows_dev // 2
        blocks.append((lax.ppermute(fwd[:mid], "chip", up), chips // 2, 0))
        blocks.append((lax.ppermute(bwd[mid:], "chip", down), chips // 2, mid))

    rel_sent = (rel_keep + rel_got).astype(BF16).reshape(chips, 2 * owned, chips, cols)
    rel_sent = rel_sent.transpose(0, 2, 1, 3).reshape(chips, 2 * owned * chips, cols)
    if rel_sent.shape[1] == rows_dev:
        shared = jnp.where(first, columns(query_back), rel_sent)
        shared, _ = lax.optimization_barrier((shared, (blocks[1][0], blocks[2][0])))
        query_cols = rel_rows = lax.all_to_all(shared, "chip", 0, 0, tiled=True)
    else:
        query_cols = lax.all_to_all(columns(query_back), "chip", 0, 0, tiled=True)
        rel_rows = lax.all_to_all(rel_sent, "chip", 0, 0, tiled=True)
    rel_sum = jnp.sum(rel_rows.astype(F32), axis=0) * jnp.sqrt(F32(count_rel) / F32(total_rows))
    rel_sum = rel_sum.reshape(chips, 2 * owned, cols).transpose(1, 0, 2).reshape(2, owned, width)
    relation_grad = jnp.where(first, lax.ppermute(rel_sum[0], "hop", [(1, 0)]), rel_sum[1])

    left_cols = jnp.where(first, query_cols, z_cols)
    partial = jnp.zeros((cols, width), F32)
    for block, step, base in blocks:
        left = lax.dynamic_index_in_dim(left_cols, chip_at(place + step), 0, keepdims=False)
        if step == chips // 2:
            left, relation_grad = lax.optimization_barrier((left, relation_grad))
        partial = partial + dot(left[base:base + block.shape[0]], block, 0, 0)
    partial = partial.reshape(2, cols // 2, width)
    keep = lax.dynamic_index_in_dim(partial, core, 0, keepdims=False)
    give = lax.dynamic_index_in_dim(partial, 1 - core, 0, keepdims=False)
    weight_grad = (keep + swap_core(give)) * (1.0 / jnp.sqrt(F32(total_rows)))
    return weight_grad[None], relation_grad, query_grad


def solution(mesh):
    hops, batch = mesh.devices.shape
    fine = Mesh(mesh.devices.reshape(hops, batch // 2, 2), ("hop", "chip", "core"))
    rows = ("chip", "core")
    return jax.shard_map(
        local,
        mesh=fine,
        in_specs=(P("hop", rows, None), P("hop", None, None), P(), P(rows)),
        out_specs=(P("hop", rows, None), P(("hop", "chip", "core"), None), P(rows, None)),
        check_vma=False,
    )
```

```python
import jax
import jax.numpy as jnp
from jax import lax
from jax.experimental import pallas as pl
from jax.experimental.pallas import tpu as pltpu
from jax.sharding import Mesh
from jax.sharding import PartitionSpec as P

F32 = jnp.float32
BF16 = jnp.bfloat16
TILE = 256
GRANT = 16 * 1024 * 1024


def dot(a, b, ca, cb):
    return lax.dot_general(a, b, (((ca,), (cb,)), ((), ())), preferred_element_type=F32)


def swap_core(block):
    return lax.ppermute(block, "core", [(0, 1), (1, 0)])


def mix(q_re, q_im, r_re, r_im):
    return (q_re * r_re - q_im * r_im).astype(BF16), (q_re * r_im + q_im * r_re).astype(BF16)


def at(step, base=0):
    return pl.ds(pl.multiple_of(base + step * TILE, TILE), TILE)


def lead_body(rows, weight, onehot, table, query, mixed, rel):
    half = weight.shape[0] // 2
    steps = half // TILE
    for step in range(steps):
        span = pl.ds(step * TILE, TILE)
        r_re = dot(onehot[...], table[:, at(step)], 1, 0)
        r_im = dot(onehot[...], table[:, at(step, half)], 1, 0)
        q_re = dot(rows[...], weight[at(step)], 1, 1).astype(BF16)
        q_im = dot(rows[...], weight[at(step, half)], 1, 1).astype(BF16)
        query[0, :, span], query[1, :, span] = q_re, q_im
        rel[0, :, span], rel[1, :, span] = r_re.astype(BF16), r_im.astype(BF16)
        z_re, z_im = mix(q_re.astype(F32), q_im.astype(F32), r_re, r_im)
        if mixed.shape[2] == TILE:
            mixed[step], mixed[steps + step] = z_re, z_im
        else:
            mixed[0, :, span], mixed[1, :, span] = z_re, z_im


def lead(rows, weight, onehot, table, chips):
    rows_dev, hidden = rows.shape
    width = weight.shape[0]
    half = width // 2
    cols = width // chips
    count_rel = table.shape[0]
    vmem = pl.BlockSpec(memory_space=pltpu.VMEM)
    pair = jax.ShapeDtypeStruct((2, rows_dev, half), BF16)
    apart = jax.ShapeDtypeStruct((chips, rows_dev, cols), BF16) if cols == TILE else pair
    query, mixed, rel = pl.pallas_call(
        lead_body,
        out_shape=(pair, apart, pair),
        in_specs=[vmem] * 4,
        out_specs=(vmem,) * 3,
        compiler_params=pltpu.CompilerParams(vmem_limit_bytes=GRANT),
        cost_estimate=pl.CostEstimate(
            flops=2 * rows_dev * width * (hidden + count_rel), bytes_accessed=2 * width * hidden, transcendentals=0
        ),
    )(rows, weight, onehot, table)
    if cols != TILE:
        mixed = mixed.reshape(2, rows_dev, chips // 2, cols).transpose(0, 2, 1, 3).reshape(chips, rows_dev, cols)
    return query, mixed, rel


def trail_body(first, query, rows, weight, rel, onehot, right, query_grad, give, keep, mixed, hidden):
    width = weight.shape[0]
    half = width // 2
    is_first = first[0] == 1
    owned = give.shape[0]

    def make_mixed(step, carry):
        mixed[:, at(step)], mixed[:, at(step, half)] = mix(
            query[0, :, at(step)].astype(F32), query[1, :, at(step)].astype(F32),
            rel[0, :, at(step)].astype(F32), rel[1, :, at(step)].astype(F32),
        )
        return carry

    lax.fori_loop(0, half // TILE, make_mixed, 0)

    def make_hidden(step, carry):
        pre = dot(mixed[...], weight[:, at(step)], 1, 0)
        sig = jax.nn.sigmoid(pre)
        cot = rows[:, at(step)]
        grad = (cot.astype(F32) * (sig * (1.0 + pre * (1.0 - sig)))).astype(BF16)
        hidden[:, at(step)] = grad
        right[:, at(step)] = jnp.where(is_first, cot, grad)
        return carry

    lax.fori_loop(0, weight.shape[1] // TILE, make_hidden, 0)

    def make_query(step, carry):
        gz_re = dot(hidden[...], weight[at(step), :], 1, 1)
        gz_im = dot(hidden[...], weight[at(step, half), :], 1, 1)
        r_re, r_im = rel[0, :, at(step)].astype(F32), rel[1, :, at(step)].astype(F32)
        query_grad[:, at(step)] = (gz_re * r_re + gz_im * r_im).astype(BF16)
        query_grad[:, at(step, half)] = (gz_im * r_re - gz_re * r_im).astype(BF16)
        a, b = query[0, :, at(step)].astype(F32), query[1, :, at(step)].astype(F32)
        for base, grad in ((0, gz_re * a + gz_im * b), (half, gz_im * a - gz_re * b)):
            head = grad.astype(BF16)
            rest = (grad - head.astype(F32)).astype(BF16)
            total = dot(onehot[...], head, 1, 0) + dot(onehot[...], rest, 1, 0)
            give[:, at(step, base)] = total[:owned]
            keep[:, at(step, base)] = total[owned:]
        return carry

    lax.fori_loop(0, half // TILE, make_query, 0)


def trail(first, query, rows, weight, rel, onehot):
    rows_dev, hidden = rows.shape
    width = weight.shape[0]
    count_rel = onehot.shape[0]
    vmem = pl.BlockSpec(memory_space=pltpu.VMEM)
    flops = 4 * rows_dev * width * hidden + 4 * rows_dev * count_rel * width
    return pl.pallas_call(
        trail_body,
        out_shape=(
            jax.ShapeDtypeStruct((rows_dev, hidden), BF16),
            jax.ShapeDtypeStruct((rows_dev, width), BF16),
            jax.ShapeDtypeStruct((count_rel // 2, width), F32),
            jax.ShapeDtypeStruct((count_rel // 2, width), F32),
        ),
        in_specs=[pl.BlockSpec(memory_space=pltpu.SMEM)] + [vmem] * 5,
        out_specs=(vmem,) * 4,
        scratch_shapes=[pltpu.VMEM((rows_dev, width), BF16), pltpu.VMEM((rows_dev, hidden), BF16)],
        compiler_params=pltpu.CompilerParams(vmem_limit_bytes=GRANT),
        cost_estimate=pl.CostEstimate(
            flops=flops, bytes_accessed=4 * width * hidden, transcendentals=rows_dev * hidden
        ),
    )(first, query, rows, weight, rel, onehot)


def local(section_rows, weights, relation_table, relation_ids):
    rows = section_rows[0]
    weight = weights[0]
    rows_dev, width = rows.shape
    half = width // 2
    count_rel = relation_table.shape[0]
    chips = lax.axis_size("chip")
    first = lax.axis_index("hop") == 0
    core = lax.axis_index("core")
    chip = lax.axis_index("chip")
    total_rows = rows_dev * chips * 2
    cols = width // chips
    owned = count_rel // (4 * chips)

    def columns(left):
        return left.reshape(left.shape[0], chips, cols).transpose(1, 0, 2)

    onehot = (relation_ids[:, None] == lax.iota(jnp.int32, count_rel)[None, :]).astype(BF16)
    number = lax.iota(jnp.int32, count_rel)
    side = number // (count_rel // 2)
    dest = number % (count_rel // 2) // (2 * owned)
    hop = number % (2 * owned) // owned
    which_core = jnp.where(side == 1, core, 1 - core)
    relation = ((hop * chips + dest) * 2 + which_core) * owned + number % owned
    onehot_t = (relation[:, None] == relation_ids[None, :]).astype(BF16)

    own_query, own_mixed, rel = lead(rows, weight, onehot, relation_table, chips)
    query = lax.ppermute(own_query, "hop", [(0, 1)])
    z_cols = lax.all_to_all(own_mixed, "chip", 0, 0, tiled=True)

    right, grad_query, rel_give, rel_keep = trail(
        first.astype(jnp.int32).reshape(1), query, rows, weight, rel, onehot_t
    )
    query_back = lax.ppermute(grad_query, "hop", [(1, 0)])
    query_grad = jnp.where(first, query_back, grad_query)
    z_cols, right = lax.optimization_barrier((z_cols, right))
    z_cols = lax.ppermute(z_cols, "hop", [(0, 1)])
    rel_got = swap_core(rel_give)

    def chip_at(place):
        place = lax.rem(place, chips)
        return jnp.where(place < (chips + 1) // 2, 2 * place, 2 * (chips - place) - 1)

    ring = list(range(0, chips, 2)) + list(range(1, chips, 2))[::-1]
    place = jnp.where(lax.rem(chip, 2) == 0, chip // 2, chips - 1 - chip // 2)
    up = [(ring[i], ring[(i + 1) % chips]) for i in range(chips)]
    down = [(b, a) for a, b in up]
    mid = rows_dev // 2
    fwd = bwd = (right[:mid], right[mid:])
    parts = [((right,), 0)]
    for s in range(1, (chips + 1) // 2):
        fwd = tuple(lax.ppermute(part, "chip", up) for part in fwd)
        bwd = tuple(lax.ppermute(part, "chip", down) for part in bwd)
        parts += [(fwd, chips - s), (bwd, s)]
    if chips % 2 == 0:
        parts.append(((lax.ppermute(fwd[0], "chip", up), lax.ppermute(bwd[1], "chip", down)), chips // 2))

    rel_sent = (rel_keep + rel_got).astype(BF16).reshape(chips, 2 * owned, chips, cols)
    rel_sent = rel_sent.transpose(0, 2, 1, 3).reshape(chips, 2 * owned * chips, cols)
    if rel_sent.shape[1] == rows_dev:
        shared = jnp.where(first, columns(query_back), rel_sent)
        shared, _ = lax.optimization_barrier((shared, (parts[1][0], parts[2][0], parts[3][0][0], parts[4][0][0], z_cols)))
        query_cols = rel_rows = lax.all_to_all(shared, "chip", 0, 0, tiled=True)
    else:
        query_cols = lax.all_to_all(columns(query_back), "chip", 0, 0, tiled=True)
        rel_rows = lax.all_to_all(rel_sent, "chip", 0, 0, tiled=True)
    rel_sum = jnp.sum(rel_rows.astype(F32), axis=0) * jnp.sqrt(F32(count_rel) / F32(total_rows))
    rel_sum = rel_sum.reshape(chips, 2 * owned, cols).transpose(1, 0, 2).reshape(2, owned, width)
    relation_grad = jnp.where(first, lax.ppermute(rel_sum[0], "hop", [(1, 0)]), rel_sum[1])

    left_cols = jnp.where(first, query_cols, z_cols)
    partial = jnp.zeros((cols, width), F32)
    for part, step in parts:
        left = lax.dynamic_index_in_dim(left_cols, chip_at(place + step), 0, keepdims=False)
        if step == chips // 2:
            left, relation_grad = lax.optimization_barrier((left, relation_grad))
        partial = partial + dot(left, jnp.concatenate(part, axis=0), 0, 0)
    partial = partial.reshape(2, cols // 2, width)
    keep = lax.dynamic_index_in_dim(partial, core, 0, keepdims=False)
    give = lax.dynamic_index_in_dim(partial, 1 - core, 0, keepdims=False)
    weight_grad = (keep + swap_core(give)) * (1.0 / jnp.sqrt(F32(total_rows)))
    return weight_grad[None], relation_grad, query_grad


def solution(mesh):
    hops, batch = mesh.devices.shape
    fine = Mesh(mesh.devices.reshape(hops, batch // 2, 2), ("hop", "chip", "core"))
    rows = ("chip", "core")
    return jax.shard_map(
        local,
        mesh=fine,
        in_specs=(P("hop", rows, None), P("hop", None, None), P(), P(rows)),
        out_specs=(P("hop", rows, None), P(("hop", "chip", "core"), None), P(rows, None)),
        check_vma=False,
    )
```

```python
import jax
import jax.numpy as jnp
from jax import lax
from jax.experimental import pallas as pl
from jax.experimental.pallas import tpu as pltpu
from jax.sharding import Mesh
from jax.sharding import PartitionSpec as P

F32 = jnp.float32
BF16 = jnp.bfloat16
TILE = 256
GRANT = 16 * 1024 * 1024


def dot(a, b, ca, cb):
    return lax.dot_general(a, b, (((ca,), (cb,)), ((), ())), preferred_element_type=F32)


def swap_core(block):
    return lax.ppermute(block, "core", [(0, 1), (1, 0)])


def mix(q_re, q_im, r_re, r_im):
    return (q_re * r_re - q_im * r_im).astype(BF16), (q_re * r_im + q_im * r_re).astype(BF16)


def at(step, base=0):
    return pl.ds(pl.multiple_of(base + step * TILE, TILE), TILE)


def lead_body(rows, weight, onehot, table, query, mixed, rel):
    half = weight.shape[0] // 2
    steps = half // TILE
    for step in range(steps):
        span = pl.ds(step * TILE, TILE)
        r_re = dot(onehot[...], table[:, at(step)], 1, 0)
        r_im = dot(onehot[...], table[:, at(step, half)], 1, 0)
        q_re = dot(rows[...], weight[at(step)], 1, 1).astype(BF16)
        q_im = dot(rows[...], weight[at(step, half)], 1, 1).astype(BF16)
        query[0, :, span], query[1, :, span] = q_re, q_im
        rel[0, :, span], rel[1, :, span] = r_re.astype(BF16), r_im.astype(BF16)
        z_re, z_im = mix(q_re.astype(F32), q_im.astype(F32), r_re, r_im)
        if mixed.shape[2] == TILE:
            mixed[step], mixed[steps + step] = z_re, z_im
        else:
            mixed[0, :, span], mixed[1, :, span] = z_re, z_im


def lead(rows, weight, onehot, table, chips):
    rows_dev, hidden = rows.shape
    width = weight.shape[0]
    half = width // 2
    cols = width // chips
    count_rel = table.shape[0]
    vmem = pl.BlockSpec(memory_space=pltpu.VMEM)
    pair = jax.ShapeDtypeStruct((2, rows_dev, half), BF16)
    apart = jax.ShapeDtypeStruct((chips, rows_dev, cols), BF16) if cols == TILE else pair
    query, mixed, rel = pl.pallas_call(
        lead_body,
        out_shape=(pair, apart, pair),
        in_specs=[vmem] * 4,
        out_specs=(vmem,) * 3,
        compiler_params=pltpu.CompilerParams(vmem_limit_bytes=GRANT),
        cost_estimate=pl.CostEstimate(
            flops=2 * rows_dev * width * (hidden + count_rel), bytes_accessed=2 * width * hidden, transcendentals=0
        ),
    )(rows, weight, onehot, table)
    if cols != TILE:
        mixed = mixed.reshape(2, rows_dev, chips // 2, cols).transpose(0, 2, 1, 3).reshape(chips, rows_dev, cols)
    return query, mixed, rel


def trail_body(first, query, rows, weight, rel, onehot, right, query_grad, give, keep, mixed, hidden):
    width = weight.shape[0]
    half = width // 2
    is_first = first[0] == 1
    owned = give.shape[0]

    def make_mixed(step, carry):
        mixed[:, at(step)], mixed[:, at(step, half)] = mix(
            query[0, :, at(step)].astype(F32), query[1, :, at(step)].astype(F32),
            rel[0, :, at(step)].astype(F32), rel[1, :, at(step)].astype(F32),
        )
        return carry

    lax.fori_loop(0, half // TILE, make_mixed, 0)

    def make_hidden(step, carry):
        pre = dot(mixed[...], weight[:, at(step)], 1, 0)
        sig = jax.nn.sigmoid(pre)
        cot = rows[:, at(step)]
        grad = (cot.astype(F32) * (sig * (1.0 + pre * (1.0 - sig)))).astype(BF16)
        hidden[:, at(step)] = grad
        right[:, at(step)] = jnp.where(is_first, cot, grad)
        return carry

    lax.fori_loop(0, weight.shape[1] // TILE, make_hidden, 0)

    def make_query(step, carry):
        gz_re = dot(hidden[...], weight[at(step), :], 1, 1)
        gz_im = dot(hidden[...], weight[at(step, half), :], 1, 1)
        r_re, r_im = rel[0, :, at(step)].astype(F32), rel[1, :, at(step)].astype(F32)
        query_grad[:, at(step)] = (gz_re * r_re + gz_im * r_im).astype(BF16)
        query_grad[:, at(step, half)] = (gz_im * r_re - gz_re * r_im).astype(BF16)
        a, b = query[0, :, at(step)].astype(F32), query[1, :, at(step)].astype(F32)
        for base, grad in ((0, gz_re * a + gz_im * b), (half, gz_im * a - gz_re * b)):
            head = grad.astype(BF16)
            rest = (grad - head.astype(F32)).astype(BF16)
            total = dot(onehot[...], head, 1, 0) + dot(onehot[...], rest, 1, 0)
            give[:, at(step, base)] = total[:owned]
            keep[:, at(step, base)] = total[owned:]
        return carry

    lax.fori_loop(0, half // TILE, make_query, 0)


def trail(first, query, rows, weight, rel, onehot):
    rows_dev, hidden = rows.shape
    width = weight.shape[0]
    count_rel = onehot.shape[0]
    vmem = pl.BlockSpec(memory_space=pltpu.VMEM)
    flops = 4 * rows_dev * width * hidden + 4 * rows_dev * count_rel * width
    return pl.pallas_call(
        trail_body,
        out_shape=(
            jax.ShapeDtypeStruct((rows_dev, hidden), BF16),
            jax.ShapeDtypeStruct((rows_dev, width), BF16),
            jax.ShapeDtypeStruct((count_rel // 2, width), F32),
            jax.ShapeDtypeStruct((count_rel // 2, width), F32),
        ),
        in_specs=[pl.BlockSpec(memory_space=pltpu.SMEM)] + [vmem] * 5,
        out_specs=(vmem,) * 4,
        scratch_shapes=[pltpu.VMEM((rows_dev, width), BF16), pltpu.VMEM((rows_dev, hidden), BF16)],
        compiler_params=pltpu.CompilerParams(vmem_limit_bytes=GRANT),
        cost_estimate=pl.CostEstimate(
            flops=flops, bytes_accessed=4 * width * hidden, transcendentals=rows_dev * hidden
        ),
    )(first, query, rows, weight, rel, onehot)


def local(section_rows, weights, relation_table, relation_ids):
    rows = section_rows[0]
    weight = weights[0]
    rows_dev, width = rows.shape
    half = width // 2
    count_rel = relation_table.shape[0]
    chips = lax.axis_size("chip")
    first = lax.axis_index("hop") == 0
    core = lax.axis_index("core")
    chip = lax.axis_index("chip")
    total_rows = rows_dev * chips * 2
    cols = width // chips
    owned = count_rel // (4 * chips)

    def columns(left):
        return left.reshape(left.shape[0], chips, cols).transpose(1, 0, 2)

    onehot = (relation_ids[:, None] == lax.iota(jnp.int32, count_rel)[None, :]).astype(BF16)
    number = lax.iota(jnp.int32, count_rel)
    side = number // (count_rel // 2)
    dest = number % (count_rel // 2) // (2 * owned)
    hop = number % (2 * owned) // owned
    which_core = jnp.where(side == 1, core, 1 - core)
    relation = ((hop * chips + dest) * 2 + which_core) * owned + number % owned
    onehot_t = (relation[:, None] == relation_ids[None, :]).astype(BF16)

    own_query, own_mixed, rel = lead(rows, weight, onehot, relation_table, chips)
    query = lax.ppermute(own_query, "hop", [(0, 1)])
    z_cols = lax.all_to_all(own_mixed, "chip", 0, 0, tiled=True)

    right, grad_query, rel_give, rel_keep = trail(
        first.astype(jnp.int32).reshape(1), query, rows, weight, rel, onehot_t
    )
    query_back = lax.ppermute(grad_query, "hop", [(1, 0)])
    query_grad = jnp.where(first, query_back, grad_query)
    z_cols, right = lax.optimization_barrier((z_cols, right))
    z_cols = lax.ppermute(z_cols, "hop", [(0, 1)])
    rel_got = swap_core(rel_give)

    def chip_at(place):
        place = lax.rem(place, chips)
        return jnp.where(place < (chips + 1) // 2, 2 * place, 2 * (chips - place) - 1)

    ring = list(range(0, chips, 2)) + list(range(1, chips, 2))[::-1]
    place = jnp.where(lax.rem(chip, 2) == 0, chip // 2, chips - 1 - chip // 2)
    up = [(ring[i], ring[(i + 1) % chips]) for i in range(chips)]
    down = [(b, a) for a, b in up]
    blocks = [(right, 0, 0)]
    fwd = bwd = right
    for s in range(1, (chips + 1) // 2):
        fwd = lax.ppermute(fwd, "chip", up)
        bwd = lax.ppermute(bwd, "chip", down)
        blocks += [(fwd, chips - s, 0), (bwd, s, 0)]
    if chips % 2 == 0:
        mid = rows_dev // 2
        blocks.append((lax.ppermute(fwd[:mid], "chip", up), chips // 2, 0))
        blocks.append((lax.ppermute(bwd[mid:], "chip", down), chips // 2, mid))

    rel_got, _ = lax.optimization_barrier((rel_got, query_back))
    rel_sent = (rel_keep + rel_got).astype(BF16).reshape(chips, 2 * owned, chips, cols)
    rel_sent = rel_sent.transpose(0, 2, 1, 3).reshape(chips, 2 * owned * chips, cols)
    if rel_sent.shape[1] == rows_dev:
        shared = jnp.where(first, columns(query_back), rel_sent)
        shared, _ = lax.optimization_barrier((shared, (blocks[1][0], blocks[2][0], z_cols)))
        query_cols = rel_rows = lax.all_to_all(shared, "chip", 0, 0, tiled=True)
    else:
        query_cols = lax.all_to_all(columns(query_back), "chip", 0, 0, tiled=True)
        rel_rows = lax.all_to_all(rel_sent, "chip", 0, 0, tiled=True)
    rel_sum = jnp.sum(rel_rows.astype(F32), axis=0) * jnp.sqrt(F32(count_rel) / F32(total_rows))
    rel_sum = rel_sum.reshape(chips, 2 * owned, cols).transpose(1, 0, 2).reshape(2, owned, width)
    relation_grad = jnp.where(first, lax.ppermute(rel_sum[0], "hop", [(1, 0)]), rel_sum[1])

    left_cols = jnp.where(first, query_cols, z_cols)
    partial = jnp.zeros((cols, width), F32)
    for block, step, base in blocks:
        left = lax.dynamic_index_in_dim(left_cols, chip_at(place + step), 0, keepdims=False)
        if step == chips // 2:
            left, relation_grad = lax.optimization_barrier((left, relation_grad))
        partial = partial + dot(left[base:base + block.shape[0]], block, 0, 0)
    partial = partial.reshape(2, cols // 2, width)
    keep = lax.dynamic_index_in_dim(partial, core, 0, keepdims=False)
    give = lax.dynamic_index_in_dim(partial, 1 - core, 0, keepdims=False)
    weight_grad = (keep + swap_core(give)) * (1.0 / jnp.sqrt(F32(total_rows)))
    return weight_grad[None], relation_grad, query_grad


def solution(mesh):
    hops, batch = mesh.devices.shape
    fine = Mesh(mesh.devices.reshape(hops, batch // 2, 2), ("hop", "chip", "core"))
    rows = ("chip", "core")
    return jax.shard_map(
        local,
        mesh=fine,
        in_specs=(P("hop", rows, None), P("hop", None, None), P(), P(rows)),
        out_specs=(P("hop", rows, None), P(("hop", "chip", "core"), None), P(rows, None)),
        check_vma=False,
    )
```

```python
import jax
import jax.numpy as jnp
from jax import lax
from jax.experimental import pallas as pl
from jax.experimental.pallas import tpu as pltpu
from jax.sharding import Mesh
from jax.sharding import PartitionSpec as P

F32 = jnp.float32
BF16 = jnp.bfloat16
TILE = 256
GRANT = 16 * 1024 * 1024


def dot(a, b, ca, cb):
    return lax.dot_general(a, b, (((ca,), (cb,)), ((), ())), preferred_element_type=F32)


def swap_core(block):
    return lax.ppermute(block, "core", [(0, 1), (1, 0)])


def mix(q_re, q_im, r_re, r_im):
    return (q_re * r_re - q_im * r_im).astype(BF16), (q_re * r_im + q_im * r_re).astype(BF16)


def at(step, base=0):
    return pl.ds(pl.multiple_of(base + step * TILE, TILE), TILE)


def lead_body(rows, weight, onehot, table, query, rel):
    half = weight.shape[0] // 2
    steps = half // TILE
    for step in range(steps):
        span = pl.ds(step * TILE, TILE)
        r_re = dot(onehot[...], table[:, at(step)], 1, 0)
        r_im = dot(onehot[...], table[:, at(step, half)], 1, 0)
        q_re = dot(rows[...], weight[at(step)], 1, 1).astype(BF16)
        q_im = dot(rows[...], weight[at(step, half)], 1, 1).astype(BF16)
        query[0, :, span], query[1, :, span] = q_re, q_im
        rel[0, :, span], rel[1, :, span] = r_re.astype(BF16), r_im.astype(BF16)


def lead(rows, weight, onehot, table):
    rows_dev, hidden = rows.shape
    width = weight.shape[0]
    half = width // 2
    count_rel = table.shape[0]
    vmem = pl.BlockSpec(memory_space=pltpu.VMEM)
    pair = jax.ShapeDtypeStruct((2, rows_dev, half), BF16)
    return pl.pallas_call(
        lead_body,
        out_shape=(pair, pair),
        in_specs=[vmem] * 4,
        out_specs=(vmem,) * 2,
        compiler_params=pltpu.CompilerParams(vmem_limit_bytes=GRANT),
        cost_estimate=pl.CostEstimate(
            flops=2 * rows_dev * width * (hidden + count_rel), bytes_accessed=2 * width * hidden, transcendentals=0
        ),
    )(rows, weight, onehot, table)


def trail_body(first, query, rows, weight, rel, onehot, right, query_grad, give, keep, mixed, hidden):
    width = weight.shape[0]
    half = width // 2
    is_first = first[0] == 1
    owned = give.shape[0]

    def make_mixed(step, carry):
        mixed[:, at(step)], mixed[:, at(step, half)] = mix(
            query[0, :, at(step)].astype(F32), query[1, :, at(step)].astype(F32),
            rel[0, :, at(step)].astype(F32), rel[1, :, at(step)].astype(F32),
        )
        return carry

    lax.fori_loop(0, half // TILE, make_mixed, 0)

    def make_hidden(step, carry):
        pre = dot(mixed[...], weight[:, at(step)], 1, 0)
        sig = jax.nn.sigmoid(pre)
        cot = rows[:, at(step)]
        grad = (cot.astype(F32) * (sig * (1.0 + pre * (1.0 - sig)))).astype(BF16)
        hidden[:, at(step)] = grad
        right[:, at(step)] = jnp.where(is_first, cot, grad)
        return carry

    lax.fori_loop(0, weight.shape[1] // TILE, make_hidden, 0)

    def make_query(step, carry):
        gz_re = dot(hidden[...], weight[at(step), :], 1, 1)
        gz_im = dot(hidden[...], weight[at(step, half), :], 1, 1)
        r_re, r_im = rel[0, :, at(step)].astype(F32), rel[1, :, at(step)].astype(F32)
        query_grad[:, at(step)] = (gz_re * r_re + gz_im * r_im).astype(BF16)
        query_grad[:, at(step, half)] = (gz_im * r_re - gz_re * r_im).astype(BF16)
        a, b = query[0, :, at(step)].astype(F32), query[1, :, at(step)].astype(F32)
        for base, grad in ((0, gz_re * a + gz_im * b), (half, gz_im * a - gz_re * b)):
            head = grad.astype(BF16)
            rest = (grad - head.astype(F32)).astype(BF16)
            total = dot(onehot[...], head, 1, 0) + dot(onehot[...], rest, 1, 0)
            give[:, at(step, base)] = total[:owned]
            keep[:, at(step, base)] = total[owned:]
        return carry

    lax.fori_loop(0, half // TILE, make_query, 0)


def trail(first, query, rows, weight, rel, onehot):
    rows_dev, hidden = rows.shape
    width = weight.shape[0]
    count_rel = onehot.shape[0]
    vmem = pl.BlockSpec(memory_space=pltpu.VMEM)
    flops = 4 * rows_dev * width * hidden + 4 * rows_dev * count_rel * width
    return pl.pallas_call(
        trail_body,
        out_shape=(
            jax.ShapeDtypeStruct((rows_dev, hidden), BF16),
            jax.ShapeDtypeStruct((rows_dev, width), BF16),
            jax.ShapeDtypeStruct((count_rel // 2, width), F32),
            jax.ShapeDtypeStruct((count_rel // 2, width), F32),
            jax.ShapeDtypeStruct((rows_dev, width), BF16),
        ),
        in_specs=[pl.BlockSpec(memory_space=pltpu.SMEM)] + [vmem] * 5,
        out_specs=(vmem,) * 5,
        scratch_shapes=[pltpu.VMEM((rows_dev, hidden), BF16)],
        compiler_params=pltpu.CompilerParams(vmem_limit_bytes=GRANT),
        cost_estimate=pl.CostEstimate(
            flops=flops, bytes_accessed=4 * width * hidden, transcendentals=rows_dev * hidden
        ),
    )(first, query, rows, weight, rel, onehot)


def local(section_rows, weights, relation_table, relation_ids):
    rows = section_rows[0]
    weight = weights[0]
    rows_dev, width = rows.shape
    half = width // 2
    count_rel = relation_table.shape[0]
    chips = lax.axis_size("chip")
    first = lax.axis_index("hop") == 0
    core = lax.axis_index("core")
    chip = lax.axis_index("chip")
    total_rows = rows_dev * chips * 2
    cols = width // chips
    owned = count_rel // (4 * chips)

    def columns(left):
        return left.reshape(left.shape[0], chips, cols).transpose(1, 0, 2)

    onehot = (relation_ids[:, None] == lax.iota(jnp.int32, count_rel)[None, :]).astype(BF16)
    number = lax.iota(jnp.int32, count_rel)
    side = number // (count_rel // 2)
    dest = number % (count_rel // 2) // (2 * owned)
    hop = number % (2 * owned) // owned
    which_core = jnp.where(side == 1, core, 1 - core)
    relation = ((hop * chips + dest) * 2 + which_core) * owned + number % owned
    onehot_t = (relation[:, None] == relation_ids[None, :]).astype(BF16)

    own_query, rel = lead(rows, weight, onehot, relation_table)
    query = lax.ppermute(own_query, "hop", [(0, 1)])
    right, grad_query, rel_give, rel_keep, mixed = trail(
        first.astype(jnp.int32).reshape(1), query, rows, weight, rel, onehot_t
    )
    query_back = lax.ppermute(grad_query, "hop", [(1, 0)])
    query_grad = jnp.where(first, query_back, grad_query)
    rel_chip = (rel_keep + swap_core(rel_give)).astype(BF16).reshape(chips, 2, owned, width)
    rel_back = lax.ppermute(rel_chip[:, 0], "hop", [(1, 0)])

    def chip_at(place):
        place = lax.rem(place, chips)
        return jnp.where(place < (chips + 1) // 2, 2 * place, 2 * (chips - place) - 1)

    ring = list(range(0, chips, 2)) + list(range(1, chips, 2))[::-1]
    place = jnp.where(lax.rem(chip, 2) == 0, chip // 2, chips - 1 - chip // 2)
    up = [(ring[i], ring[(i + 1) % chips]) for i in range(chips)]
    down = [(b, a) for a, b in up]
    blocks = [(right, 0, 0)]
    fwd = bwd = right
    for s in range(1, (chips + 1) // 2):
        fwd = lax.ppermute(fwd, "chip", up)
        bwd = lax.ppermute(bwd, "chip", down)
        blocks += [(fwd, chips - s, 0), (bwd, s, 0)]
    if chips % 2 == 0:
        mid = rows_dev // 2
        blocks.append((lax.ppermute(fwd[:mid], "chip", up), chips // 2, 0))
        blocks.append((lax.ppermute(bwd[mid:], "chip", down), chips // 2, mid))

    rel_own = jnp.where(first, rel_back, rel_chip[:, 1]).reshape(chips, owned, chips, cols)
    rel_own = rel_own.transpose(0, 2, 1, 3).reshape(chips, owned * chips, cols)
    left = columns(jnp.where(first, query_back, mixed))
    sent = jnp.concatenate([left, rel_own], axis=1)
    sent, _ = lax.optimization_barrier((sent, (blocks[1][0], blocks[2][0])))
    received = lax.all_to_all(sent, "chip", 0, 0, tiled=True)
    left_cols, rel_rows = received[:, :rows_dev], received[:, rows_dev:]
    rel_sum = jnp.sum(rel_rows.astype(F32), axis=0) * jnp.sqrt(F32(count_rel) / F32(total_rows))
    relation_grad = rel_sum.reshape(chips, owned, cols).transpose(1, 0, 2).reshape(owned, width)

    partial = jnp.zeros((cols, width), F32)
    for block, step, base in blocks:
        left = lax.dynamic_index_in_dim(left_cols, chip_at(place + step), 0, keepdims=False)
        partial = partial + dot(left[base:base + block.shape[0]], block, 0, 0)
    partial = partial.reshape(2, cols // 2, width)
    keep = lax.dynamic_index_in_dim(partial, core, 0, keepdims=False)
    give = lax.dynamic_index_in_dim(partial, 1 - core, 0, keepdims=False)
    weight_grad = (keep + swap_core(give)) * (1.0 / jnp.sqrt(F32(total_rows)))
    return weight_grad[None], relation_grad, query_grad


def solution(mesh):
    hops, batch = mesh.devices.shape
    fine = Mesh(mesh.devices.reshape(hops, batch // 2, 2), ("hop", "chip", "core"))
    rows = ("chip", "core")
    return jax.shard_map(
        local,
        mesh=fine,
        in_specs=(P("hop", rows, None), P("hop", None, None), P(), P(rows)),
        out_specs=(P("hop", rows, None), P(("hop", "chip", "core"), None), P(rows, None)),
        check_vma=False,
    )
```

```python
import jax
import jax.numpy as jnp
from jax import lax
from jax.experimental import pallas as pl
from jax.experimental.pallas import tpu as pltpu
from jax.sharding import Mesh
from jax.sharding import PartitionSpec as P

F32 = jnp.float32
BF16 = jnp.bfloat16
TILE = 256
GRANT = 16 * 1024 * 1024


def dot(a, b, ca, cb):
    return lax.dot_general(a, b, (((ca,), (cb,)), ((), ())), preferred_element_type=F32)


def swap_core(block):
    return lax.ppermute(block, "core", [(0, 1), (1, 0)])


def mix(q_re, q_im, r_re, r_im):
    return (q_re * r_re - q_im * r_im).astype(BF16), (q_re * r_im + q_im * r_re).astype(BF16)


def at(step, base=0):
    return pl.ds(pl.multiple_of(base + step * TILE, TILE), TILE)


def lead_body(rows, weight, onehot, table, query, rel):
    half = weight.shape[0] // 2
    steps = half // TILE
    for step in range(steps):
        span = pl.ds(step * TILE, TILE)
        r_re = dot(onehot[...], table[:, at(step)], 1, 0)
        r_im = dot(onehot[...], table[:, at(step, half)], 1, 0)
        q_re = dot(rows[...], weight[at(step)], 1, 1).astype(BF16)
        q_im = dot(rows[...], weight[at(step, half)], 1, 1).astype(BF16)
        query[0, :, span], query[1, :, span] = q_re, q_im
        rel[0, :, span], rel[1, :, span] = r_re.astype(BF16), r_im.astype(BF16)


def lead(rows, weight, onehot, table):
    rows_dev, hidden = rows.shape
    width = weight.shape[0]
    half = width // 2
    count_rel = table.shape[0]
    vmem = pl.BlockSpec(memory_space=pltpu.VMEM)
    pair = jax.ShapeDtypeStruct((2, rows_dev, half), BF16)
    return pl.pallas_call(
        lead_body,
        out_shape=(pair, pair),
        in_specs=[vmem] * 4,
        out_specs=(vmem,) * 2,
        compiler_params=pltpu.CompilerParams(vmem_limit_bytes=GRANT),
        cost_estimate=pl.CostEstimate(
            flops=2 * rows_dev * width * (hidden + count_rel), bytes_accessed=2 * width * hidden, transcendentals=0
        ),
    )(rows, weight, onehot, table)


def trail_body(first, query, rows, weight, rel, onehot, right, query_grad, give, keep, mixed, hidden):
    width = weight.shape[0]
    half = width // 2
    is_first = first[0] == 1
    owned = give.shape[0]

    def make_mixed(step, carry):
        mixed[:, at(step)], mixed[:, at(step, half)] = mix(
            query[0, :, at(step)].astype(F32), query[1, :, at(step)].astype(F32),
            rel[0, :, at(step)].astype(F32), rel[1, :, at(step)].astype(F32),
        )
        return carry

    lax.fori_loop(0, half // TILE, make_mixed, 0)

    def make_hidden(step, carry):
        pre = dot(mixed[...], weight[:, at(step)], 1, 0)
        sig = jax.nn.sigmoid(pre)
        cot = rows[:, at(step)]
        grad = (cot.astype(F32) * (sig * (1.0 + pre * (1.0 - sig)))).astype(BF16)
        hidden[:, at(step)] = grad
        right[:, at(step)] = jnp.where(is_first, cot, grad)
        return carry

    lax.fori_loop(0, weight.shape[1] // TILE, make_hidden, 0)

    def make_query(step, carry):
        gz_re = dot(hidden[...], weight[at(step), :], 1, 1)
        gz_im = dot(hidden[...], weight[at(step, half), :], 1, 1)
        r_re, r_im = rel[0, :, at(step)].astype(F32), rel[1, :, at(step)].astype(F32)
        query_grad[:, at(step)] = (gz_re * r_re + gz_im * r_im).astype(BF16)
        query_grad[:, at(step, half)] = (gz_im * r_re - gz_re * r_im).astype(BF16)
        a, b = query[0, :, at(step)].astype(F32), query[1, :, at(step)].astype(F32)
        for base, grad in ((0, gz_re * a + gz_im * b), (half, gz_im * a - gz_re * b)):
            head = grad.astype(BF16)
            rest = (grad - head.astype(F32)).astype(BF16)
            total = dot(onehot[...], head, 1, 0) + dot(onehot[...], rest, 1, 0)
            give[:, at(step, base)] = total[:owned]
            keep[:, at(step, base)] = total[owned:]
        return carry

    lax.fori_loop(0, half // TILE, make_query, 0)


def trail(first, query, rows, weight, rel, onehot):
    rows_dev, hidden = rows.shape
    width = weight.shape[0]
    count_rel = onehot.shape[0]
    vmem = pl.BlockSpec(memory_space=pltpu.VMEM)
    flops = 4 * rows_dev * width * hidden + 4 * rows_dev * count_rel * width
    return pl.pallas_call(
        trail_body,
        out_shape=(
            jax.ShapeDtypeStruct((rows_dev, hidden), BF16),
            jax.ShapeDtypeStruct((rows_dev, width), BF16),
            jax.ShapeDtypeStruct((count_rel // 2, width), F32),
            jax.ShapeDtypeStruct((count_rel // 2, width), F32),
            jax.ShapeDtypeStruct((rows_dev, width), BF16),
        ),
        in_specs=[pl.BlockSpec(memory_space=pltpu.SMEM)] + [vmem] * 5,
        out_specs=(vmem,) * 5,
        scratch_shapes=[pltpu.VMEM((rows_dev, hidden), BF16)],
        compiler_params=pltpu.CompilerParams(vmem_limit_bytes=GRANT),
        cost_estimate=pl.CostEstimate(
            flops=flops, bytes_accessed=4 * width * hidden, transcendentals=rows_dev * hidden
        ),
    )(first, query, rows, weight, rel, onehot)


def local(section_rows, weights, relation_table, relation_ids):
    rows = section_rows[0]
    weight = weights[0]
    rows_dev, width = rows.shape
    half = width // 2
    count_rel = relation_table.shape[0]
    chips = lax.axis_size("chip")
    first = lax.axis_index("hop") == 0
    core = lax.axis_index("core")
    chip = lax.axis_index("chip")
    total_rows = rows_dev * chips * 2
    cols = width // chips
    owned = count_rel // (4 * chips)

    def columns(left):
        return left.reshape(left.shape[0], chips, cols).transpose(1, 0, 2)

    onehot = (relation_ids[:, None] == lax.iota(jnp.int32, count_rel)[None, :]).astype(BF16)
    number = lax.iota(jnp.int32, count_rel)
    side = number // (count_rel // 2)
    dest = number % (count_rel // 2) // (2 * owned)
    hop = number % (2 * owned) // owned
    which_core = jnp.where(side == 1, core, 1 - core)
    relation = ((hop * chips + dest) * 2 + which_core) * owned + number % owned
    onehot_t = (relation[:, None] == relation_ids[None, :]).astype(BF16)

    own_query, rel = lead(rows, weight, onehot, relation_table)
    query = lax.ppermute(own_query, "hop", [(0, 1)])
    right, grad_query, rel_give, rel_keep, mixed = trail(
        first.astype(jnp.int32).reshape(1), query, rows, weight, rel, onehot_t
    )
    query_back = lax.ppermute(grad_query, "hop", [(1, 0)])
    query_grad = jnp.where(first, query_back, grad_query)
    rel_chip = (rel_keep + swap_core(rel_give)).astype(BF16).reshape(chips, 2, owned, width)
    rel_back = lax.ppermute(rel_chip[:, 0], "hop", [(1, 0)])

    def chip_at(place):
        place = lax.rem(place, chips)
        return jnp.where(place < (chips + 1) // 2, 2 * place, 2 * (chips - place) - 1)

    ring = list(range(0, chips, 2)) + list(range(1, chips, 2))[::-1]
    place = jnp.where(lax.rem(chip, 2) == 0, chip // 2, chips - 1 - chip // 2)
    up = [(ring[i], ring[(i + 1) % chips]) for i in range(chips)]
    down = [(b, a) for a, b in up]
    blocks = [(right, 0, 0)]
    fwd = bwd = right
    for s in range(1, (chips + 1) // 2):
        fwd = lax.ppermute(fwd, "chip", up)
        bwd = lax.ppermute(bwd, "chip", down)
        blocks += [(fwd, chips - s, 0), (bwd, s, 0)]
    if chips % 2 == 0:
        mid = rows_dev // 2
        blocks.append((lax.ppermute(fwd[:mid], "chip", up), chips // 2, 0))
        blocks.append((lax.ppermute(bwd[mid:], "chip", down), chips // 2, mid))

    rel_own = jnp.where(first, rel_back, rel_chip[:, 1]).reshape(chips, owned, chips, cols)
    rel_own = rel_own.transpose(0, 2, 1, 3).reshape(chips, owned * chips, cols)
    left = columns(jnp.where(first, query_back, mixed))
    sent = jnp.concatenate([left, rel_own], axis=1)
    sent, _ = lax.optimization_barrier((sent, (blocks[3][0], blocks[4][0])))
    received = lax.all_to_all(sent, "chip", 0, 0, tiled=True)
    left_cols, rel_rows = received[:, :rows_dev], received[:, rows_dev:]
    rel_sum = jnp.sum(rel_rows.astype(F32), axis=0) * jnp.sqrt(F32(count_rel) / F32(total_rows))
    relation_grad = rel_sum.reshape(chips, owned, cols).transpose(1, 0, 2).reshape(owned, width)

    partial = jnp.zeros((cols, width), F32)
    for block, step, base in blocks:
        left = lax.dynamic_index_in_dim(left_cols, chip_at(place + step), 0, keepdims=False)
        partial = partial + dot(left[base:base + block.shape[0]], block, 0, 0)
    partial = partial.reshape(2, cols // 2, width)
    keep = lax.dynamic_index_in_dim(partial, core, 0, keepdims=False)
    give = lax.dynamic_index_in_dim(partial, 1 - core, 0, keepdims=False)
    weight_grad = (keep + swap_core(give)) * (1.0 / jnp.sqrt(F32(total_rows)))
    return weight_grad[None], relation_grad, query_grad


def solution(mesh):
    hops, batch = mesh.devices.shape
    fine = Mesh(mesh.devices.reshape(hops, batch // 2, 2), ("hop", "chip", "core"))
    rows = ("chip", "core")
    return jax.shard_map(
        local,
        mesh=fine,
        in_specs=(P("hop", rows, None), P("hop", None, None), P(), P(rows)),
        out_specs=(P("hop", rows, None), P(("hop", "chip", "core"), None), P(rows, None)),
        check_vma=False,
    )
```

```python
import jax
import jax.numpy as jnp
from jax import lax
from jax.experimental import pallas as pl
from jax.experimental.pallas import tpu as pltpu
from jax.sharding import Mesh
from jax.sharding import PartitionSpec as P

F32 = jnp.float32
BF16 = jnp.bfloat16
TILE = 256
GRANT = 16 * 1024 * 1024


def dot(a, b, ca, cb):
    return lax.dot_general(a, b, (((ca,), (cb,)), ((), ())), preferred_element_type=F32)


def swap_core(block):
    return lax.ppermute(block, "core", [(0, 1), (1, 0)])


def mix(q_re, q_im, r_re, r_im):
    return (q_re * r_re - q_im * r_im).astype(BF16), (q_re * r_im + q_im * r_re).astype(BF16)


def at(step, base=0):
    return pl.ds(pl.multiple_of(base + step * TILE, TILE), TILE)


def lead_body(rows, weight, query):
    half = weight.shape[0] // 2
    for step in range(half // TILE):
        span = pl.ds(step * TILE, TILE)
        query[0, :, span] = dot(rows[...], weight[at(step)], 1, 1).astype(BF16)
        query[1, :, span] = dot(rows[...], weight[at(step, half)], 1, 1).astype(BF16)


def lead(rows, weight):
    rows_dev, hidden = rows.shape
    width = weight.shape[0]
    vmem = pl.BlockSpec(memory_space=pltpu.VMEM)
    return pl.pallas_call(
        lead_body,
        out_shape=jax.ShapeDtypeStruct((2, rows_dev, width // 2), BF16),
        in_specs=[vmem] * 2,
        out_specs=vmem,
        compiler_params=pltpu.CompilerParams(vmem_limit_bytes=GRANT),
        cost_estimate=pl.CostEstimate(
            flops=2 * rows_dev * width * hidden, bytes_accessed=2 * width * hidden, transcendentals=0
        ),
    )(rows, weight)


def trail_body(first, query, rows, weight, rel, onehot, right, query_grad, give, keep, mixed, hidden):
    width = weight.shape[0]
    half = width // 2
    is_first = first[0] == 1
    owned = give.shape[0]

    def make_mixed(step, carry):
        mixed[:, at(step)], mixed[:, at(step, half)] = mix(
            query[0, :, at(step)].astype(F32), query[1, :, at(step)].astype(F32),
            rel[0, :, at(step)].astype(F32), rel[1, :, at(step)].astype(F32),
        )
        return carry

    lax.fori_loop(0, half // TILE, make_mixed, 0)

    def make_hidden(step, carry):
        pre = dot(mixed[...], weight[:, at(step)], 1, 0)
        sig = jax.nn.sigmoid(pre)
        cot = rows[:, at(step)]
        grad = (cot.astype(F32) * (sig * (1.0 + pre * (1.0 - sig)))).astype(BF16)
        hidden[:, at(step)] = grad
        right[:, at(step)] = jnp.where(is_first, cot, grad)
        return carry

    lax.fori_loop(0, weight.shape[1] // TILE, make_hidden, 0)

    def make_query(step, carry):
        gz_re = dot(hidden[...], weight[at(step), :], 1, 1)
        gz_im = dot(hidden[...], weight[at(step, half), :], 1, 1)
        r_re, r_im = rel[0, :, at(step)].astype(F32), rel[1, :, at(step)].astype(F32)
        query_grad[:, at(step)] = (gz_re * r_re + gz_im * r_im).astype(BF16)
        query_grad[:, at(step, half)] = (gz_im * r_re - gz_re * r_im).astype(BF16)
        a, b = query[0, :, at(step)].astype(F32), query[1, :, at(step)].astype(F32)
        for base, grad in ((0, gz_re * a + gz_im * b), (half, gz_im * a - gz_re * b)):
            head = grad.astype(BF16)
            rest = (grad - head.astype(F32)).astype(BF16)
            total = dot(onehot[...], head, 1, 0) + dot(onehot[...], rest, 1, 0)
            give[:, at(step, base)] = total[:owned]
            keep[:, at(step, base)] = total[owned:]
        return carry

    lax.fori_loop(0, half // TILE, make_query, 0)


def trail(first, query, rows, weight, rel, onehot):
    rows_dev, hidden = rows.shape
    width = weight.shape[0]
    count_rel = onehot.shape[0]
    vmem = pl.BlockSpec(memory_space=pltpu.VMEM)
    flops = 4 * rows_dev * width * hidden + 4 * rows_dev * count_rel * width
    return pl.pallas_call(
        trail_body,
        out_shape=(
            jax.ShapeDtypeStruct((rows_dev, hidden), BF16),
            jax.ShapeDtypeStruct((rows_dev, width), BF16),
            jax.ShapeDtypeStruct((count_rel // 2, width), F32),
            jax.ShapeDtypeStruct((count_rel // 2, width), F32),
            jax.ShapeDtypeStruct((rows_dev, width), BF16),
        ),
        in_specs=[pl.BlockSpec(memory_space=pltpu.SMEM)] + [vmem] * 5,
        out_specs=(vmem,) * 5,
        scratch_shapes=[pltpu.VMEM((rows_dev, hidden), BF16)],
        compiler_params=pltpu.CompilerParams(vmem_limit_bytes=GRANT),
        cost_estimate=pl.CostEstimate(
            flops=flops, bytes_accessed=4 * width * hidden, transcendentals=rows_dev * hidden
        ),
    )(first, query, rows, weight, rel, onehot)


def local(section_rows, weights, relation_table, relation_ids):
    rows = section_rows[0]
    weight = weights[0]
    rows_dev, width = rows.shape
    half = width // 2
    count_rel = relation_table.shape[0]
    chips = lax.axis_size("chip")
    first = lax.axis_index("hop") == 0
    core = lax.axis_index("core")
    chip = lax.axis_index("chip")
    total_rows = rows_dev * chips * 2
    cols = width // chips
    owned = count_rel // (4 * chips)

    def columns(left):
        return left.reshape(left.shape[0], chips, cols).transpose(1, 0, 2)

    onehot = (relation_ids[:, None] == lax.iota(jnp.int32, count_rel)[None, :]).astype(BF16)
    number = lax.iota(jnp.int32, count_rel)
    side = number // (count_rel // 2)
    dest = number % (count_rel // 2) // (2 * owned)
    hop = number % (2 * owned) // owned
    which_core = jnp.where(side == 1, core, 1 - core)
    relation = ((hop * chips + dest) * 2 + which_core) * owned + number % owned
    onehot_t = (relation[:, None] == relation_ids[None, :]).astype(BF16)

    own_query = lead(rows, weight)
    query = lax.ppermute(own_query, "hop", [(0, 1)])
    rel = dot(onehot, relation_table, 1, 0).astype(BF16)
    rel = rel.reshape(rows_dev, 2, half).transpose(1, 0, 2)
    right, grad_query, rel_give, rel_keep, mixed = trail(
        first.astype(jnp.int32).reshape(1), query, rows, weight, rel, onehot_t
    )
    query_back = lax.ppermute(grad_query, "hop", [(1, 0)])
    query_grad = jnp.where(first, query_back, grad_query)
    rel_chip = (rel_keep + swap_core(rel_give)).astype(BF16).reshape(chips, 2, owned, width)
    rel_back = lax.ppermute(rel_chip[:, 0], "hop", [(1, 0)])

    def chip_at(place):
        place = lax.rem(place, chips)
        return jnp.where(place < (chips + 1) // 2, 2 * place, 2 * (chips - place) - 1)

    ring = list(range(0, chips, 2)) + list(range(1, chips, 2))[::-1]
    place = jnp.where(lax.rem(chip, 2) == 0, chip // 2, chips - 1 - chip // 2)
    up = [(ring[i], ring[(i + 1) % chips]) for i in range(chips)]
    down = [(b, a) for a, b in up]
    blocks = [(right, 0, 0)]
    fwd = bwd = right
    for s in range(1, (chips + 1) // 2):
        fwd = lax.ppermute(fwd, "chip", up)
        bwd = lax.ppermute(bwd, "chip", down)
        blocks += [(fwd, chips - s, 0), (bwd, s, 0)]

    rel_own = jnp.where(first, rel_back, rel_chip[:, 1]).reshape(chips, owned, chips, cols)
    rel_own = rel_own.transpose(0, 2, 1, 3).reshape(chips, owned * chips, cols)
    left = columns(jnp.where(first, query_back, mixed))
    sent = jnp.concatenate([left, rel_own], axis=1)
    sent, _ = lax.optimization_barrier((sent, (blocks[3][0], blocks[4][0])))
    received = lax.all_to_all(sent, "chip", 0, 0, tiled=True)
    left_cols, rel_rows = received[:, :rows_dev], received[:, rows_dev:]
    rel_sum = jnp.sum(rel_rows.astype(F32), axis=0) * jnp.sqrt(F32(count_rel) / F32(total_rows))
    relation_grad = rel_sum.reshape(chips, owned, cols).transpose(1, 0, 2).reshape(owned, width)

    def add(partial, blocks):
        for block, step, base in blocks:
            left = lax.dynamic_index_in_dim(left_cols, chip_at(place + step), 0, keepdims=False)
            partial = partial + dot(left[base:base + block.shape[0]], block, 0, 0)
        return partial

    partial = add(jnp.zeros((cols, width), F32), blocks[:5])
    if chips % 2 == 0:
        mid = rows_dev // 2
        top, bottom, partial = lax.optimization_barrier((fwd[:mid], bwd[mid:], partial))
        blocks.append((lax.ppermute(top, "chip", up), chips // 2, 0))
        blocks.append((lax.ppermute(bottom, "chip", down), chips // 2, mid))
    partial = add(partial, blocks[5:])
    partial = partial.reshape(2, cols // 2, width)
    keep = lax.dynamic_index_in_dim(partial, core, 0, keepdims=False)
    give = lax.dynamic_index_in_dim(partial, 1 - core, 0, keepdims=False)
    weight_grad = (keep + swap_core(give)) * (1.0 / jnp.sqrt(F32(total_rows)))
    return weight_grad[None], relation_grad, query_grad


def solution(mesh):
    hops, batch = mesh.devices.shape
    fine = Mesh(mesh.devices.reshape(hops, batch // 2, 2), ("hop", "chip", "core"))
    rows = ("chip", "core")
    return jax.shard_map(
        local,
        mesh=fine,
        in_specs=(P("hop", rows, None), P("hop", None, None), P(), P(rows)),
        out_specs=(P("hop", rows, None), P(("hop", "chip", "core"), None), P(rows, None)),
        check_vma=False,
    )
```

```python
import jax
import jax.numpy as jnp
from jax import lax
from jax.experimental import pallas as pl
from jax.experimental.pallas import tpu as pltpu
from jax.sharding import Mesh
from jax.sharding import PartitionSpec as P

F32 = jnp.float32
BF16 = jnp.bfloat16
TILE = 256
GRANT = 16 * 1024 * 1024


def dot(a, b, ca, cb):
    return lax.dot_general(a, b, (((ca,), (cb,)), ((), ())), preferred_element_type=F32)


def swap_core(block):
    return lax.ppermute(block, "core", [(0, 1), (1, 0)])


def mix(q_re, q_im, r_re, r_im):
    return (q_re * r_re - q_im * r_im).astype(BF16), (q_re * r_im + q_im * r_re).astype(BF16)


def at(step, base=0):
    return pl.ds(pl.multiple_of(base + step * TILE, TILE), TILE)


def lead_body(rows, weight, query):
    half = weight.shape[0] // 2
    for step in range(half // TILE):
        span = pl.ds(step * TILE, TILE)
        query[0, :, span] = dot(rows[...], weight[at(step)], 1, 1).astype(BF16)
        query[1, :, span] = dot(rows[...], weight[at(step, half)], 1, 1).astype(BF16)


def lead(rows, weight):
    rows_dev, hidden = rows.shape
    width = weight.shape[0]
    vmem = pl.BlockSpec(memory_space=pltpu.VMEM)
    return pl.pallas_call(
        lead_body,
        out_shape=jax.ShapeDtypeStruct((2, rows_dev, width // 2), BF16),
        in_specs=[vmem] * 2,
        out_specs=vmem,
        compiler_params=pltpu.CompilerParams(vmem_limit_bytes=GRANT),
        cost_estimate=pl.CostEstimate(
            flops=2 * rows_dev * width * hidden, bytes_accessed=2 * width * hidden, transcendentals=0
        ),
    )(rows, weight)


def trail_body(first, query, rows, weight, rel, onehot, right, query_grad, give, keep, mixed, hidden):
    width = weight.shape[0]
    half = width // 2
    is_first = first[0] == 1
    owned = give.shape[0]

    def make_mixed(step, carry):
        mixed[:, at(step)], mixed[:, at(step, half)] = mix(
            query[0, :, at(step)].astype(F32), query[1, :, at(step)].astype(F32),
            rel[0, :, at(step)].astype(F32), rel[1, :, at(step)].astype(F32),
        )
        return carry

    lax.fori_loop(0, half // TILE, make_mixed, 0)

    def make_hidden(step, carry):
        pre = dot(mixed[...], weight[:, at(step)], 1, 0)
        sig = jax.nn.sigmoid(pre)
        cot = rows[:, at(step)]
        grad = (cot.astype(F32) * (sig * (1.0 + pre * (1.0 - sig)))).astype(BF16)
        hidden[:, at(step)] = grad
        right[:, at(step)] = jnp.where(is_first, cot, grad)
        return carry

    lax.fori_loop(0, weight.shape[1] // TILE, make_hidden, 0)

    def make_query(step, carry):
        gz_re = dot(hidden[...], weight[at(step), :], 1, 1)
        gz_im = dot(hidden[...], weight[at(step, half), :], 1, 1)
        r_re, r_im = rel[0, :, at(step)].astype(F32), rel[1, :, at(step)].astype(F32)
        query_grad[:, at(step)] = (gz_re * r_re + gz_im * r_im).astype(BF16)
        query_grad[:, at(step, half)] = (gz_im * r_re - gz_re * r_im).astype(BF16)
        a, b = query[0, :, at(step)].astype(F32), query[1, :, at(step)].astype(F32)
        for base, grad in ((0, gz_re * a + gz_im * b), (half, gz_im * a - gz_re * b)):
            head = grad.astype(BF16)
            rest = (grad - head.astype(F32)).astype(BF16)
            total = dot(onehot[...], head, 1, 0) + dot(onehot[...], rest, 1, 0)
            give[:, at(step, base)] = total[:owned]
            keep[:, at(step, base)] = total[owned:]
        return carry

    lax.fori_loop(0, half // TILE, make_query, 0)


def trail(first, query, rows, weight, rel, onehot):
    rows_dev, hidden = rows.shape
    width = weight.shape[0]
    count_rel = onehot.shape[0]
    vmem = pl.BlockSpec(memory_space=pltpu.VMEM)
    flops = 4 * rows_dev * width * hidden + 4 * rows_dev * count_rel * width
    return pl.pallas_call(
        trail_body,
        out_shape=(
            jax.ShapeDtypeStruct((rows_dev, hidden), BF16),
            jax.ShapeDtypeStruct((rows_dev, width), BF16),
            jax.ShapeDtypeStruct((count_rel // 2, width), F32),
            jax.ShapeDtypeStruct((count_rel // 2, width), F32),
            jax.ShapeDtypeStruct((rows_dev, width), BF16),
        ),
        in_specs=[pl.BlockSpec(memory_space=pltpu.SMEM)] + [vmem] * 5,
        out_specs=(vmem,) * 5,
        scratch_shapes=[pltpu.VMEM((rows_dev, hidden), BF16)],
        compiler_params=pltpu.CompilerParams(vmem_limit_bytes=GRANT),
        cost_estimate=pl.CostEstimate(
            flops=flops, bytes_accessed=4 * width * hidden, transcendentals=rows_dev * hidden
        ),
    )(first, query, rows, weight, rel, onehot)


def local(section_rows, weights, relation_table, relation_ids):
    rows = section_rows[0]
    weight = weights[0]
    rows_dev, width = rows.shape
    half = width // 2
    count_rel = relation_table.shape[0]
    chips = lax.axis_size("chip")
    first = lax.axis_index("hop") == 0
    core = lax.axis_index("core")
    chip = lax.axis_index("chip")
    total_rows = rows_dev * chips * 2
    cols = width // chips
    owned = count_rel // (4 * chips)

    def columns(left):
        return left.reshape(left.shape[0], chips, cols).transpose(1, 0, 2)

    onehot = (relation_ids[:, None] == lax.iota(jnp.int32, count_rel)[None, :]).astype(BF16)
    number = lax.iota(jnp.int32, count_rel)
    side = number // (count_rel // 2)
    dest = number % (count_rel // 2) // (2 * owned)
    hop = number % (2 * owned) // owned
    which_core = jnp.where(side == 1, core, 1 - core)
    relation = ((hop * chips + dest) * 2 + which_core) * owned + number % owned
    onehot_t = (relation[:, None] == relation_ids[None, :]).astype(BF16)

    own_query = lead(rows, weight)
    query = lax.ppermute(own_query, "hop", [(0, 1)])
    rel = dot(onehot, relation_table, 1, 0).astype(BF16)
    rel = rel.reshape(rows_dev, 2, half).transpose(1, 0, 2)
    right, grad_query, rel_give, rel_keep, mixed = trail(
        first.astype(jnp.int32).reshape(1), query, rows, weight, rel, onehot_t
    )
    query_back = lax.ppermute(grad_query, "hop", [(1, 0)])
    query_grad = jnp.where(first, query_back, grad_query)
    rel_chip = (rel_keep + swap_core(rel_give)).astype(BF16).reshape(chips, 2, owned, width)
    rel_back = lax.ppermute(rel_chip[:, 0], "hop", [(1, 0)])

    def chip_at(place):
        place = lax.rem(place, chips)
        return jnp.where(place < (chips + 1) // 2, 2 * place, 2 * (chips - place) - 1)

    ring = list(range(0, chips, 2)) + list(range(1, chips, 2))[::-1]
    place = jnp.where(lax.rem(chip, 2) == 0, chip // 2, chips - 1 - chip // 2)
    up = [(ring[i], ring[(i + 1) % chips]) for i in range(chips)]
    down = [(b, a) for a, b in up]
    blocks = [(right, 0, 0)]
    fwd = bwd = right
    for s in range(1, (chips + 1) // 2):
        fwd = lax.ppermute(fwd, "chip", up)
        bwd = lax.ppermute(bwd, "chip", down)
        blocks += [(fwd, chips - s, 0), (bwd, s, 0)]

    rel_own = jnp.where(first, rel_back, rel_chip[:, 1]).reshape(chips, owned, chips, cols)
    rel_own = rel_own.transpose(0, 2, 1, 3).reshape(chips, owned * chips, cols)
    left = columns(jnp.where(first, query_back, mixed))
    sent = jnp.concatenate([left, rel_own], axis=1)
    sent, _ = lax.optimization_barrier((sent, (blocks[-2][0], blocks[-1][0])))
    received = lax.all_to_all(sent, "chip", 0, 0, tiled=True)
    left_cols, rel_rows = received[:, :rows_dev], received[:, rows_dev:]
    rel_sum = jnp.sum(rel_rows.astype(F32), axis=0) * jnp.sqrt(F32(count_rel) / F32(total_rows))
    relation_grad = rel_sum.reshape(chips, owned, cols).transpose(1, 0, 2).reshape(owned, width)

    if chips % 2 == 0:
        mid = rows_dev // 2
        blocks.append((lax.ppermute(fwd[:mid], "chip", up), chips // 2, 0))
        blocks.append((lax.ppermute(bwd[mid:], "chip", down), chips // 2, mid))
    right_all = jnp.zeros((chips * rows_dev, width), BF16)
    for block, step, base in blocks:
        start = chip_at(place + step) * rows_dev + base
        right_all = lax.dynamic_update_slice_in_dim(right_all, block, start, 0)
    partial = dot(left_cols.reshape(chips * rows_dev, cols), right_all, 0, 0)
    partial = partial.reshape(2, cols // 2, width)
    keep = lax.dynamic_index_in_dim(partial, core, 0, keepdims=False)
    give = lax.dynamic_index_in_dim(partial, 1 - core, 0, keepdims=False)
    weight_grad = (keep + swap_core(give)) * (1.0 / jnp.sqrt(F32(total_rows)))
    return weight_grad[None], relation_grad, query_grad


def solution(mesh):
    hops, batch = mesh.devices.shape
    fine = Mesh(mesh.devices.reshape(hops, batch // 2, 2), ("hop", "chip", "core"))
    rows = ("chip", "core")
    return jax.shard_map(
        local,
        mesh=fine,
        in_specs=(P("hop", rows, None), P("hop", None, None), P(), P(rows)),
        out_specs=(P("hop", rows, None), P(("hop", "chip", "core"), None), P(rows, None)),
        check_vma=False,
    )
```

```python
import jax
import jax.numpy as jnp
from jax import lax
from jax.experimental import pallas as pl
from jax.experimental.pallas import tpu as pltpu
from jax.sharding import Mesh
from jax.sharding import PartitionSpec as P

F32 = jnp.float32
BF16 = jnp.bfloat16
TILE = 256
GRANT = 16 * 1024 * 1024


def dot(a, b, ca, cb):
    return lax.dot_general(a, b, (((ca,), (cb,)), ((), ())), preferred_element_type=F32)


def swap_core(block):
    return lax.ppermute(block, "core", [(0, 1), (1, 0)])


def mix(q_re, q_im, r_re, r_im):
    return (q_re * r_re - q_im * r_im).astype(BF16), (q_re * r_im + q_im * r_re).astype(BF16)


def at(step, base=0):
    return pl.ds(pl.multiple_of(base + step * TILE, TILE), TILE)


def lead_body(rows, weight, query):
    half = weight.shape[0] // 2
    for step in range(half // TILE):
        span = pl.ds(step * TILE, TILE)
        query[0, :, span] = dot(rows[...], weight[at(step)], 1, 1).astype(BF16)
        query[1, :, span] = dot(rows[...], weight[at(step, half)], 1, 1).astype(BF16)


def lead(rows, weight):
    rows_dev, hidden = rows.shape
    width = weight.shape[0]
    vmem = pl.BlockSpec(memory_space=pltpu.VMEM)
    return pl.pallas_call(
        lead_body,
        out_shape=jax.ShapeDtypeStruct((2, rows_dev, width // 2), BF16),
        in_specs=[vmem] * 2,
        out_specs=vmem,
        compiler_params=pltpu.CompilerParams(vmem_limit_bytes=GRANT),
        cost_estimate=pl.CostEstimate(
            flops=2 * rows_dev * width * hidden, bytes_accessed=2 * width * hidden, transcendentals=0
        ),
    )(rows, weight)


def trail_body(first, query, rows, weight, rel, onehot, right, query_grad, give, keep, mixed, hidden):
    width = weight.shape[0]
    half = width // 2
    is_first = first[0] == 1
    owned = give.shape[0]

    def make_mixed(step, carry):
        mixed[:, at(step)], mixed[:, at(step, half)] = mix(
            query[0, :, at(step)].astype(F32), query[1, :, at(step)].astype(F32),
            rel[0, :, at(step)].astype(F32), rel[1, :, at(step)].astype(F32),
        )
        return carry

    lax.fori_loop(0, half // TILE, make_mixed, 0)

    def make_hidden(step, carry):
        pre = dot(mixed[...], weight[:, at(step)], 1, 0)
        sig = jax.nn.sigmoid(pre)
        cot = rows[:, at(step)]
        grad = (cot.astype(F32) * (sig * (1.0 + pre * (1.0 - sig)))).astype(BF16)
        hidden[:, at(step)] = grad
        right[:, at(step)] = jnp.where(is_first, cot, grad)
        return carry

    lax.fori_loop(0, weight.shape[1] // TILE, make_hidden, 0)

    def make_query(step, carry):
        gz_re = dot(hidden[...], weight[at(step), :], 1, 1)
        gz_im = dot(hidden[...], weight[at(step, half), :], 1, 1)
        r_re, r_im = rel[0, :, at(step)].astype(F32), rel[1, :, at(step)].astype(F32)
        query_grad[:, at(step)] = (gz_re * r_re + gz_im * r_im).astype(BF16)
        query_grad[:, at(step, half)] = (gz_im * r_re - gz_re * r_im).astype(BF16)
        a, b = query[0, :, at(step)].astype(F32), query[1, :, at(step)].astype(F32)
        for base, grad in ((0, gz_re * a + gz_im * b), (half, gz_im * a - gz_re * b)):
            head = grad.astype(BF16)
            rest = (grad - head.astype(F32)).astype(BF16)
            total = dot(onehot[...], head, 1, 0) + dot(onehot[...], rest, 1, 0)
            give[:, at(step, base)] = total[:owned]
            keep[:, at(step, base)] = total[owned:]
        return carry

    lax.fori_loop(0, half // TILE, make_query, 0)


def trail(first, query, rows, weight, rel, onehot):
    rows_dev, hidden = rows.shape
    width = weight.shape[0]
    count_rel = onehot.shape[0]
    vmem = pl.BlockSpec(memory_space=pltpu.VMEM)
    flops = 4 * rows_dev * width * hidden + 4 * rows_dev * count_rel * width
    return pl.pallas_call(
        trail_body,
        out_shape=(
            jax.ShapeDtypeStruct((rows_dev, hidden), BF16),
            jax.ShapeDtypeStruct((rows_dev, width), BF16),
            jax.ShapeDtypeStruct((count_rel // 2, width), F32),
            jax.ShapeDtypeStruct((count_rel // 2, width), F32),
            jax.ShapeDtypeStruct((rows_dev, width), BF16),
        ),
        in_specs=[pl.BlockSpec(memory_space=pltpu.SMEM)] + [vmem] * 5,
        out_specs=(vmem,) * 5,
        scratch_shapes=[pltpu.VMEM((rows_dev, hidden), BF16)],
        compiler_params=pltpu.CompilerParams(vmem_limit_bytes=GRANT),
        cost_estimate=pl.CostEstimate(
            flops=flops, bytes_accessed=4 * width * hidden, transcendentals=rows_dev * hidden
        ),
    )(first, query, rows, weight, rel, onehot)


def local(section_rows, weights, relation_table, relation_ids):
    rows = section_rows[0]
    weight = weights[0]
    rows_dev, width = rows.shape
    half = width // 2
    count_rel = relation_table.shape[0]
    chips = lax.axis_size("chip")
    first = lax.axis_index("hop") == 0
    core = lax.axis_index("core")
    chip = lax.axis_index("chip")
    total_rows = rows_dev * chips * 2
    cols = width // chips
    owned = count_rel // (4 * chips)

    def columns(left):
        return left.reshape(left.shape[0], chips, cols).transpose(1, 0, 2)

    onehot = (relation_ids[:, None] == lax.iota(jnp.int32, count_rel)[None, :]).astype(BF16)
    number = lax.iota(jnp.int32, count_rel)
    side = number // (count_rel // 2)
    dest = number % (count_rel // 2) // (2 * owned)
    hop = number % (2 * owned) // owned
    which_core = jnp.where(side == 1, core, 1 - core)
    relation = ((hop * chips + dest) * 2 + which_core) * owned + number % owned
    onehot_t = (relation[:, None] == relation_ids[None, :]).astype(BF16)

    own_query = lead(rows, weight)
    query = lax.ppermute(own_query, "hop", [(0, 1)])
    rel = dot(onehot, relation_table, 1, 0).astype(BF16)
    rel = rel.reshape(rows_dev, 2, half).transpose(1, 0, 2)
    right, grad_query, rel_give, rel_keep, mixed = trail(
        first.astype(jnp.int32).reshape(1), query, rows, weight, rel, onehot_t
    )
    query_back = lax.ppermute(grad_query, "hop", [(1, 0)])
    query_grad = jnp.where(first, query_back, grad_query)
    rel_chip = (rel_keep + swap_core(rel_give)).astype(BF16).reshape(chips, 2, owned, width)
    rel_back = lax.ppermute(rel_chip[:, 0], "hop", [(1, 0)])

    def chip_at(place):
        place = lax.rem(place, chips)
        return jnp.where(place < (chips + 1) // 2, 2 * place, 2 * (chips - place) - 1)

    ring = list(range(0, chips, 2)) + list(range(1, chips, 2))[::-1]
    place = jnp.where(lax.rem(chip, 2) == 0, chip // 2, chips - 1 - chip // 2)
    up = [(ring[i], ring[(i + 1) % chips]) for i in range(chips)]
    down = [(b, a) for a, b in up]
    blocks = [(right, 0, 0)]
    fwd = bwd = right
    for s in range(1, (chips + 1) // 2):
        fwd = lax.ppermute(fwd, "chip", up)
        bwd = lax.ppermute(bwd, "chip", down)
        blocks += [(fwd, chips - s, 0), (bwd, s, 0)]

    rel_own = jnp.where(first, rel_back, rel_chip[:, 1]).reshape(chips, owned, chips, cols)
    rel_own = rel_own.transpose(0, 2, 1, 3).reshape(chips, owned * chips, cols)
    left = columns(jnp.where(first, query_back, mixed))
    sent = jnp.concatenate([left, rel_own], axis=1)
    sent, _ = lax.optimization_barrier((sent, (blocks[3][0], blocks[4][0])))
    received = lax.all_to_all(sent, "chip", 0, 0, tiled=True)
    left_cols, rel_rows = received[:, :rows_dev], received[:, rows_dev:]
    rel_sum = jnp.sum(rel_rows.astype(F32), axis=0) * jnp.sqrt(F32(count_rel) / F32(total_rows))
    relation_grad = rel_sum.reshape(chips, owned, cols).transpose(1, 0, 2).reshape(owned, width)

    if chips % 2 == 0:
        mid = rows_dev // 2
        blocks.append((lax.ppermute(fwd[:mid], "chip", up), chips // 2, 0))
        blocks.append((lax.ppermute(bwd[mid:], "chip", down), chips // 2, mid))
    right_all = jnp.zeros((chips * rows_dev, width), BF16)
    for block, step, base in blocks:
        start = chip_at(place + step) * rows_dev + base
        right_all = lax.dynamic_update_slice_in_dim(right_all, block, start, 0)
    partial = dot(left_cols.reshape(chips * rows_dev, cols), right_all, 0, 0)
    partial = partial.reshape(2, cols // 2, width)
    keep = lax.dynamic_index_in_dim(partial, core, 0, keepdims=False)
    give = lax.dynamic_index_in_dim(partial, 1 - core, 0, keepdims=False)
    weight_grad = (keep + swap_core(give)) * (1.0 / jnp.sqrt(F32(total_rows)))
    return weight_grad[None], relation_grad, query_grad


def solution(mesh):
    hops, batch = mesh.devices.shape
    fine = Mesh(mesh.devices.reshape(hops, batch // 2, 2), ("hop", "chip", "core"))
    rows = ("chip", "core")
    return jax.shard_map(
        local,
        mesh=fine,
        in_specs=(P("hop", rows, None), P("hop", None, None), P(), P(rows)),
        out_specs=(P("hop", rows, None), P(("hop", "chip", "core"), None), P(rows, None)),
        check_vma=False,
    )
```

```python
import jax
import jax.numpy as jnp
from jax import lax
from jax.experimental import pallas as pl
from jax.experimental.pallas import tpu as pltpu
from jax.sharding import Mesh
from jax.sharding import PartitionSpec as P

F32 = jnp.float32
BF16 = jnp.bfloat16
TILE = 256
GRANT = 16 * 1024 * 1024


def dot(a, b, ca, cb):
    return lax.dot_general(a, b, (((ca,), (cb,)), ((), ())), preferred_element_type=F32)


def swap_core(block):
    return lax.ppermute(block, "core", [(0, 1), (1, 0)])


def mix(q_re, q_im, r_re, r_im):
    return (q_re * r_re - q_im * r_im).astype(BF16), (q_re * r_im + q_im * r_re).astype(BF16)


def at(step, base=0):
    return pl.ds(pl.multiple_of(base + step * TILE, TILE), TILE)


def lead_body(rows, weight, query):
    half = weight.shape[0] // 2
    for step in range(half // TILE):
        span = pl.ds(step * TILE, TILE)
        query[0, :, span] = dot(rows[...], weight[at(step)], 1, 1).astype(BF16)
        query[1, :, span] = dot(rows[...], weight[at(step, half)], 1, 1).astype(BF16)


def lead(rows, weight):
    rows_dev, hidden = rows.shape
    width = weight.shape[0]
    vmem = pl.BlockSpec(memory_space=pltpu.VMEM)
    return pl.pallas_call(
        lead_body,
        out_shape=jax.ShapeDtypeStruct((2, rows_dev, width // 2), BF16),
        in_specs=[vmem] * 2,
        out_specs=vmem,
        compiler_params=pltpu.CompilerParams(vmem_limit_bytes=GRANT),
        cost_estimate=pl.CostEstimate(
            flops=2 * rows_dev * width * hidden, bytes_accessed=2 * width * hidden, transcendentals=0
        ),
    )(rows, weight)


def trail_body(first, query, rows, weight, rel, onehot, right, query_grad, give, keep, mixed, hidden):
    width = weight.shape[0]
    half = width // 2
    is_first = first[0] == 1
    owned = give.shape[0]

    def make_mixed(step, carry):
        mixed[:, at(step)], mixed[:, at(step, half)] = mix(
            query[0, :, at(step)].astype(F32), query[1, :, at(step)].astype(F32),
            rel[0, :, at(step)].astype(F32), rel[1, :, at(step)].astype(F32),
        )
        return carry

    lax.fori_loop(0, half // TILE, make_mixed, 0)

    def make_hidden(step, carry):
        pre = dot(mixed[...], weight[:, at(step)], 1, 0)
        sig = jax.nn.sigmoid(pre)
        cot = rows[:, at(step)]
        grad = (cot.astype(F32) * (sig * (1.0 + pre * (1.0 - sig)))).astype(BF16)
        hidden[:, at(step)] = grad
        right[:, at(step)] = jnp.where(is_first, cot, grad)
        return carry

    lax.fori_loop(0, weight.shape[1] // TILE, make_hidden, 0)

    def make_query(step, carry):
        gz_re = dot(hidden[...], weight[at(step), :], 1, 1)
        gz_im = dot(hidden[...], weight[at(step, half), :], 1, 1)
        r_re, r_im = rel[0, :, at(step)].astype(F32), rel[1, :, at(step)].astype(F32)
        query_grad[:, at(step)] = (gz_re * r_re + gz_im * r_im).astype(BF16)
        query_grad[:, at(step, half)] = (gz_im * r_re - gz_re * r_im).astype(BF16)
        a, b = query[0, :, at(step)].astype(F32), query[1, :, at(step)].astype(F32)
        for base, grad in ((0, gz_re * a + gz_im * b), (half, gz_im * a - gz_re * b)):
            head = grad.astype(BF16)
            rest = (grad - head.astype(F32)).astype(BF16)
            total = dot(onehot[...], head, 1, 0) + dot(onehot[...], rest, 1, 0)
            give[:, at(step, base)] = total[:owned]
            keep[:, at(step, base)] = total[owned:]
        return carry

    lax.fori_loop(0, half // TILE, make_query, 0)


def trail(first, query, rows, weight, rel, onehot):
    rows_dev, hidden = rows.shape
    width = weight.shape[0]
    count_rel = onehot.shape[0]
    vmem = pl.BlockSpec(memory_space=pltpu.VMEM)
    flops = 4 * rows_dev * width * hidden + 4 * rows_dev * count_rel * width
    return pl.pallas_call(
        trail_body,
        out_shape=(
            jax.ShapeDtypeStruct((rows_dev, hidden), BF16),
            jax.ShapeDtypeStruct((rows_dev, width), BF16),
            jax.ShapeDtypeStruct((count_rel // 2, width), F32),
            jax.ShapeDtypeStruct((count_rel // 2, width), F32),
            jax.ShapeDtypeStruct((rows_dev, width), BF16),
        ),
        in_specs=[pl.BlockSpec(memory_space=pltpu.SMEM)] + [vmem] * 5,
        out_specs=(vmem,) * 5,
        scratch_shapes=[pltpu.VMEM((rows_dev, hidden), BF16)],
        compiler_params=pltpu.CompilerParams(vmem_limit_bytes=GRANT),
        cost_estimate=pl.CostEstimate(
            flops=flops, bytes_accessed=4 * width * hidden, transcendentals=rows_dev * hidden
        ),
    )(first, query, rows, weight, rel, onehot)


def local(section_rows, weights, relation_table, relation_ids):
    rows = section_rows[0]
    weight = weights[0]
    rows_dev, width = rows.shape
    half = width // 2
    count_rel = relation_table.shape[0]
    chips = lax.axis_size("chip")
    first = lax.axis_index("hop") == 0
    core = lax.axis_index("core")
    chip = lax.axis_index("chip")
    total_rows = rows_dev * chips * 2
    cols = width // chips
    owned = count_rel // (4 * chips)

    def columns(left):
        return left.reshape(left.shape[0], chips, cols).transpose(1, 0, 2)

    onehot = (relation_ids[:, None] == lax.iota(jnp.int32, count_rel)[None, :]).astype(BF16)
    number = lax.iota(jnp.int32, count_rel)
    side = number // (count_rel // 2)
    dest = number % (count_rel // 2) // (2 * owned)
    hop = number % (2 * owned) // owned
    which_core = jnp.where(side == 1, core, 1 - core)
    relation = ((hop * chips + dest) * 2 + which_core) * owned + number % owned
    onehot_t = (relation[:, None] == relation_ids[None, :]).astype(BF16)

    own_query = lead(rows, weight)
    query = lax.ppermute(own_query, "hop", [(0, 1)])
    rel = dot(onehot, relation_table, 1, 0).astype(BF16)
    rel = rel.reshape(rows_dev, 2, half).transpose(1, 0, 2)
    right, grad_query, rel_give, rel_keep, mixed = trail(
        first.astype(jnp.int32).reshape(1), query, rows, weight, rel, onehot_t
    )
    query_back = lax.ppermute(grad_query, "hop", [(1, 0)])
    query_grad = jnp.where(first, query_back, grad_query)
    rel_chip = (rel_keep + swap_core(rel_give)).astype(BF16).reshape(chips, 2, owned, width)
    rel_back = lax.ppermute(rel_chip[:, 0], "hop", [(1, 0)])

    def chip_at(place):
        place = lax.rem(place, chips)
        return jnp.where(place < (chips + 1) // 2, 2 * place, 2 * (chips - place) - 1)

    ring = list(range(0, chips, 2)) + list(range(1, chips, 2))[::-1]
    place = jnp.where(lax.rem(chip, 2) == 0, chip // 2, chips - 1 - chip // 2)
    up = [(ring[i], ring[(i + 1) % chips]) for i in range(chips)]
    down = [(b, a) for a, b in up]
    blocks = [(right, 0, 0)]
    fwd = bwd = right
    for s in range(1, (chips + 1) // 2):
        fwd = lax.ppermute(fwd, "chip", up)
        bwd = lax.ppermute(bwd, "chip", down)
        blocks += [(fwd, chips - s, 0), (bwd, s, 0)]

    rel_own = jnp.where(first, rel_back, rel_chip[:, 1]).reshape(chips, owned, chips, cols)
    rel_own = rel_own.transpose(0, 2, 1, 3).reshape(chips, owned * chips, cols)
    left = columns(jnp.where(first, query_back, mixed))
    sent = jnp.concatenate([left, rel_own], axis=1)
    sent, _ = lax.optimization_barrier((sent, (blocks[3][0], blocks[4][0])))
    received = lax.all_to_all(sent, "chip", 0, 0, tiled=True)
    left_cols, rel_rows = received[:, :rows_dev], received[:, rows_dev:]
    rel_sum = jnp.sum(rel_rows.astype(F32), axis=0) * jnp.sqrt(F32(count_rel) / F32(total_rows))
    relation_grad = rel_sum.reshape(chips, owned, cols).transpose(1, 0, 2).reshape(owned, width)

    if chips % 2 == 0:
        mid = rows_dev // 2
        blocks.append((lax.ppermute(fwd[:mid], "chip", up), chips // 2, 0))
        blocks.append((lax.ppermute(bwd[mid:], "chip", down), chips // 2, mid))
    right_all = jnp.zeros((chips * rows_dev, width), BF16)
    for block, step, base in blocks:
        start = chip_at(place + step) * rows_dev + base
        right_all = lax.dynamic_update_slice_in_dim(right_all, block, start, 0)
    lower, upper = left_cols[..., :cols // 2], left_cols[..., cols // 2:]
    give = jnp.where(core == 0, upper, lower).reshape(chips * rows_dev, cols // 2)
    keep = jnp.where(core == 0, lower, upper).reshape(chips * rows_dev, cols // 2)
    got = swap_core(dot(give, right_all, 0, 0))
    weight_grad = (dot(keep, right_all, 0, 0) + got) * (1.0 / jnp.sqrt(F32(total_rows)))
    return weight_grad[None], relation_grad, query_grad


def solution(mesh):
    hops, batch = mesh.devices.shape
    fine = Mesh(mesh.devices.reshape(hops, batch // 2, 2), ("hop", "chip", "core"))
    rows = ("chip", "core")
    return jax.shard_map(
        local,
        mesh=fine,
        in_specs=(P("hop", rows, None), P("hop", None, None), P(), P(rows)),
        out_specs=(P("hop", rows, None), P(("hop", "chip", "core"), None), P(rows, None)),
        check_vma=False,
    )
```

```python
import jax
import jax.numpy as jnp
from jax import lax
from jax.experimental import pallas as pl
from jax.experimental.pallas import tpu as pltpu
from jax.sharding import Mesh
from jax.sharding import PartitionSpec as P

F32 = jnp.float32
BF16 = jnp.bfloat16
TILE = 256
GRANT = 16 * 1024 * 1024


def dot(a, b, ca, cb):
    return lax.dot_general(a, b, (((ca,), (cb,)), ((), ())), preferred_element_type=F32)


def swap_core(block):
    return lax.ppermute(block, "core", [(0, 1), (1, 0)])


def mix(q_re, q_im, r_re, r_im):
    return (q_re * r_re - q_im * r_im).astype(BF16), (q_re * r_im + q_im * r_re).astype(BF16)


def at(step, base=0):
    return pl.ds(pl.multiple_of(base + step * TILE, TILE), TILE)


def lead_body(rows, weight, query):
    half = weight.shape[0] // 2
    for step in range(half // TILE):
        span = pl.ds(step * TILE, TILE)
        query[0, :, span] = dot(rows[...], weight[at(step)], 1, 1).astype(BF16)
        query[1, :, span] = dot(rows[...], weight[at(step, half)], 1, 1).astype(BF16)


def lead(rows, weight):
    rows_dev, hidden = rows.shape
    width = weight.shape[0]
    vmem = pl.BlockSpec(memory_space=pltpu.VMEM)
    return pl.pallas_call(
        lead_body,
        out_shape=jax.ShapeDtypeStruct((2, rows_dev, width // 2), BF16),
        in_specs=[vmem] * 2,
        out_specs=vmem,
        compiler_params=pltpu.CompilerParams(vmem_limit_bytes=GRANT),
        cost_estimate=pl.CostEstimate(
            flops=2 * rows_dev * width * hidden, bytes_accessed=2 * width * hidden, transcendentals=0
        ),
    )(rows, weight)


def trail_body(first, query, rows, weight, rel, onehot, right, query_grad, give, keep, mixed, hidden):
    width = weight.shape[0]
    half = width // 2
    is_first = first[0] == 1
    owned = give.shape[0]

    def make_mixed(step, carry):
        mixed[:, at(step)], mixed[:, at(step, half)] = mix(
            query[0, :, at(step)].astype(F32), query[1, :, at(step)].astype(F32),
            rel[0, :, at(step)].astype(F32), rel[1, :, at(step)].astype(F32),
        )
        return carry

    lax.fori_loop(0, half // TILE, make_mixed, 0)

    def make_hidden(step, carry):
        pre = dot(mixed[...], weight[:, at(step)], 1, 0)
        sig = jax.nn.sigmoid(pre)
        cot = rows[:, at(step)]
        grad = (cot.astype(F32) * (sig * (1.0 + pre * (1.0 - sig)))).astype(BF16)
        hidden[:, at(step)] = grad
        right[:, at(step)] = jnp.where(is_first, cot, grad)
        return carry

    lax.fori_loop(0, weight.shape[1] // TILE, make_hidden, 0)

    def make_query(step, carry):
        gz_re = dot(hidden[...], weight[at(step), :], 1, 1)
        gz_im = dot(hidden[...], weight[at(step, half), :], 1, 1)
        r_re, r_im = rel[0, :, at(step)].astype(F32), rel[1, :, at(step)].astype(F32)
        query_grad[:, at(step)] = (gz_re * r_re + gz_im * r_im).astype(BF16)
        query_grad[:, at(step, half)] = (gz_im * r_re - gz_re * r_im).astype(BF16)
        a, b = query[0, :, at(step)].astype(F32), query[1, :, at(step)].astype(F32)
        for base, grad in ((0, gz_re * a + gz_im * b), (half, gz_im * a - gz_re * b)):
            head = grad.astype(BF16)
            rest = (grad - head.astype(F32)).astype(BF16)
            total = dot(onehot[...], head, 1, 0) + dot(onehot[...], rest, 1, 0)
            give[:, at(step, base)] = total[:owned]
            keep[:, at(step, base)] = total[owned:]
        return carry

    lax.fori_loop(0, half // TILE, make_query, 0)


def trail(first, query, rows, weight, rel, onehot):
    rows_dev, hidden = rows.shape
    width = weight.shape[0]
    count_rel = onehot.shape[0]
    vmem = pl.BlockSpec(memory_space=pltpu.VMEM)
    flops = 4 * rows_dev * width * hidden + 4 * rows_dev * count_rel * width
    return pl.pallas_call(
        trail_body,
        out_shape=(
            jax.ShapeDtypeStruct((rows_dev, hidden), BF16),
            jax.ShapeDtypeStruct((rows_dev, width), BF16),
            jax.ShapeDtypeStruct((count_rel // 2, width), F32),
            jax.ShapeDtypeStruct((count_rel // 2, width), F32),
            jax.ShapeDtypeStruct((rows_dev, width), BF16),
        ),
        in_specs=[pl.BlockSpec(memory_space=pltpu.SMEM)] + [vmem] * 5,
        out_specs=(vmem,) * 5,
        scratch_shapes=[pltpu.VMEM((rows_dev, hidden), BF16)],
        compiler_params=pltpu.CompilerParams(vmem_limit_bytes=GRANT),
        cost_estimate=pl.CostEstimate(
            flops=flops, bytes_accessed=4 * width * hidden, transcendentals=rows_dev * hidden
        ),
    )(first, query, rows, weight, rel, onehot)


def local(section_rows, weights, relation_table, relation_ids):
    rows = section_rows[0]
    weight = weights[0]
    rows_dev, width = rows.shape
    half = width // 2
    count_rel = relation_table.shape[0]
    chips = lax.axis_size("chip")
    first = lax.axis_index("hop") == 0
    core = lax.axis_index("core")
    chip = lax.axis_index("chip")
    total_rows = rows_dev * chips * 2
    cols = width // chips
    owned = count_rel // (4 * chips)

    def columns(left):
        return left.reshape(left.shape[0], chips, cols).transpose(1, 0, 2)

    onehot = (relation_ids[:, None] == lax.iota(jnp.int32, count_rel)[None, :]).astype(BF16)
    number = lax.iota(jnp.int32, count_rel)
    side = number // (count_rel // 2)
    dest = number % (count_rel // 2) // (2 * owned)
    hop = number % (2 * owned) // owned
    which_core = jnp.where(side == 1, core, 1 - core)
    relation = ((hop * chips + dest) * 2 + which_core) * owned + number % owned
    onehot_t = (relation[:, None] == relation_ids[None, :]).astype(BF16)

    own_query = lead(rows, weight)
    query = lax.ppermute(own_query, "hop", [(0, 1)])
    rel = dot(onehot, relation_table, 1, 0).astype(BF16)
    rel = rel.reshape(rows_dev, 2, half).transpose(1, 0, 2)
    right, grad_query, rel_give, rel_keep, mixed = trail(
        first.astype(jnp.int32).reshape(1), query, rows, weight, rel, onehot_t
    )
    query_back = lax.ppermute(grad_query, "hop", [(1, 0)])
    query_grad = jnp.where(first, query_back, grad_query)
    rel_chip = (rel_keep + swap_core(rel_give)).astype(BF16).reshape(chips, 2, owned, width)
    rel_back = lax.ppermute(rel_chip[:, 0], "hop", [(1, 0)])

    def chip_at(place):
        place = lax.rem(place, chips)
        return jnp.where(place < (chips + 1) // 2, 2 * place, 2 * (chips - place) - 1)

    ring = list(range(0, chips, 2)) + list(range(1, chips, 2))[::-1]
    place = jnp.where(lax.rem(chip, 2) == 0, chip // 2, chips - 1 - chip // 2)
    up = [(ring[i], ring[(i + 1) % chips]) for i in range(chips)]
    down = [(b, a) for a, b in up]
    blocks = [(right, 0, 0)]
    fwd = bwd = right
    for s in range(1, (chips + 1) // 2):
        fwd = lax.ppermute(fwd, "chip", up)
        bwd = lax.ppermute(bwd, "chip", down)
        blocks += [(fwd, chips - s, 0), (bwd, s, 0)]

    rel_own = jnp.where(first, rel_back, rel_chip[:, 1]).reshape(chips, owned, chips, cols)
    rel_own = rel_own.transpose(0, 2, 1, 3).reshape(chips, owned * chips, cols)
    left = columns(jnp.where(first, query_back, mixed))
    sent = jnp.concatenate([left, rel_own], axis=1)
    sent, _ = lax.optimization_barrier((sent, (blocks[3][0], blocks[4][0])))
    received = lax.all_to_all(sent, "chip", 0, 0, tiled=True)
    left_cols, rel_rows = received[:, :rows_dev], received[:, rows_dev:]
    rel_sum = jnp.sum(rel_rows.astype(F32), axis=0) * jnp.sqrt(F32(count_rel) / F32(total_rows))
    relation_grad = rel_sum.reshape(chips, owned, cols).transpose(1, 0, 2).reshape(owned, width)

    if chips % 2 == 0:
        mid = rows_dev // 2
        blocks.append((lax.ppermute(fwd[:mid], "chip", up), chips // 2, 0))
        blocks.append((lax.ppermute(bwd[mid:], "chip", down), chips // 2, mid))
    right_all = jnp.zeros((chips * rows_dev, width), BF16)
    for block, step, base in blocks:
        start = chip_at(place + step) * rows_dev + base
        right_all = lax.dynamic_update_slice_in_dim(right_all, block, start, 0)
    lower, upper = left_cols[..., :cols // 2], left_cols[..., cols // 2:]
    give = jnp.where(core == 0, upper, lower).reshape(chips * rows_dev, cols // 2)
    keep = jnp.where(core == 0, lower, upper).reshape(chips * rows_dev, cols // 2)
    got = swap_core(dot(give, right_all, 0, 0))
    own = lax.optimization_barrier(dot(keep, right_all, 0, 0))
    weight_grad = (own + got) * (1.0 / jnp.sqrt(F32(total_rows)))
    return weight_grad[None], relation_grad, query_grad


def solution(mesh):
    hops, batch = mesh.devices.shape
    fine = Mesh(mesh.devices.reshape(hops, batch // 2, 2), ("hop", "chip", "core"))
    rows = ("chip", "core")
    return jax.shard_map(
        local,
        mesh=fine,
        in_specs=(P("hop", rows, None), P("hop", None, None), P(), P(rows)),
        out_specs=(P("hop", rows, None), P(("hop", "chip", "core"), None), P(rows, None)),
        check_vma=False,
    )
```

```python
import jax
import jax.numpy as jnp
from jax import lax
from jax.experimental import pallas as pl
from jax.experimental.pallas import tpu as pltpu
from jax.sharding import Mesh
from jax.sharding import PartitionSpec as P

F32 = jnp.float32
BF16 = jnp.bfloat16
TILE = 256
GRANT = 16 * 1024 * 1024


def dot(a, b, ca, cb):
    return lax.dot_general(a, b, (((ca,), (cb,)), ((), ())), preferred_element_type=F32)


def swap_core(block):
    return lax.ppermute(block, "core", [(0, 1), (1, 0)])


def mix(q_re, q_im, r_re, r_im):
    return (q_re * r_re - q_im * r_im).astype(BF16), (q_re * r_im + q_im * r_re).astype(BF16)


def at(step, base=0):
    return pl.ds(pl.multiple_of(base + step * TILE, TILE), TILE)


def lead_body(rows, weight, query):
    half = weight.shape[0] // 2
    for step in range(half // TILE):
        span = pl.ds(step * TILE, TILE)
        query[0, :, span] = dot(rows[...], weight[at(step)], 1, 1).astype(BF16)
        query[1, :, span] = dot(rows[...], weight[at(step, half)], 1, 1).astype(BF16)


def lead(rows, weight):
    rows_dev, hidden = rows.shape
    width = weight.shape[0]
    vmem = pl.BlockSpec(memory_space=pltpu.VMEM)
    return pl.pallas_call(
        lead_body,
        out_shape=jax.ShapeDtypeStruct((2, rows_dev, width // 2), BF16),
        in_specs=[vmem] * 2,
        out_specs=vmem,
        compiler_params=pltpu.CompilerParams(vmem_limit_bytes=GRANT),
        cost_estimate=pl.CostEstimate(
            flops=2 * rows_dev * width * hidden, bytes_accessed=2 * width * hidden, transcendentals=0
        ),
    )(rows, weight)


def trail_body(first, query, rows, weight, rel, onehot, right, query_grad, give, keep, mixed, hidden):
    width = weight.shape[0]
    half = width // 2
    is_first = first[0] == 1
    owned = give.shape[0]

    def make_mixed(step, carry):
        mixed[:, at(step)], mixed[:, at(step, half)] = mix(
            query[0, :, at(step)].astype(F32), query[1, :, at(step)].astype(F32),
            rel[0, :, at(step)].astype(F32), rel[1, :, at(step)].astype(F32),
        )
        return carry

    lax.fori_loop(0, half // TILE, make_mixed, 0)

    def make_hidden(step, carry):
        pre = dot(mixed[...], weight[:, at(step)], 1, 0)
        sig = jax.nn.sigmoid(pre)
        cot = rows[:, at(step)]
        grad = (cot.astype(F32) * (sig * (1.0 + pre * (1.0 - sig)))).astype(BF16)
        hidden[:, at(step)] = grad
        right[:, at(step)] = jnp.where(is_first, cot, grad)
        return carry

    lax.fori_loop(0, weight.shape[1] // TILE, make_hidden, 0)

    def make_query(step, carry):
        gz_re = dot(hidden[...], weight[at(step), :], 1, 1)
        gz_im = dot(hidden[...], weight[at(step, half), :], 1, 1)
        r_re, r_im = rel[0, :, at(step)].astype(F32), rel[1, :, at(step)].astype(F32)
        query_grad[:, at(step)] = (gz_re * r_re + gz_im * r_im).astype(BF16)
        query_grad[:, at(step, half)] = (gz_im * r_re - gz_re * r_im).astype(BF16)
        a, b = query[0, :, at(step)].astype(F32), query[1, :, at(step)].astype(F32)
        for base, grad in ((0, gz_re * a + gz_im * b), (half, gz_im * a - gz_re * b)):
            head = grad.astype(BF16)
            rest = (grad - head.astype(F32)).astype(BF16)
            total = dot(onehot[...], head, 1, 0) + dot(onehot[...], rest, 1, 0)
            give[:, at(step, base)] = total[:owned]
            keep[:, at(step, base)] = total[owned:]
        return carry

    lax.fori_loop(0, half // TILE, make_query, 0)


def trail(first, query, rows, weight, rel, onehot):
    rows_dev, hidden = rows.shape
    width = weight.shape[0]
    count_rel = onehot.shape[0]
    vmem = pl.BlockSpec(memory_space=pltpu.VMEM)
    flops = 4 * rows_dev * width * hidden + 4 * rows_dev * count_rel * width
    return pl.pallas_call(
        trail_body,
        out_shape=(
            jax.ShapeDtypeStruct((rows_dev, hidden), BF16),
            jax.ShapeDtypeStruct((rows_dev, width), BF16),
            jax.ShapeDtypeStruct((count_rel // 2, width), F32),
            jax.ShapeDtypeStruct((count_rel // 2, width), F32),
            jax.ShapeDtypeStruct((rows_dev, width), BF16),
        ),
        in_specs=[pl.BlockSpec(memory_space=pltpu.SMEM)] + [vmem] * 5,
        out_specs=(vmem,) * 5,
        scratch_shapes=[pltpu.VMEM((rows_dev, hidden), BF16)],
        compiler_params=pltpu.CompilerParams(vmem_limit_bytes=GRANT),
        cost_estimate=pl.CostEstimate(
            flops=flops, bytes_accessed=4 * width * hidden, transcendentals=rows_dev * hidden
        ),
    )(first, query, rows, weight, rel, onehot)


def local(section_rows, weights, relation_table, relation_ids):
    rows = section_rows[0]
    weight = weights[0]
    rows_dev, width = rows.shape
    half = width // 2
    count_rel = relation_table.shape[0]
    chips = lax.axis_size("chip")
    first = lax.axis_index("hop") == 0
    core = lax.axis_index("core")
    chip = lax.axis_index("chip")
    total_rows = rows_dev * chips * 2
    cols = width // chips
    owned = count_rel // (4 * chips)

    def columns(left):
        return left.reshape(left.shape[0], chips, cols).transpose(1, 0, 2)

    onehot = (relation_ids[:, None] == lax.iota(jnp.int32, count_rel)[None, :]).astype(BF16)
    number = lax.iota(jnp.int32, count_rel)
    side = number // (count_rel // 2)
    dest = number % (count_rel // 2) // (2 * owned)
    hop = number % (2 * owned) // owned
    which_core = jnp.where(side == 1, core, 1 - core)
    relation = ((hop * chips + dest) * 2 + which_core) * owned + number % owned
    onehot_t = (relation[:, None] == relation_ids[None, :]).astype(BF16)

    own_query = lead(rows, weight)
    query = lax.ppermute(own_query, "hop", [(0, 1)])
    rel = dot(onehot, relation_table, 1, 0).astype(BF16)
    rel = rel.reshape(rows_dev, 2, half).transpose(1, 0, 2)
    right, grad_query, rel_give, rel_keep, mixed = trail(
        first.astype(jnp.int32).reshape(1), query, rows, weight, rel, onehot_t
    )
    query_back = lax.ppermute(grad_query, "hop", [(1, 0)])
    query_grad = jnp.where(first, query_back, grad_query)
    rel_chip = (rel_keep + swap_core(rel_give)).astype(BF16).reshape(chips, 2, owned, width)
    rel_back = lax.ppermute(rel_chip[:, 0], "hop", [(1, 0)])

    def chip_at(place):
        place = lax.rem(place, chips)
        return jnp.where(place < (chips + 1) // 2, 2 * place, 2 * (chips - place) - 1)

    ring = list(range(0, chips, 2)) + list(range(1, chips, 2))[::-1]
    place = jnp.where(lax.rem(chip, 2) == 0, chip // 2, chips - 1 - chip // 2)
    up = [(ring[i], ring[(i + 1) % chips]) for i in range(chips)]
    down = [(b, a) for a, b in up]
    blocks = [(right, 0, 0)]
    fwd = bwd = right
    for s in range(1, (chips + 1) // 2):
        fwd = lax.ppermute(fwd, "chip", up)
        bwd = lax.ppermute(bwd, "chip", down)
        blocks += [(fwd, chips - s, 0), (bwd, s, 0)]

    rel_own = jnp.where(first, rel_back, rel_chip[:, 1]).reshape(chips, owned, chips, cols)
    rel_own = rel_own.transpose(0, 2, 1, 3).reshape(chips, owned * chips, cols)
    left = columns(jnp.where(first, query_back, mixed))
    sent = jnp.concatenate([left, rel_own], axis=1)
    sent, _ = lax.optimization_barrier((sent, (blocks[3][0], blocks[4][0])))
    received = lax.all_to_all(sent, "chip", 0, 0, tiled=True)
    left_cols, rel_rows = received[:, :rows_dev], received[:, rows_dev:]
    rel_sum = jnp.sum(rel_rows.astype(F32), axis=0) * jnp.sqrt(F32(count_rel) / F32(total_rows))
    relation_grad = rel_sum.reshape(chips, owned, cols).transpose(1, 0, 2).reshape(owned, width)

    if chips % 2 == 0:
        mid = rows_dev // 2
        blocks.append((lax.ppermute(fwd[:mid], "chip", up), chips // 2, 0))
        blocks.append((lax.ppermute(bwd[mid:], "chip", down), chips // 2, mid))
    right_all, _ = lax.optimization_barrier((jnp.zeros((chips * rows_dev, width), BF16), rel_chip))
    for block, step, base in blocks:
        start = chip_at(place + step) * rows_dev + base
        right_all = lax.dynamic_update_slice_in_dim(right_all, block, start, 0)
    lower, upper = left_cols[..., :cols // 2], left_cols[..., cols // 2:]
    give = jnp.where(core == 0, upper, lower).reshape(chips * rows_dev, cols // 2)
    keep = jnp.where(core == 0, lower, upper).reshape(chips * rows_dev, cols // 2)
    got = swap_core(dot(give, right_all, 0, 0))
    own = lax.optimization_barrier(dot(keep, right_all, 0, 0))
    weight_grad = (own + got) * (1.0 / jnp.sqrt(F32(total_rows)))
    return weight_grad[None], relation_grad, query_grad


def solution(mesh):
    hops, batch = mesh.devices.shape
    fine = Mesh(mesh.devices.reshape(hops, batch // 2, 2), ("hop", "chip", "core"))
    rows = ("chip", "core")
    return jax.shard_map(
        local,
        mesh=fine,
        in_specs=(P("hop", rows, None), P("hop", None, None), P(), P(rows)),
        out_specs=(P("hop", rows, None), P(("hop", "chip", "core"), None), P(rows, None)),
        check_vma=False,
    )
```

```python
import jax
import jax.numpy as jnp
from jax import lax
from jax.experimental import pallas as pl
from jax.experimental.pallas import tpu as pltpu
from jax.sharding import Mesh
from jax.sharding import PartitionSpec as P

F32 = jnp.float32
BF16 = jnp.bfloat16
TILE = 256
GRANT = 16 * 1024 * 1024


def dot(a, b, ca, cb):
    return lax.dot_general(a, b, (((ca,), (cb,)), ((), ())), preferred_element_type=F32)


def swap_core(block):
    return lax.ppermute(block, "core", [(0, 1), (1, 0)])


def mix(q_re, q_im, r_re, r_im):
    return (q_re * r_re - q_im * r_im).astype(BF16), (q_re * r_im + q_im * r_re).astype(BF16)


def at(step, base=0):
    return pl.ds(pl.multiple_of(base + step * TILE, TILE), TILE)


def lead_body(rows, weight, query):
    half = weight.shape[0] // 2
    for step in range(half // TILE):
        span = pl.ds(step * TILE, TILE)
        query[0, :, span] = dot(rows[...], weight[at(step)], 1, 1).astype(BF16)
        query[1, :, span] = dot(rows[...], weight[at(step, half)], 1, 1).astype(BF16)


def lead(rows, weight):
    rows_dev, hidden = rows.shape
    width = weight.shape[0]
    vmem = pl.BlockSpec(memory_space=pltpu.VMEM)
    return pl.pallas_call(
        lead_body,
        out_shape=jax.ShapeDtypeStruct((2, rows_dev, width // 2), BF16),
        in_specs=[vmem] * 2,
        out_specs=vmem,
        compiler_params=pltpu.CompilerParams(vmem_limit_bytes=GRANT),
        cost_estimate=pl.CostEstimate(
            flops=2 * rows_dev * width * hidden, bytes_accessed=2 * width * hidden, transcendentals=0
        ),
    )(rows, weight)


def trail_body(first, query, rows, weight, rel, onehot, right, query_grad, give, keep, mixed, hidden):
    width = weight.shape[0]
    half = width // 2
    is_first = first[0] == 1
    owned = give.shape[0]

    def make_mixed(step, carry):
        mixed[:, at(step)], mixed[:, at(step, half)] = mix(
            query[0, :, at(step)].astype(F32), query[1, :, at(step)].astype(F32),
            rel[0, :, at(step)].astype(F32), rel[1, :, at(step)].astype(F32),
        )
        return carry

    lax.fori_loop(0, half // TILE, make_mixed, 0)

    def make_hidden(step, carry):
        pre = dot(mixed[...], weight[:, at(step)], 1, 0)
        sig = jax.nn.sigmoid(pre)
        cot = rows[:, at(step)]
        grad = (cot.astype(F32) * (sig * (1.0 + pre * (1.0 - sig)))).astype(BF16)
        hidden[:, at(step)] = grad
        right[:, at(step)] = jnp.where(is_first, cot, grad)
        return carry

    lax.fori_loop(0, weight.shape[1] // TILE, make_hidden, 0)

    def make_query(step, carry):
        gz_re = dot(hidden[...], weight[at(step), :], 1, 1)
        gz_im = dot(hidden[...], weight[at(step, half), :], 1, 1)
        r_re, r_im = rel[0, :, at(step)].astype(F32), rel[1, :, at(step)].astype(F32)
        query_grad[:, at(step)] = (gz_re * r_re + gz_im * r_im).astype(BF16)
        query_grad[:, at(step, half)] = (gz_im * r_re - gz_re * r_im).astype(BF16)
        a, b = query[0, :, at(step)].astype(F32), query[1, :, at(step)].astype(F32)
        for base, grad in ((0, gz_re * a + gz_im * b), (half, gz_im * a - gz_re * b)):
            head = grad.astype(BF16)
            rest = (grad - head.astype(F32)).astype(BF16)
            total = dot(onehot[...], head, 1, 0) + dot(onehot[...], rest, 1, 0)
            give[:, at(step, base)] = total[:owned]
            keep[:, at(step, base)] = total[owned:]
        return carry

    lax.fori_loop(0, half // TILE, make_query, 0)


def trail(first, query, rows, weight, rel, onehot):
    rows_dev, hidden = rows.shape
    width = weight.shape[0]
    count_rel = onehot.shape[0]
    vmem = pl.BlockSpec(memory_space=pltpu.VMEM)
    flops = 4 * rows_dev * width * hidden + 4 * rows_dev * count_rel * width
    return pl.pallas_call(
        trail_body,
        out_shape=(
            jax.ShapeDtypeStruct((rows_dev, hidden), BF16),
            jax.ShapeDtypeStruct((rows_dev, width), BF16),
            jax.ShapeDtypeStruct((count_rel // 2, width), F32),
            jax.ShapeDtypeStruct((count_rel // 2, width), F32),
            jax.ShapeDtypeStruct((rows_dev, width), BF16),
        ),
        in_specs=[pl.BlockSpec(memory_space=pltpu.SMEM)] + [vmem] * 5,
        out_specs=(vmem,) * 5,
        scratch_shapes=[pltpu.VMEM((rows_dev, hidden), BF16)],
        compiler_params=pltpu.CompilerParams(vmem_limit_bytes=GRANT),
        cost_estimate=pl.CostEstimate(
            flops=flops, bytes_accessed=4 * width * hidden, transcendentals=rows_dev * hidden
        ),
    )(first, query, rows, weight, rel, onehot)


def local(section_rows, weights, relation_table, relation_ids):
    rows = section_rows[0]
    weight = weights[0]
    rows_dev, width = rows.shape
    half = width // 2
    count_rel = relation_table.shape[0]
    chips = lax.axis_size("chip")
    first = lax.axis_index("hop") == 0
    core = lax.axis_index("core")
    chip = lax.axis_index("chip")
    total_rows = rows_dev * chips * 2
    cols = width // chips
    owned = count_rel // (4 * chips)

    def columns(left):
        return left.reshape(left.shape[0], chips, cols).transpose(1, 0, 2)

    onehot = (relation_ids[:, None] == lax.iota(jnp.int32, count_rel)[None, :]).astype(BF16)
    number = lax.iota(jnp.int32, count_rel)
    side = number // (count_rel // 2)
    dest = number % (count_rel // 2) // (2 * owned)
    hop = number % (2 * owned) // owned
    which_core = jnp.where(side == 1, core, 1 - core)
    relation = ((hop * chips + dest) * 2 + which_core) * owned + number % owned
    onehot_t = (relation[:, None] == relation_ids[None, :]).astype(BF16)

    own_query = lead(rows, weight)
    query = lax.ppermute(own_query, "hop", [(0, 1)])
    rel = dot(onehot, relation_table, 1, 0).astype(BF16)
    rel = rel.reshape(rows_dev, 2, half).transpose(1, 0, 2)
    right, grad_query, rel_give, rel_keep, mixed = trail(
        first.astype(jnp.int32).reshape(1), query, rows, weight, rel, onehot_t
    )
    query_back = lax.ppermute(grad_query, "hop", [(1, 0)])
    rel_chip = (rel_keep + swap_core(rel_give)).astype(BF16).reshape(chips, 2, owned, width)
    query_back, _ = lax.optimization_barrier((query_back, rel_chip))
    query_grad = jnp.where(first, query_back, grad_query)
    rel_back = lax.ppermute(rel_chip[:, 0], "hop", [(1, 0)])

    def chip_at(place):
        place = lax.rem(place, chips)
        return jnp.where(place < (chips + 1) // 2, 2 * place, 2 * (chips - place) - 1)

    ring = list(range(0, chips, 2)) + list(range(1, chips, 2))[::-1]
    place = jnp.where(lax.rem(chip, 2) == 0, chip // 2, chips - 1 - chip // 2)
    up = [(ring[i], ring[(i + 1) % chips]) for i in range(chips)]
    down = [(b, a) for a, b in up]
    blocks = [(right, 0, 0)]
    fwd = bwd = right
    for s in range(1, (chips + 1) // 2):
        fwd = lax.ppermute(fwd, "chip", up)
        bwd = lax.ppermute(bwd, "chip", down)
        blocks += [(fwd, chips - s, 0), (bwd, s, 0)]

    rel_own = jnp.where(first, rel_back, rel_chip[:, 1]).reshape(chips, owned, chips, cols)
    rel_own = rel_own.transpose(0, 2, 1, 3).reshape(chips, owned * chips, cols)
    left = columns(jnp.where(first, query_back, mixed))
    sent = jnp.concatenate([left, rel_own], axis=1)
    sent, _ = lax.optimization_barrier((sent, (blocks[3][0], blocks[4][0])))
    received = lax.all_to_all(sent, "chip", 0, 0, tiled=True)
    left_cols, rel_rows = received[:, :rows_dev], received[:, rows_dev:]
    rel_sum = jnp.sum(rel_rows.astype(F32), axis=0) * jnp.sqrt(F32(count_rel) / F32(total_rows))
    relation_grad = rel_sum.reshape(chips, owned, cols).transpose(1, 0, 2).reshape(owned, width)

    if chips % 2 == 0:
        mid = rows_dev // 2
        blocks.append((lax.ppermute(fwd[:mid], "chip", up), chips // 2, 0))
        blocks.append((lax.ppermute(bwd[mid:], "chip", down), chips // 2, mid))
    right_all = jnp.zeros((chips * rows_dev, width), BF16)
    for block, step, base in blocks:
        start = chip_at(place + step) * rows_dev + base
        right_all = lax.dynamic_update_slice_in_dim(right_all, block, start, 0)
    lower, upper = left_cols[..., :cols // 2], left_cols[..., cols // 2:]
    give = jnp.where(core == 0, upper, lower).reshape(chips * rows_dev, cols // 2)
    keep = jnp.where(core == 0, lower, upper).reshape(chips * rows_dev, cols // 2)
    got = swap_core(dot(give, right_all, 0, 0))
    own = lax.optimization_barrier(dot(keep, right_all, 0, 0))
    weight_grad = (own + got) * (1.0 / jnp.sqrt(F32(total_rows)))
    return weight_grad[None], relation_grad, query_grad


def solution(mesh):
    hops, batch = mesh.devices.shape
    fine = Mesh(mesh.devices.reshape(hops, batch // 2, 2), ("hop", "chip", "core"))
    rows = ("chip", "core")
    return jax.shard_map(
        local,
        mesh=fine,
        in_specs=(P("hop", rows, None), P("hop", None, None), P(), P(rows)),
        out_specs=(P("hop", rows, None), P(("hop", "chip", "core"), None), P(rows, None)),
        check_vma=False,
    )
```

```python
import jax
import jax.numpy as jnp
from jax import lax
from jax.experimental import pallas as pl
from jax.experimental.pallas import tpu as pltpu
from jax.sharding import Mesh
from jax.sharding import PartitionSpec as P

F32 = jnp.float32
BF16 = jnp.bfloat16
TILE = 256
GRANT = 8 * 1024 * 1024


def dot(a, b, ca, cb):
    return lax.dot_general(a, b, (((ca,), (cb,)), ((), ())), preferred_element_type=F32)


def swap_core(block):
    return lax.ppermute(block, "core", [(0, 1), (1, 0)])


def mix(q_re, q_im, r_re, r_im):
    return (q_re * r_re - q_im * r_im).astype(BF16), (q_re * r_im + q_im * r_re).astype(BF16)


def at(step, base=0):
    return pl.ds(pl.multiple_of(base + step * TILE, TILE), TILE)


def lead_body(rows, weight, query):
    half = weight.shape[0] // 2
    for step in range(half // TILE):
        span = pl.ds(step * TILE, TILE)
        query[0, :, span] = dot(rows[...], weight[at(step)], 1, 1).astype(BF16)
        query[1, :, span] = dot(rows[...], weight[at(step, half)], 1, 1).astype(BF16)


def lead(rows, weight):
    rows_dev, hidden = rows.shape
    width = weight.shape[0]
    vmem = pl.BlockSpec(memory_space=pltpu.VMEM)
    return pl.pallas_call(
        lead_body,
        out_shape=jax.ShapeDtypeStruct((2, rows_dev, width // 2), BF16),
        in_specs=[vmem] * 2,
        out_specs=vmem,
        compiler_params=pltpu.CompilerParams(vmem_limit_bytes=GRANT),
        cost_estimate=pl.CostEstimate(
            flops=2 * rows_dev * width * hidden, bytes_accessed=2 * width * hidden, transcendentals=0
        ),
    )(rows, weight)


def trail_body(first, query, rows, weight, rel, onehot, right, query_grad, give, keep, mixed, hidden):
    width = weight.shape[0]
    half = width // 2
    is_first = first[0] == 1
    owned = give.shape[0]

    def make_mixed(step, carry):
        mixed[:, at(step)], mixed[:, at(step, half)] = mix(
            query[0, :, at(step)].astype(F32), query[1, :, at(step)].astype(F32),
            rel[0, :, at(step)].astype(F32), rel[1, :, at(step)].astype(F32),
        )
        return carry

    lax.fori_loop(0, half // TILE, make_mixed, 0)

    def make_hidden(step, carry):
        pre = dot(mixed[...], weight[:, at(step)], 1, 0)
        sig = jax.nn.sigmoid(pre)
        cot = rows[:, at(step)]
        grad = (cot.astype(F32) * (sig * (1.0 + pre * (1.0 - sig)))).astype(BF16)
        hidden[:, at(step)] = grad
        right[:, at(step)] = jnp.where(is_first, cot, grad)
        return carry

    lax.fori_loop(0, weight.shape[1] // TILE, make_hidden, 0)

    def make_query(step, carry):
        gz_re = dot(hidden[...], weight[at(step), :], 1, 1)
        gz_im = dot(hidden[...], weight[at(step, half), :], 1, 1)
        r_re, r_im = rel[0, :, at(step)].astype(F32), rel[1, :, at(step)].astype(F32)
        query_grad[:, at(step)] = (gz_re * r_re + gz_im * r_im).astype(BF16)
        query_grad[:, at(step, half)] = (gz_im * r_re - gz_re * r_im).astype(BF16)
        a, b = query[0, :, at(step)].astype(F32), query[1, :, at(step)].astype(F32)
        for base, grad in ((0, gz_re * a + gz_im * b), (half, gz_im * a - gz_re * b)):
            head = grad.astype(BF16)
            rest = (grad - head.astype(F32)).astype(BF16)
            total = dot(onehot[...], head, 1, 0) + dot(onehot[...], rest, 1, 0)
            give[:, at(step, base)] = total[:owned]
            keep[:, at(step, base)] = total[owned:]
        return carry

    lax.fori_loop(0, half // TILE, make_query, 0)


def trail(first, query, rows, weight, rel, onehot):
    rows_dev, hidden = rows.shape
    width = weight.shape[0]
    count_rel = onehot.shape[0]
    vmem = pl.BlockSpec(memory_space=pltpu.VMEM)
    flops = 4 * rows_dev * width * hidden + 4 * rows_dev * count_rel * width
    return pl.pallas_call(
        trail_body,
        out_shape=(
            jax.ShapeDtypeStruct((rows_dev, hidden), BF16),
            jax.ShapeDtypeStruct((rows_dev, width), BF16),
            jax.ShapeDtypeStruct((count_rel // 2, width), F32),
            jax.ShapeDtypeStruct((count_rel // 2, width), F32),
            jax.ShapeDtypeStruct((rows_dev, width), BF16),
        ),
        in_specs=[pl.BlockSpec(memory_space=pltpu.SMEM)] + [vmem] * 5,
        out_specs=(vmem,) * 5,
        scratch_shapes=[pltpu.VMEM((rows_dev, hidden), BF16)],
        compiler_params=pltpu.CompilerParams(vmem_limit_bytes=GRANT),
        cost_estimate=pl.CostEstimate(
            flops=flops, bytes_accessed=4 * width * hidden, transcendentals=rows_dev * hidden
        ),
    )(first, query, rows, weight, rel, onehot)


def local(section_rows, weights, relation_table, relation_ids):
    rows = section_rows[0]
    weight = weights[0]
    rows_dev, width = rows.shape
    half = width // 2
    count_rel = relation_table.shape[0]
    chips = lax.axis_size("chip")
    first = lax.axis_index("hop") == 0
    core = lax.axis_index("core")
    chip = lax.axis_index("chip")
    total_rows = rows_dev * chips * 2
    cols = width // chips
    owned = count_rel // (4 * chips)

    def columns(left):
        return left.reshape(left.shape[0], chips, cols).transpose(1, 0, 2)

    onehot = (relation_ids[:, None] == lax.iota(jnp.int32, count_rel)[None, :]).astype(BF16)
    number = lax.iota(jnp.int32, count_rel)
    side = number // (count_rel // 2)
    dest = number % (count_rel // 2) // (2 * owned)
    hop = number % (2 * owned) // owned
    which_core = jnp.where(side == 1, core, 1 - core)
    relation = ((hop * chips + dest) * 2 + which_core) * owned + number % owned
    onehot_t = (relation[:, None] == relation_ids[None, :]).astype(BF16)

    own_query = lead(rows, weight)
    query = lax.ppermute(own_query, "hop", [(0, 1)])
    rel = dot(onehot, relation_table, 1, 0).astype(BF16)
    rel = rel.reshape(rows_dev, 2, half).transpose(1, 0, 2)
    right, grad_query, rel_give, rel_keep, mixed = trail(
        first.astype(jnp.int32).reshape(1), query, rows, weight, rel, onehot_t
    )
    query_back = lax.ppermute(grad_query, "hop", [(1, 0)])
    rel_chip = (rel_keep + swap_core(rel_give)).astype(BF16).reshape(chips, 2, owned, width)
    query_back, _ = lax.optimization_barrier((query_back, rel_chip))
    query_grad = jnp.where(first, query_back, grad_query)
    rel_back = lax.ppermute(rel_chip[:, 0], "hop", [(1, 0)])

    def chip_at(place):
        place = lax.rem(place, chips)
        return jnp.where(place < (chips + 1) // 2, 2 * place, 2 * (chips - place) - 1)

    ring = list(range(0, chips, 2)) + list(range(1, chips, 2))[::-1]
    place = jnp.where(lax.rem(chip, 2) == 0, chip // 2, chips - 1 - chip // 2)
    up = [(ring[i], ring[(i + 1) % chips]) for i in range(chips)]
    down = [(b, a) for a, b in up]
    blocks = [(right, 0, 0)]
    fwd = bwd = right
    for s in range(1, (chips + 1) // 2):
        fwd = lax.ppermute(fwd, "chip", up)
        bwd = lax.ppermute(bwd, "chip", down)
        blocks += [(fwd, chips - s, 0), (bwd, s, 0)]

    rel_own = jnp.where(first, rel_back, rel_chip[:, 1]).reshape(chips, owned, chips, cols)
    rel_own = rel_own.transpose(0, 2, 1, 3).reshape(chips, owned * chips, cols)
    left = columns(jnp.where(first, query_back, mixed))
    sent = jnp.concatenate([left, rel_own], axis=1)
    sent, _ = lax.optimization_barrier((sent, (blocks[3][0], blocks[4][0])))
    received = lax.all_to_all(sent, "chip", 0, 0, tiled=True)
    left_cols, rel_rows = received[:, :rows_dev], received[:, rows_dev:]
    rel_sum = jnp.sum(rel_rows.astype(F32), axis=0) * jnp.sqrt(F32(count_rel) / F32(total_rows))
    relation_grad = rel_sum.reshape(chips, owned, cols).transpose(1, 0, 2).reshape(owned, width)

    if chips % 2 == 0:
        mid = rows_dev // 2
        blocks.append((lax.ppermute(fwd[:mid], "chip", up), chips // 2, 0))
        blocks.append((lax.ppermute(bwd[mid:], "chip", down), chips // 2, mid))
    right_all = jnp.zeros((chips * rows_dev, width), BF16)
    for block, step, base in blocks:
        start = chip_at(place + step) * rows_dev + base
        right_all = lax.dynamic_update_slice_in_dim(right_all, block, start, 0)
    lower, upper = left_cols[..., :cols // 2], left_cols[..., cols // 2:]
    give = jnp.where(core == 0, upper, lower).reshape(chips * rows_dev, cols // 2)
    keep = jnp.where(core == 0, lower, upper).reshape(chips * rows_dev, cols // 2)
    got = swap_core(dot(give, right_all, 0, 0))
    own = lax.optimization_barrier(dot(keep, right_all, 0, 0))
    weight_grad = (own + got) * (1.0 / jnp.sqrt(F32(total_rows)))
    return weight_grad[None], relation_grad, query_grad


def solution(mesh):
    hops, batch = mesh.devices.shape
    fine = Mesh(mesh.devices.reshape(hops, batch // 2, 2), ("hop", "chip", "core"))
    rows = ("chip", "core")
    return jax.shard_map(
        local,
        mesh=fine,
        in_specs=(P("hop", rows, None), P("hop", None, None), P(), P(rows)),
        out_specs=(P("hop", rows, None), P(("hop", "chip", "core"), None), P(rows, None)),
        check_vma=False,
    )
```

```python
import jax
import jax.numpy as jnp
from jax import lax
from jax.experimental import pallas as pl
from jax.experimental.pallas import tpu as pltpu
from jax.sharding import Mesh
from jax.sharding import PartitionSpec as P

F32 = jnp.float32
BF16 = jnp.bfloat16
TILE = 512
GRANT = 16 * 1024 * 1024


def dot(a, b, ca, cb):
    return lax.dot_general(a, b, (((ca,), (cb,)), ((), ())), preferred_element_type=F32)


def swap_core(block):
    return lax.ppermute(block, "core", [(0, 1), (1, 0)])


def mix(q_re, q_im, r_re, r_im):
    return (q_re * r_re - q_im * r_im).astype(BF16), (q_re * r_im + q_im * r_re).astype(BF16)


def at(step, base=0):
    return pl.ds(pl.multiple_of(base + step * TILE, TILE), TILE)


def lead_body(rows, weight, query):
    half = weight.shape[0] // 2
    for step in range(half // TILE):
        span = pl.ds(step * TILE, TILE)
        query[0, :, span] = dot(rows[...], weight[at(step)], 1, 1).astype(BF16)
        query[1, :, span] = dot(rows[...], weight[at(step, half)], 1, 1).astype(BF16)


def lead(rows, weight):
    rows_dev, hidden = rows.shape
    width = weight.shape[0]
    vmem = pl.BlockSpec(memory_space=pltpu.VMEM)
    return pl.pallas_call(
        lead_body,
        out_shape=jax.ShapeDtypeStruct((2, rows_dev, width // 2), BF16),
        in_specs=[vmem] * 2,
        out_specs=vmem,
        compiler_params=pltpu.CompilerParams(vmem_limit_bytes=GRANT),
        cost_estimate=pl.CostEstimate(
            flops=2 * rows_dev * width * hidden, bytes_accessed=2 * width * hidden, transcendentals=0
        ),
    )(rows, weight)


def trail_body(first, query, rows, weight, rel, onehot, right, query_grad, give, keep, mixed, hidden):
    width = weight.shape[0]
    half = width // 2
    is_first = first[0] == 1
    owned = give.shape[0]

    def make_mixed(step, carry):
        mixed[:, at(step)], mixed[:, at(step, half)] = mix(
            query[0, :, at(step)].astype(F32), query[1, :, at(step)].astype(F32),
            rel[0, :, at(step)].astype(F32), rel[1, :, at(step)].astype(F32),
        )
        return carry

    lax.fori_loop(0, half // TILE, make_mixed, 0)

    def make_hidden(step, carry):
        pre = dot(mixed[...], weight[:, at(step)], 1, 0)
        sig = jax.nn.sigmoid(pre)
        cot = rows[:, at(step)]
        grad = (cot.astype(F32) * (sig * (1.0 + pre * (1.0 - sig)))).astype(BF16)
        hidden[:, at(step)] = grad
        right[:, at(step)] = jnp.where(is_first, cot, grad)
        return carry

    lax.fori_loop(0, weight.shape[1] // TILE, make_hidden, 0)

    def make_query(step, carry):
        gz_re = dot(hidden[...], weight[at(step), :], 1, 1)
        gz_im = dot(hidden[...], weight[at(step, half), :], 1, 1)
        r_re, r_im = rel[0, :, at(step)].astype(F32), rel[1, :, at(step)].astype(F32)
        query_grad[:, at(step)] = (gz_re * r_re + gz_im * r_im).astype(BF16)
        query_grad[:, at(step, half)] = (gz_im * r_re - gz_re * r_im).astype(BF16)
        a, b = query[0, :, at(step)].astype(F32), query[1, :, at(step)].astype(F32)
        for base, grad in ((0, gz_re * a + gz_im * b), (half, gz_im * a - gz_re * b)):
            head = grad.astype(BF16)
            rest = (grad - head.astype(F32)).astype(BF16)
            total = dot(onehot[...], head, 1, 0) + dot(onehot[...], rest, 1, 0)
            give[:, at(step, base)] = total[:owned]
            keep[:, at(step, base)] = total[owned:]
        return carry

    lax.fori_loop(0, half // TILE, make_query, 0)


def trail(first, query, rows, weight, rel, onehot):
    rows_dev, hidden = rows.shape
    width = weight.shape[0]
    count_rel = onehot.shape[0]
    vmem = pl.BlockSpec(memory_space=pltpu.VMEM)
    flops = 4 * rows_dev * width * hidden + 4 * rows_dev * count_rel * width
    return pl.pallas_call(
        trail_body,
        out_shape=(
            jax.ShapeDtypeStruct((rows_dev, hidden), BF16),
            jax.ShapeDtypeStruct((rows_dev, width), BF16),
            jax.ShapeDtypeStruct((count_rel // 2, width), F32),
            jax.ShapeDtypeStruct((count_rel // 2, width), F32),
            jax.ShapeDtypeStruct((rows_dev, width), BF16),
        ),
        in_specs=[pl.BlockSpec(memory_space=pltpu.SMEM)] + [vmem] * 5,
        out_specs=(vmem,) * 5,
        scratch_shapes=[pltpu.VMEM((rows_dev, hidden), BF16)],
        compiler_params=pltpu.CompilerParams(vmem_limit_bytes=GRANT),
        cost_estimate=pl.CostEstimate(
            flops=flops, bytes_accessed=4 * width * hidden, transcendentals=rows_dev * hidden
        ),
    )(first, query, rows, weight, rel, onehot)


def local(section_rows, weights, relation_table, relation_ids):
    rows = section_rows[0]
    weight = weights[0]
    rows_dev, width = rows.shape
    half = width // 2
    count_rel = relation_table.shape[0]
    chips = lax.axis_size("chip")
    first = lax.axis_index("hop") == 0
    core = lax.axis_index("core")
    chip = lax.axis_index("chip")
    total_rows = rows_dev * chips * 2
    cols = width // chips
    owned = count_rel // (4 * chips)

    def columns(left):
        return left.reshape(left.shape[0], chips, cols).transpose(1, 0, 2)

    onehot = (relation_ids[:, None] == lax.iota(jnp.int32, count_rel)[None, :]).astype(BF16)
    number = lax.iota(jnp.int32, count_rel)
    side = number // (count_rel // 2)
    dest = number % (count_rel // 2) // (2 * owned)
    hop = number % (2 * owned) // owned
    which_core = jnp.where(side == 1, core, 1 - core)
    relation = ((hop * chips + dest) * 2 + which_core) * owned + number % owned
    onehot_t = (relation[:, None] == relation_ids[None, :]).astype(BF16)

    own_query = lead(rows, weight)
    query = lax.ppermute(own_query, "hop", [(0, 1)])
    rel = dot(onehot, relation_table, 1, 0).astype(BF16)
    rel = rel.reshape(rows_dev, 2, half).transpose(1, 0, 2)
    right, grad_query, rel_give, rel_keep, mixed = trail(
        first.astype(jnp.int32).reshape(1), query, rows, weight, rel, onehot_t
    )
    query_back = lax.ppermute(grad_query, "hop", [(1, 0)])
    rel_chip = (rel_keep + swap_core(rel_give)).astype(BF16).reshape(chips, 2, owned, width)
    query_back, _ = lax.optimization_barrier((query_back, rel_chip))
    query_grad = jnp.where(first, query_back, grad_query)
    rel_back = lax.ppermute(rel_chip[:, 0], "hop", [(1, 0)])

    def chip_at(place):
        place = lax.rem(place, chips)
        return jnp.where(place < (chips + 1) // 2, 2 * place, 2 * (chips - place) - 1)

    ring = list(range(0, chips, 2)) + list(range(1, chips, 2))[::-1]
    place = jnp.where(lax.rem(chip, 2) == 0, chip // 2, chips - 1 - chip // 2)
    up = [(ring[i], ring[(i + 1) % chips]) for i in range(chips)]
    down = [(b, a) for a, b in up]
    blocks = [(right, 0, 0)]
    fwd = bwd = right
    for s in range(1, (chips + 1) // 2):
        fwd = lax.ppermute(fwd, "chip", up)
        bwd = lax.ppermute(bwd, "chip", down)
        blocks += [(fwd, chips - s, 0), (bwd, s, 0)]

    rel_own = jnp.where(first, rel_back, rel_chip[:, 1]).reshape(chips, owned, chips, cols)
    rel_own = rel_own.transpose(0, 2, 1, 3).reshape(chips, owned * chips, cols)
    left = columns(jnp.where(first, query_back, mixed))
    sent = jnp.concatenate([left, rel_own], axis=1)
    sent, _ = lax.optimization_barrier((sent, (blocks[3][0], blocks[4][0])))
    received = lax.all_to_all(sent, "chip", 0, 0, tiled=True)
    left_cols, rel_rows = received[:, :rows_dev], received[:, rows_dev:]
    rel_sum = jnp.sum(rel_rows.astype(F32), axis=0) * jnp.sqrt(F32(count_rel) / F32(total_rows))
    relation_grad = rel_sum.reshape(chips, owned, cols).transpose(1, 0, 2).reshape(owned, width)

    if chips % 2 == 0:
        mid = rows_dev // 2
        blocks.append((lax.ppermute(fwd[:mid], "chip", up), chips // 2, 0))
        blocks.append((lax.ppermute(bwd[mid:], "chip", down), chips // 2, mid))
    right_all = jnp.zeros((chips * rows_dev, width), BF16)
    for block, step, base in blocks:
        start = chip_at(place + step) * rows_dev + base
        right_all = lax.dynamic_update_slice_in_dim(right_all, block, start, 0)
    lower, upper = left_cols[..., :cols // 2], left_cols[..., cols // 2:]
    give = jnp.where(core == 0, upper, lower).reshape(chips * rows_dev, cols // 2)
    keep = jnp.where(core == 0, lower, upper).reshape(chips * rows_dev, cols // 2)
    got = swap_core(dot(give, right_all, 0, 0))
    own = lax.optimization_barrier(dot(keep, right_all, 0, 0))
    weight_grad = (own + got) * (1.0 / jnp.sqrt(F32(total_rows)))
    return weight_grad[None], relation_grad, query_grad


def solution(mesh):
    hops, batch = mesh.devices.shape
    fine = Mesh(mesh.devices.reshape(hops, batch // 2, 2), ("hop", "chip", "core"))
    rows = ("chip", "core")
    return jax.shard_map(
        local,
        mesh=fine,
        in_specs=(P("hop", rows, None), P("hop", None, None), P(), P(rows)),
        out_specs=(P("hop", rows, None), P(("hop", "chip", "core"), None), P(rows, None)),
        check_vma=False,
    )
```
